128 devices in a mesh: ctx: 16 (over x, y), exp: 8 (over z, core).
Axes of the slice: x: 4, y: 4, z: 4, core: 2. Of those that a mesh axis runs over, the one named last changes fastest.
Arguments:
- mixer_in: bfloat16 [2048, 8192], P('ctx', 'exp'), may hold values from -6 to 6
- gate_in: bfloat16 [2048, 8192], P('ctx', 'exp'), may hold values from -6 to 6
- conv_weight: float32 [4, 8192], P(None, 'exp'), may hold values from -3 to 3
- conv_bias: float32 [8192], P('exp'), may hold values from -3 to 3
- x_proj: bfloat16 [8192, 544], P('exp'), may hold values from -0.03125 to 0.03125
- dt_proj: bfloat16 [512, 8192], P(None, 'exp'), may hold values from -0.25 to 0.25
- dt_bias: float32 [8192], P('exp'), may hold values from -1.5 to 0.5
- decay_rate: float32 [16, 8192], P(None, 'exp'), may hold values from 9.765625e-05 to 0.1
- skip: float32 [8192], P('exp'), may hold values from 0.5 to 1.5
- out_proj: bfloat16 [8192, 4096], P('exp', 'ctx'), may hold values from -0.015625 to 0.015625
- residual: bfloat16 [2048, 4096], P(('ctx', 'exp')), may hold values from -6 to 6
- gain: float32 [4096], replicated, may hold values from 0.5 to 1.5
- router: bfloat16 [4096, 8], replicated, may hold values from -0.09375 to 0.09375
- w_gate: bfloat16 [8, 4096, 12288], P('exp', None, 'ctx'), may hold values from -0.09375 to 0.09375
- w_up: bfloat16 [8, 4096, 12288], P('exp', None, 'ctx'), may hold values from -0.09375 to 0.09375
- w_down: bfloat16 [8, 12288, 4096], P('exp', 'ctx'), may hold values from -0.0546875 to 0.0546875
- expert_ids: int32 [2048, 2], P(('ctx', 'exp')), may hold values from 0 to 7, all different within a row; in each aligned block of 16 rows (0 to 15, 16 to 31, ...) at most 5 rows name the same one
Outputs:
- block_out: bfloat16 [2048, 4096], P(('ctx', 'exp'))
The draws below stay inside these ranges and needn't reach their ends.
Inputs may be any that keep to these rules, and one draw needn't show every extreme that they name: `expert_ids`: the two ids of a token differ. In each aligned block of 16 tokens no expert is named more than 5 times.
All inputs are finite; a program needn't handle non-finite values.
Results may differ from the reference program's by a relative error of at most 0.007.
Values may be sent and summed in bfloat16 or wider, within the bound.
A program may use at most 128 MiB of HBM per device.

```python
import math
import jax
import jax.numpy as jnp
import numpy as np
from jax import lax

D = 4096
DI = 8192
NS = 16
DTR = 512
KCONV = 4
FF = 12288
TOP = 2
TOKENS = 2048
ROWS_DEV = 16
EXPERTS = 8
CAP = 5
N_CTX = 16
N_EXP = 8


def level_of(key, extent, split, smallest, top_value):
    loudness, own = 1.0, jax.random.fold_in(key, 6)
    for dim, shards_of in split:
        heights = jnp.exp(jax.random.uniform(jax.random.fold_in(own, dim), (shards_of,), jnp.float32, smallest / len(split), top_value / len(split)))
        loudness = loudness * jnp.repeat(heights, extent[dim] // shards_of).reshape([-1 if axis == dim else 1 for axis in range(len(extent))])
    return loudness


def deal_out(stream_key, own, number, rows, count, top, bound, lean):
    order = jax.random.permutation(stream_key, count)
    packed, usual = shares(count, rows * top, bound, lean, True), shares(count, rows * top, bound, lean, False)
    places = jnp.arange(count)

    def named(tallies, offset_by):
        used = int((tallies > 0).sum())
        fixed = max(1, used // 4)
        shifted = fixed + (places - fixed + offset_by * (used - fixed)) % max(1, count - fixed)
        return jnp.zeros((count,), jnp.int32).at[order[jnp.where(places < fixed, places, shifted)]].set(jnp.asarray(tallies, jnp.int32))

    tallies = jnp.where(number % 4 == 0, named(packed, number // 4), named(usual, number - number // 4 - 1))
    mixed = jax.random.permutation(jax.random.fold_in(own, 3), count)
    giver, sink = mixed[0:count // 2 * 2:2], mixed[1:count // 2 * 2:2]
    margin = jnp.minimum(tallies[giver] - 1, bound - tallies[sink]) // 2
    margin = jnp.where((giver == order[0]) | (sink == order[0]) | (tallies[sink] == 0), 0, jnp.maximum(margin, 0))
    shifted = jax.random.randint(jax.random.fold_in(own, 4), (count // 2,), 0, 1 << 20) % (margin + 1)
    tallies = tallies.at[giver].add(-shifted).at[sink].add(shifted)
    labels = jnp.searchsorted(jnp.cumsum(tallies), jnp.arange(rows * top), side="right").astype(jnp.int32)
    listing = labels.reshape(top, rows).T
    listing = listing[jax.random.permutation(jax.random.fold_in(own, 1), rows)]
    offset_by = jax.random.randint(jax.random.fold_in(own, 2), (rows, 1), 0, top)
    return jnp.take_along_axis(listing, (jnp.arange(top)[None, :] + offset_by) % top, axis=1)


def shares(count, total, bound, skew, full):
    weights = [(1 << 20) // math.isqrt(rank ** skew) + 1 for rank in range(1, count + 1)]
    largest = bound if full else min(bound, max(-(-total // count), total * weights[0] // sum(weights)))
    least = 1 if total - largest >= count - 1 else 0
    counts, rest = [largest] + [least] * (count - 1), total - largest - least * (count - 1)
    while rest > 0:
        free = [i for i in range(1, count) if counts[i] < largest] or [i for i in range(1, count) if counts[i] < bound]
        mass, left = sum([weights[i] for i in free]), rest
        for i in free:
            addition = min(bound - counts[i], max(1, left * weights[i] // mass), rest)
            counts[i] = counts[i] + addition
            rest = rest - addition
    return np.array(counts)


def gaussian(stream_key, dims, scale, most, cuts=(), kind=jnp.bfloat16):
    values = jax.random.normal(stream_key, dims, jnp.float32) * scale
    if len(cuts) > 0:
        values = level_of(stream_key, dims, cuts, -0.22, 0.18) * values
    return jnp.clip(values, min=-most, max=most).astype(kind)


def setup_inputs(seed: int = 0) -> dict:
    splits = jax.random.split(jax.random.key(seed), 18)
    mixer_in = gaussian(splits[0], (TOKENS, DI), 1.0, 6.0, ((0, 16), (1, 8)))
    gate_in = gaussian(splits[1], (TOKENS, DI), 1.0, 6.0, ((0, 16), (1, 8)))
    conv_weight = gaussian(splits[2], (KCONV, DI), 0.5, 3.0, ((1, 8),), jnp.float32)
    conv_bias = gaussian(splits[3], (DI,), 0.5, 3.0, ((0, 8),), jnp.float32)
    x_proj = gaussian(splits[4], (DI, DTR + 2 * NS), (4 * DI) ** -0.5, 0.03125, ((0, 8),))
    dt_proj = gaussian(splits[5], (DTR, DI), DTR ** -0.5, 0.25, ((1, 8),))
    dt_bias = jnp.clip(-1.5 + 2.0 * jax.random.uniform(splits[6], (DI,), jnp.float32) ** level_of(splits[6], (DI,), ((0, 8),), -0.2, 0.2), -1.5, 0.5)
    decay_rate = jnp.clip(jnp.exp(math.log(0.1) - 6.931472 * jax.random.uniform(splits[7], (NS, DI), jnp.float32) ** level_of(splits[7], (NS, DI), ((1, 8),), -0.2, 0.2)), 9.765625145519152e-05, 0.1)
    skip = jnp.clip(0.5 + 1.0 * jax.random.uniform(splits[8], (DI,), jnp.float32) ** level_of(splits[8], (DI,), ((0, 8),), -0.2, 0.2), 0.5, 1.5)
    out_proj = gaussian(splits[9], (DI, D), (16 * DI) ** -0.5, 0.015625, ((0, 8), (1, 16)))
    residual = gaussian(splits[10], (TOKENS, D), 1.0, 6.0, ((0, 128),))
    gain = jnp.clip(1.0 + 0.1 * jax.random.normal(splits[11], (D,), jnp.float32), 0.5, 1.5)
    router = gaussian(splits[12], (D, EXPERTS), D ** -0.5, 0.09375)
    w_gate = gaussian(splits[13], (EXPERTS, D, FF), D ** -0.5, 0.09375, ((0, 8), (2, 16)))
    w_up = gaussian(splits[14], (EXPERTS, D, FF), D ** -0.5, 0.09375, ((0, 8), (2, 16)))
    w_down = gaussian(splits[15], (EXPERTS, FF, D), FF ** -0.5, 0.0546875, ((0, 8), (1, 16)))
    expert_ids_keys = jax.random.split(jax.random.fold_in(splits[16], 1), TOKENS // ROWS_DEV)
    expert_ids_turns = jax.random.permutation(jax.random.fold_in(splits[16], 3), TOKENS // ROWS_DEV)
    expert_ids = jax.vmap(lambda own, number: deal_out(jax.random.fold_in(splits[16], 2), own, number, ROWS_DEV, EXPERTS, TOP, CAP, 2))(expert_ids_keys, expert_ids_turns).reshape((TOKENS, TOP))
    return {"mixer_in": mixer_in, "gate_in": gate_in, "conv_weight": conv_weight, "conv_bias": conv_bias, "x_proj": x_proj, "dt_proj": dt_proj, "dt_bias": dt_bias, "decay_rate": decay_rate, "skip": skip, "out_proj": out_proj, "residual": residual, "gain": gain, "router": router, "w_gate": w_gate, "w_up": w_up, "w_down": w_down, "expert_ids": expert_ids}


def reference(mixer_in, gate_in, conv_weight, conv_bias, x_proj, dt_proj, dt_bias, decay_rate, skip, out_proj, residual, gain, router, w_gate, w_up, w_down, expert_ids):
    zeros_head = jnp.zeros((KCONV - 1, DI), jnp.float32)
    padded = jnp.concatenate([zeros_head, mixer_in.astype(jnp.float32)], axis=0)
    conv_sum = conv_bias[None, :] + conv_weight[0][None, :] * padded[0:TOKENS]
    for offset in range(1, KCONV):
        conv_sum = conv_sum + conv_weight[offset][None, :] * padded[offset:offset + TOKENS]
    conv_out = jax.nn.silu(conv_sum).astype(jnp.bfloat16)
    projected = jnp.dot(conv_out, x_proj, preferred_element_type=jnp.float32)
    step_low = projected[:, :DTR].astype(jnp.bfloat16)
    b_mat = projected[:, DTR:DTR + NS]
    c_mat = projected[:, DTR + NS:]
    step_size = jax.nn.softplus(jnp.dot(step_low, dt_proj, preferred_element_type=jnp.float32) + dt_bias[None, :])
    x_value = conv_out.astype(jnp.float32)
    drive = step_size * x_value

    def scan_step(carry_state, pieces):
        step_row, drive_row, b_row, c_row = pieces
        carry_state = jnp.exp(-decay_rate * step_row[None, :]) * carry_state + b_row[:, None] * drive_row[None, :]
        return (carry_state, lax.optimization_barrier(jnp.sum(c_row[:, None] * carry_state, axis=0)))
    _, scan_out = lax.scan(scan_step, jnp.zeros((NS, DI), jnp.float32), (step_size, drive, b_mat, c_mat))
    scan_out = scan_out + skip[None, :] * x_value
    gated = (scan_out * jax.nn.silu(gate_in.astype(jnp.float32))).astype(jnp.bfloat16)
    mamba_out = jnp.dot(gated, out_proj, preferred_element_type=jnp.float32)
    stream = residual.astype(jnp.float32) + mamba_out
    normed = (stream * lax.rsqrt(lax.optimization_barrier(jnp.mean(stream * stream, axis=1, keepdims=True)) + 1e-06) * gain[None, :]).astype(jnp.bfloat16)
    logits = jnp.dot(normed, router, preferred_element_type=jnp.float32)
    picked = jnp.take_along_axis(logits, expert_ids, axis=1)
    first_gate = jax.nn.sigmoid(picked[:, 0] - picked[:, 1])
    gate_weights = jnp.stack([first_gate, 1.0 - first_gate], axis=1)
    max_rows = min(CAP * N_CTX * N_EXP, TOKENS)

    def one_expert(pieces):
        gate_mat, up_mat, down_mat, expert_index = pieces
        named_mask = expert_ids == expert_index
        chosen = jnp.any(named_mask, axis=1)
        row_order = jnp.argsort(jnp.where(chosen, 0, 1).astype(jnp.int32), stable=True)[:max_rows].astype(jnp.int32)
        rows_in = jnp.take(normed, row_order, axis=0)
        gate_val = jnp.dot(rows_in, gate_mat, preferred_element_type=jnp.float32)
        up_val = jnp.dot(rows_in, up_mat, preferred_element_type=jnp.float32)
        hidden = (jax.nn.silu(gate_val) * up_val).astype(jnp.bfloat16)
        expert_out = jnp.dot(hidden, down_mat, preferred_element_type=jnp.float32).astype(jnp.bfloat16)
        weight = lax.optimization_barrier(jnp.sum(jnp.where(named_mask, gate_weights, jnp.zeros_like(gate_weights)), axis=1))
        weight = jnp.take(weight, row_order)
        return (row_order, weight[:, None] * expert_out.astype(jnp.float32))
    orders, contribs = lax.map(one_expert, (w_gate, w_up, w_down, jnp.arange(EXPERTS, dtype=jnp.int32)))
    expert_mix = jnp.zeros((TOKENS, D), jnp.float32).at[orders.reshape(-1)].add(contribs.reshape(-1, D))
    return (stream + expert_mix).astype(jnp.bfloat16)
```

```python
import functools

import jax
import jax.numpy as jnp
import numpy as np
from jax import lax
from jax.experimental import pallas as pl
from jax.experimental.pallas import tpu as pltpu
from jax.sharding import PartitionSpec as P

F32 = jnp.float32
BF16 = jnp.bfloat16
VMEM_LIMIT = 60 * 1024 * 1024


def from_behind(value, axis, steps):
    count = lax.axis_size(axis)
    first, last = (max(0, -steps), min(count, count - steps))
    return lax.ppermute(value, axis, [(source, source + steps) for source in range(first, last)])


def entering_2(part, axis, combine, identity):
    place = lax.axis_index(axis)
    gathered = jax.tree.map(lambda a: lax.all_gather(a, axis), part)
    state = jax.tree.map(lambda a, e: jnp.zeros_like(a) + jnp.asarray(e, a.dtype), part, identity)

    def one(lap, state):
        return combine(
            state, jax.tree.map(lambda a: lax.dynamic_index_in_dim(a, lap, 0, False), gathered)
        )

    return lax.fori_loop(0, place, one, state)


def link_pairs(earlier, later):
    return (earlier[0] * later[0], later[0] * earlier[1] + later[1])


def mixer_conv(padded, conv_weight, conv_bias, length):
    conv_sum = conv_bias[None, :] + conv_weight[0][None, :] * padded[0:length]
    for offset in range(1, conv_weight.shape[0]):
        conv_sum = conv_sum + conv_weight[offset][None, :] * padded[offset : offset + length]
    return jax.nn.silu(conv_sum).astype(jnp.bfloat16)


def remote(src, dst, send_sem, recv_sem, device):
    return pltpu.make_async_remote_copy(
        src_ref=src,
        dst_ref=dst,
        send_sem=send_sem,
        recv_sem=recv_sem,
        device_id=device,
        device_id_type=pl.DeviceIdType.MESH,
    )


def greet(devices):
    barrier = pltpu.get_barrier_semaphore()
    for device in devices:
        pl.semaphore_signal(barrier, inc=1, device_id=device, device_id_type=pl.DeviceIdType.MESH)
    pl.semaphore_wait(barrier, len(devices))


def wrap(index, count):
    return lax.rem(index + count, count)


def dot(a, b):
    return jnp.dot(a, b, preferred_element_type=F32)


class Half:
    def __init__(self, half, mx, my):
        self.half = half
        self.mx, self.my = mx, my
        self.p, self.q = (mx, my) if half == 0 else (my, mx)

    def one(self, step):
        p = wrap(self.p + step, 4)
        return {"ctx": p * 4 + self.my if self.half == 0 else self.mx * 4 + p}

    def two(self, step):
        q = wrap(self.q + step, 4)
        return {"ctx": self.mx * 4 + q if self.half == 0 else q * 4 + self.my}

    def unit(self, u, v):
        return (u, v) if self.half == 0 else (v, u)

    def group(self, v):
        return (slice(None), v) if self.half == 0 else (v, slice(None))


def moe_kernel(
    normed,
    stream,
    gates,
    spread_a,
    spread_b,
    pick_a,
    pick_b,
    fetch,
    w_gate,
    w_up,
    w_down,
    out,
    go,
    rcv,
    rback,
    xa,
    xb,
    wgu,
    wd,
    lhs,
    acc,
    hid,
    oa,
    ob,
    far,
    near,
    tot,
    far2,
    near2,
    w_sem,
    d_send,
    d_recv,
    g_send,
    g_recv,
    s_send,
    s_recv,
    r_send,
    r_recv,
):
    ctx, exp = lax.axis_index("ctx"), lax.axis_index("exp")
    mx, my = ctx // 4, ctx % 4
    halves = (Half(0, mx, my), Half(1, mx, my))
    xs, os = (xa, xb), (oa, ob)
    lo, hi = pl.ds(0, 1024), pl.ds(1024, 1024)
    every = slice(None)

    loads = [
        pltpu.make_async_copy(w_gate.at[0], wgu.at[:, pl.ds(0, 768)], w_sem.at[0]),
        pltpu.make_async_copy(w_up.at[0], wgu.at[:, pl.ds(768, 768)], w_sem.at[1]),
        pltpu.make_async_copy(w_down.at[0], wd, w_sem.at[2]),
    ]
    for load in loads:
        load.start()
    greet(
        [h.one(s) for h in halves for s in (1, -1)]
        + [{"exp": lax.rem(exp + d, 8)} for d in range(1, 8)]
    )

    rows = normed[...]
    packed = dot(spread_a[...], rows[:, :2048]) + dot(spread_b[...], rows[:, 2048:])
    go[...] = packed.astype(BF16).reshape(8, 16, 2048)
    sends = []
    for d in range(1, 8):
        peer = lax.rem(exp + d, 8)
        c = remote(go.at[peer], rcv.at[exp], d_send.at[d], d_recv.at[d], {"exp": peer})
        c.start()
        sends.append(c)
    rcv[pl.ds(exp, 1)] = go[pl.ds(exp, 1)]
    acc[...] = jnp.zeros_like(acc)
    for c in sends:
        c.wait_recv()
    flat = rcv[...].reshape(128, 2048)
    xa[pl.ds(mx, 1), pl.ds(my, 1)] = dot(pick_a[...], flat).astype(BF16)[None, None]
    xb[pl.ds(mx, 1), pl.ds(my, 1)] = dot(pick_b[...], flat).astype(BF16)[None, None]
    for c in sends:
        c.wait_send()

    sent = []

    def push(h, x, at, cols, g, k, device):
        place = x.at[at + (every, cols)] if cols is not None else x.at[at]
        c = remote(place, place, g_send.at[h, g, k], g_recv.at[h, g, k], device)
        c.start()
        sent.append(c)
        return c

    first, second = [], [[None] * 4, [None] * 4]

    def second_start(i, g, u):
        h, x = halves[i], xs[i]
        at = h.unit(u, h.q)
        second[i][g] = [
            push(i, x, at, None, g + 1, 0, h.two(1)),
            push(i, x, at, None, g + 1, 1, h.two(-1)),
        ]

    def second_pass(i, g, u):
        h, x = halves[i], xs[i]
        second[i][g][0].wait_recv()
        a = push(i, x, h.unit(u, wrap(h.q - 1, 4)), lo, g + 1, 2, h.two(1))
        second[i][g][1].wait_recv()
        b = push(i, x, h.unit(u, wrap(h.q + 1, 4)), hi, g + 1, 3, h.two(-1))
        second[i][g] += [a, b]

    for i, (h, x) in enumerate(zip(halves, xs)):
        at = h.unit(h.p, h.q)
        first.append(
            [push(i, x, at, None, 0, 0, h.one(1)), push(i, x, at, None, 0, 1, h.one(-1))]
        )
    for i, h in enumerate(halves):
        second_start(i, 0, h.p)
    for i, (h, x) in enumerate(zip(halves, xs)):
        left, right = wrap(h.p - 1, 4), wrap(h.p + 1, 4)
        first[i][0].wait_recv()
        first[i].append(push(i, x, h.unit(left, h.q), lo, 0, 2, h.one(1)))
        first[i][1].wait_recv()
        first[i].append(push(i, x, h.unit(right, h.q), hi, 0, 3, h.one(-1)))
        second_start(i, 1, left)
        second_start(i, 2, right)
    for i, h in enumerate(halves):
        first[i][2].wait_recv()
        first[i][3].wait_recv()
        second_start(i, 3, wrap(h.p + 2, 4))

    def gate_up(i, v):
        h = halves[i]
        at = h.group(v)
        lhs[...] = xs[i][at].reshape(160, 2048)

        @pl.loop(0, 6)
        def _(j):
            cols = pl.ds(pl.multiple_of(j * 256, 256), 256)
            part = dot(lhs[...], wgu[pl.ds(i * 2048, 2048), cols])
            place = at + (every, cols)
            acc[place] = acc[place] + part.reshape(4, 40, 256)

    loads[0].wait()
    loads[1].wait()
    for i, h in enumerate(halves):
        gate_up(i, h.q)
    for g in range(4):
        for i, h in enumerate(halves):
            u = (h.p, wrap(h.p - 1, 4), wrap(h.p + 1, 4), wrap(h.p + 2, 4))[g]
            second_pass(i, g, u)
    for i, h in enumerate(halves):
        gate_up(i, wrap(h.q - 1, 4))
        gate_up(i, wrap(h.q + 1, 4))
    for i, h in enumerate(halves):
        for g in range(4):
            second[i][g][2].wait_recv()
            second[i][g][3].wait_recv()
        gate_up(i, wrap(h.q + 2, 4))

    @pl.loop(0, 16)
    def _(n):
        at = (n // 4, n % 4)
        gate = acc[at + (every, pl.ds(0, 768))]
        up = acc[at + (every, pl.ds(768, 768))]
        hid[at] = (gate * jax.nn.sigmoid(gate) * up).astype(BF16)

    loads[2].wait()

    def down(i, v):
        at = halves[i].group(v)
        lhs[:, pl.ds(0, 768)] = hid[at].reshape(160, 768)

        @pl.loop(0, 8)
        def _(j):
            start = pl.multiple_of(j * 256, 256)
            part = dot(lhs[:, pl.ds(0, 768)], wd[:, pl.ds(i * 2048 + start, 256)])
            os[i][at + (every, pl.ds(start, 256))] = part.reshape(4, 40, 256).astype(BF16)

    def send(src, dst, i, stage, k, device):
        c = remote(src, dst, s_send.at[i, stage, k], s_recv.at[i, stage, k], device)
        c.start()
        sent.append(c)
        return c

    def ring_far(i, stage, chunk, ahead, behind, step):
        return [
            send(chunk(2, lo), ahead, i, stage, 0, step(1)),
            send(chunk(2, hi), behind, i, stage, 1, step(-1)),
        ]

    def add_into(ref, at, other, other_at):
        ref[at] = (ref[at].astype(F32) + other[other_at].astype(F32)).astype(BF16)

    stage_one = [None, None]
    for i, h in enumerate(halves):
        down(i, wrap(h.q + 2, 4))
        o, at = os[i], h.group(wrap(h.q + 2, 4))
        stage_one[i] = [
            send(o.at[at + (every, lo)], far.at[i, 0], i, 0, 0, h.two(1)),
            send(o.at[at + (every, hi)], far.at[i, 1], i, 0, 1, h.two(-1)),
        ]
    for i, h in enumerate(halves):
        o = os[i]
        down(i, wrap(h.q + 1, 4))
        at = h.group(wrap(h.q + 1, 4))
        stage_one[i].append(
            send(o.at[at + (every, hi)], near.at[i, 0, :, :, hi], i, 0, 2, h.two(1))
        )
        down(i, wrap(h.q - 1, 4))
        at = h.group(wrap(h.q - 1, 4))
        stage_one[i].append(
            send(o.at[at + (every, lo)], near.at[i, 1, :, :, lo], i, 0, 3, h.two(-1))
        )
    for i, h in enumerate(halves):
        down(i, h.q)
    for i, h in enumerate(halves):
        o = os[i]
        stage_one[i][0].wait_recv()
        at = h.group(wrap(h.q + 1, 4)) + (every, lo)
        add_into(o, at, far, (i, 0))
        stage_one[i].append(send(o.at[at], near.at[i, 0, :, :, lo], i, 0, 4, h.two(1)))
        stage_one[i][1].wait_recv()
        at = h.group(wrap(h.q - 1, 4)) + (every, hi)
        add_into(o, at, far, (i, 1))
        stage_one[i].append(send(o.at[at], near.at[i, 1, :, :, hi], i, 0, 5, h.two(-1)))

    stage_two = [None, None]
    for i, h in enumerate(halves):
        for c in stage_one[i][2:]:
            c.wait_recv()

        def total(u):
            mine = os[i][h.unit(u, h.q)].astype(F32)
            tot[i, u] = (mine + near[i, 0, u].astype(F32) + near[i, 1, u].astype(F32)).astype(BF16)

        opposite, ahead, behind = wrap(h.p + 2, 4), wrap(h.p + 1, 4), wrap(h.p - 1, 4)
        total(opposite)
        stage_two[i] = [
            send(tot.at[i, opposite, :, lo], far2.at[i, 0], i, 1, 0, h.one(1)),
            send(tot.at[i, opposite, :, hi], far2.at[i, 1], i, 1, 1, h.one(-1)),
        ]
        total(ahead)
        total(behind)
        stage_two[i].append(send(tot.at[i, ahead, :, hi], near2.at[i, 0, :, hi], i, 1, 2, h.one(1)))
        stage_two[i].append(
            send(tot.at[i, behind, :, lo], near2.at[i, 1, :, lo], i, 1, 3, h.one(-1))
        )
        total(h.p)
    for i, h in enumerate(halves):
        ahead, behind = wrap(h.p + 1, 4), wrap(h.p - 1, 4)
        stage_two[i][0].wait_recv()
        add_into(tot, (i, ahead, every, lo), far2, (i, 0))
        stage_two[i].append(send(tot.at[i, ahead, :, lo], near2.at[i, 0, :, lo], i, 1, 4, h.one(1)))
        stage_two[i][1].wait_recv()
        add_into(tot, (i, behind, every, hi), far2, (i, 1))
        stage_two[i].append(
            send(tot.at[i, behind, :, hi], near2.at[i, 1, :, hi], i, 1, 5, h.one(-1))
        )
    ends = []
    for i, h in enumerate(halves):
        for c in stage_two[i][2:]:
            c.wait_recv()
        final = (
            tot[i, h.p].astype(F32) + near2[i, 0].astype(F32) + near2[i, 1].astype(F32)
        ).astype(BF16)
        ends.append(final)

    across = (((0,), (0,)), ((), ()))
    back = lax.dot_general(pick_a[...], ends[0], across, preferred_element_type=F32)
    back = back + lax.dot_general(pick_b[...], ends[1], across, preferred_element_type=F32)
    go[...] = back.astype(BF16).reshape(8, 16, 2048)
    sends = []
    for d in range(1, 8):
        peer = lax.rem(exp + d, 8)
        c = remote(go.at[peer], rback.at[exp], r_send.at[d], r_recv.at[d], {"exp": peer})
        c.start()
        sends.append(c)
    rback[pl.ds(exp, 1)] = go[pl.ds(exp, 1)]
    for c in sends:
        c.wait_recv()
    flat = rback[...].reshape(128, 2048)
    g = gates[...]
    for i in range(2):
        cols = pl.ds(i * 2048, 2048)
        mix = g[:, 0:1] * dot(fetch[i, 0], flat) + g[:, 1:2] * dot(fetch[i, 1], flat)
        out[:, cols] = (stream[:, cols] + mix).astype(BF16)
    for c in sends + sent:
        c.wait_send()


def expert_layer(normed, stream, gates, expert_ids, w_gate, w_up, w_down):
    flat_ids = expert_ids.reshape(-1)
    hits = (flat_ids[:, None] == jnp.arange(8, dtype=jnp.int32)[None, :]).astype(jnp.int32)
    earlier = jnp.cumsum(hits, axis=0) - hits
    slot = jnp.sum(earlier * hits, axis=1)
    target = (flat_ids * 16 + slot).reshape(16, 2)
    places = jnp.arange(128, dtype=jnp.int32)
    first = target[:, 0][:, None] == places[None, :]
    both = first | (target[:, 1][:, None] == places[None, :])
    spread_a = both.T.astype(BF16)
    spread_b = jnp.roll(spread_a, 8, axis=0)
    fetch_a = jnp.stack([first, both & ~first]).astype(BF16)
    fetch = jnp.stack([fetch_a, jnp.roll(fetch_a, 8, axis=2)])
    pick = np.zeros((2, 40, 128), np.float32)
    for j in range(8):
        for s in range(5):
            pick[0, j * 5 + s, j * 16 + s] = 1.0
            pick[1, j * 5 + s, j * 16 + 8 + s] = 1.0
    pick_a, pick_b = jnp.asarray(pick[0], BF16), jnp.asarray(pick[1], BF16)
    vmem = pl.BlockSpec(memory_space=pltpu.VMEM)
    anywhere = pl.BlockSpec(memory_space=pl.ANY)
    dma = pltpu.SemaphoreType.DMA
    return pl.pallas_call(
        moe_kernel,
        out_shape=jax.ShapeDtypeStruct((16, 4096), BF16),
        in_specs=[vmem] * 8 + [anywhere] * 3,
        out_specs=vmem,
        scratch_shapes=[
            pltpu.VMEM((8, 16, 2048), BF16),
            pltpu.VMEM((8, 16, 2048), BF16),
            pltpu.VMEM((8, 16, 2048), BF16),
            pltpu.VMEM((4, 4, 40, 2048), BF16),
            pltpu.VMEM((4, 4, 40, 2048), BF16),
            pltpu.VMEM((4096, 1536), BF16),
            pltpu.VMEM((768, 4096), BF16),
            pltpu.VMEM((160, 2048), BF16),
            pltpu.VMEM((4, 4, 40, 1536), F32),
            pltpu.VMEM((4, 4, 40, 768), BF16),
            pltpu.VMEM((4, 4, 40, 2048), BF16),
            pltpu.VMEM((4, 4, 40, 2048), BF16),
            pltpu.VMEM((2, 2, 4, 40, 1024), BF16),
            pltpu.VMEM((2, 2, 4, 40, 2048), BF16),
            pltpu.VMEM((2, 4, 40, 2048), BF16),
            pltpu.VMEM((2, 2, 40, 1024), BF16),
            pltpu.VMEM((2, 2, 40, 2048), BF16),
            dma((3,)),
            dma((8,)),
            dma((8,)),
            dma((2, 5, 4)),
            dma((2, 5, 4)),
            dma((2, 2, 6)),
            dma((2, 2, 6)),
            dma((8,)),
            dma((8,)),
        ],
        compiler_params=pltpu.CompilerParams(
            collective_id=1, has_side_effects=True, vmem_limit_bytes=VMEM_LIMIT
        ),
        cost_estimate=pl.CostEstimate(flops=12_000_000_000, bytes_accessed=19_000_000, transcendentals=0),
    )(normed, stream, gates, spread_a, spread_b, pick_a, pick_b, fetch, w_gate, w_up, w_down)


def shards(
    mixer_in,
    gate_in,
    conv_weight,
    conv_bias,
    x_proj,
    dt_proj,
    dt_bias,
    decay_rate,
    skip,
    out_proj,
    residual,
    gain,
    router,
    w_gate,
    w_up,
    w_down,
    expert_ids,
):
    length, channels = mixer_in.shape
    kernel_width = conv_weight.shape[0]
    rim_rows = from_behind(mixer_in[length - (kernel_width - 1) :], "ctx", 1)
    padded = jnp.concatenate([rim_rows, mixer_in], axis=0).astype(jnp.float32)
    conv_out = mixer_conv(padded, conv_weight, conv_bias, length)
    projected = lax.psum(jnp.dot(conv_out, x_proj, preferred_element_type=jnp.float32), "exp")
    rank_width = dt_proj.shape[0]
    state_count = (projected.shape[1] - rank_width) // 2
    step_low = projected[:, :rank_width].astype(jnp.bfloat16)
    b_mat = projected[:, rank_width : rank_width + state_count]
    c_mat = projected[:, rank_width + state_count :]
    step_size = jax.nn.softplus(
        jnp.dot(step_low, dt_proj, preferred_element_type=jnp.float32) + dt_bias[None, :]
    )
    x_value = conv_out.astype(jnp.float32)
    drive = step_size * x_value
    total_step = jnp.sum(step_size, axis=0)
    block_width = 256
    block_count = channels // block_width
    group_len = 32
    group_count = length // group_len
    b_groups = b_mat.reshape(group_count, group_len, state_count)
    c_groups = c_mat.reshape(group_count, group_len, state_count)

    def to_blocks(values):
        return values.reshape(values.shape[0], block_count, block_width).transpose(1, 0, 2)

    def local_scan(pieces):
        step_b, drive_b, rate_b = pieces
        steps_g = step_b.reshape(group_count, group_len, block_width)
        running = jnp.cumsum(steps_g, axis=1)
        exponent = rate_b[None, None] * running[:, :, None, :]
        inputs = b_groups[:, :, :, None] * drive_b.reshape(group_count, group_len, 1, block_width)
        decay_in = jnp.exp(-exponent)
        inner = decay_in * jnp.cumsum(jnp.exp(exponent) * inputs, axis=1)
        group_decay = decay_in[:, -1]
        group_final = inner[:, -1]

        def carry_step(state, parts):
            decay_part, final_part = parts
            return (decay_part * state + final_part, state)

        last_state, entering = lax.scan(
            carry_step,
            jnp.zeros((state_count, block_width), jnp.float32),
            (group_decay, group_final),
        )
        states = inner + decay_in * entering[:, None]
        local_out = jnp.sum(c_groups[:, :, :, None] * states, axis=2).reshape(length, block_width)
        return (local_out, last_state)

    local_blocks, final_blocks = lax.map(
        local_scan, (to_blocks(step_size), to_blocks(drive), to_blocks(decay_rate))
    )
    b_total = final_blocks.transpose(1, 0, 2).reshape(state_count, channels)
    a_total = jnp.exp(-decay_rate * total_step[None, :])
    carry_in = entering_2(
        (a_total, b_total), "ctx", link_pairs, (jnp.ones_like(a_total), jnp.zeros_like(b_total))
    )[1]
    cumulative = jnp.cumsum(step_size, axis=0)

    def carried(pieces):
        cum_b, rate_b, carry_b = pieces
        weight = jnp.exp(-rate_b[None] * cum_b[:, None, :]) * carry_b[None]
        return jnp.sum(c_mat[:, :, None] * weight, axis=1)

    carry_blocks = lax.map(
        carried, (to_blocks(cumulative), to_blocks(decay_rate), to_blocks(carry_in))
    )
    scan_out = (local_blocks + carry_blocks).transpose(1, 0, 2).reshape(length, channels) + skip[
        None, :
    ] * x_value
    gated = (scan_out * jax.nn.silu(gate_in.astype(jnp.float32))).astype(jnp.bfloat16)
    tok_rows = residual.shape[0]
    exp_count = lax.axis_size("exp")
    full_out = lax.all_gather(out_proj, "ctx", axis=1, tiled=True)
    mamba_out = lax.psum_scatter(
        jnp.dot(gated, full_out, preferred_element_type=jnp.float32),
        "exp",
        scatter_dimension=0,
        tiled=True,
    )
    stream = residual.astype(jnp.float32) + mamba_out
    normed = (
        stream * lax.rsqrt(jnp.mean(stream * stream, axis=1, keepdims=True) + 1e-06) * gain[None, :]
    ).astype(jnp.bfloat16)
    logits = jnp.dot(normed, router, preferred_element_type=jnp.float32)
    picked = jnp.take_along_axis(logits, expert_ids, axis=1)
    first_gate = jax.nn.sigmoid(picked[:, 0] - picked[:, 1])
    gate_weights = jnp.stack([first_gate, 1.0 - first_gate], axis=1)
    return expert_layer(normed, stream, gate_weights, expert_ids, w_gate, w_up, w_down)


def solution(mesh):
    in_specs = (
        P("ctx", "exp"),
        P("ctx", "exp"),
        P(None, "exp"),
        P("exp"),
        P("exp", None),
        P(None, "exp"),
        P("exp"),
        P(None, "exp"),
        P("exp"),
        P("exp", "ctx"),
        P(("ctx", "exp"), None),
        P(),
        P(),
        P("exp", None, "ctx"),
        P("exp", None, "ctx"),
        P("exp", "ctx", None),
        P(("ctx", "exp"), None),
    )
    out_specs = P(("ctx", "exp"), None)
    return jax.shard_map(shards, mesh=mesh, in_specs=in_specs, out_specs=out_specs, check_vma=False)
```

```python
import jax
import jax.numpy as jnp
import numpy as np
from jax import lax
from jax.experimental import pallas as pl
from jax.experimental.pallas import tpu as pltpu
from jax.sharding import PartitionSpec as P

F32 = jnp.float32
BF16 = jnp.bfloat16
VMEM_LIMIT = 60 * 1024 * 1024


def remote(src, dst, send_sem, recv_sem, device):
    return pltpu.make_async_remote_copy(
        src_ref=src,
        dst_ref=dst,
        send_sem=send_sem,
        recv_sem=recv_sem,
        device_id=device,
        device_id_type=pl.DeviceIdType.MESH,
    )


def greet(devices):
    barrier = pltpu.get_barrier_semaphore()
    for device in devices:
        pl.semaphore_signal(barrier, inc=1, device_id=device, device_id_type=pl.DeviceIdType.MESH)
    pl.semaphore_wait(barrier, len(devices))


def wrap(index, count):
    return lax.rem(index + count, count)


def dot(a, b):
    return jnp.dot(a, b, preferred_element_type=F32)


class Half:
    def __init__(self, half, mx, my):
        self.half = half
        self.mx, self.my = mx, my
        self.p, self.q = (mx, my) if half == 0 else (my, mx)

    def one(self, step):
        p = wrap(self.p + step, 4)
        return {"ctx": p * 4 + self.my if self.half == 0 else self.mx * 4 + p}

    def two(self, step):
        q = wrap(self.q + step, 4)
        return {"ctx": self.mx * 4 + q if self.half == 0 else q * 4 + self.my}

    def unit(self, u, v):
        return (u, v) if self.half == 0 else (v, u)

    def group(self, v):
        return (slice(None), v) if self.half == 0 else (v, slice(None))


def moe_kernel(
    normed,
    stream,
    gates,
    spread_a,
    spread_b,
    pick_a,
    pick_b,
    fetch,
    w_gate,
    w_up,
    w_down,
    out,
    go,
    rcv,
    rback,
    xa,
    xb,
    wgu,
    wd,
    lhs,
    acc,
    hid,
    oa,
    ob,
    far,
    near,
    tot,
    far2,
    near2,
    w_sem,
    d_send,
    d_recv,
    g_send,
    g_recv,
    s_send,
    s_recv,
    r_send,
    r_recv,
):
    ctx, exp = lax.axis_index("ctx"), lax.axis_index("exp")
    mx, my = ctx // 4, ctx % 4
    halves = (Half(0, mx, my), Half(1, mx, my))
    xs, os = (xa, xb), (oa, ob)
    lo, hi = pl.ds(0, 1024), pl.ds(1024, 1024)
    every = slice(None)

    loads = [
        pltpu.make_async_copy(w_gate.at[0], wgu.at[:, pl.ds(0, 768)], w_sem.at[0]),
        pltpu.make_async_copy(w_up.at[0], wgu.at[:, pl.ds(768, 768)], w_sem.at[1]),
        pltpu.make_async_copy(w_down.at[0], wd, w_sem.at[2]),
    ]
    for load in loads:
        load.start()
    greet(
        [h.one(s) for h in halves for s in (1, -1)]
        + [{"exp": lax.rem(exp + d, 8)} for d in range(1, 8)]
    )

    rows = normed[...]
    packed = dot(spread_a[...], rows[:, :2048]) + dot(spread_b[...], rows[:, 2048:])
    go[...] = packed.astype(BF16).reshape(8, 16, 2048)
    sends = []
    for d in range(1, 8):
        peer = lax.rem(exp + d, 8)
        c = remote(go.at[peer], rcv.at[exp], d_send.at[d], d_recv.at[d], {"exp": peer})
        c.start()
        sends.append(c)
    rcv[pl.ds(exp, 1)] = go[pl.ds(exp, 1)]
    acc[...] = jnp.zeros_like(acc)
    for c in sends:
        c.wait_recv()
    flat = rcv[...].reshape(128, 2048)
    xa[pl.ds(mx, 1), pl.ds(my, 1)] = dot(pick_a[...], flat).astype(BF16)[None, None]
    xb[pl.ds(mx, 1), pl.ds(my, 1)] = dot(pick_b[...], flat).astype(BF16)[None, None]
    for c in sends:
        c.wait_send()

    sent = []

    def push(h, x, at, cols, g, k, device):
        place = x.at[at + (every, cols)] if cols is not None else x.at[at]
        c = remote(place, place, g_send.at[h, g, k], g_recv.at[h, g, k], device)
        c.start()
        sent.append(c)
        return c

    first, second = [], [[None] * 4, [None] * 4]

    def second_start(i, g, u):
        h, x = halves[i], xs[i]
        at = h.unit(u, h.q)
        second[i][g] = [
            push(i, x, at, None, g + 1, 0, h.two(1)),
            push(i, x, at, None, g + 1, 1, h.two(-1)),
        ]

    def second_pass(i, g, u):
        h, x = halves[i], xs[i]
        second[i][g][0].wait_recv()
        a = push(i, x, h.unit(u, wrap(h.q - 1, 4)), lo, g + 1, 2, h.two(1))
        second[i][g][1].wait_recv()
        b = push(i, x, h.unit(u, wrap(h.q + 1, 4)), hi, g + 1, 3, h.two(-1))
        second[i][g] += [a, b]

    for i, (h, x) in enumerate(zip(halves, xs)):
        at = h.unit(h.p, h.q)
        first.append(
            [push(i, x, at, None, 0, 0, h.one(1)), push(i, x, at, None, 0, 1, h.one(-1))]
        )
    for i, h in enumerate(halves):
        second_start(i, 0, h.p)
    for i, (h, x) in enumerate(zip(halves, xs)):
        left, right = wrap(h.p - 1, 4), wrap(h.p + 1, 4)
        first[i][0].wait_recv()
        first[i].append(push(i, x, h.unit(left, h.q), lo, 0, 2, h.one(1)))
        first[i][1].wait_recv()
        first[i].append(push(i, x, h.unit(right, h.q), hi, 0, 3, h.one(-1)))
        second_start(i, 1, left)
        second_start(i, 2, right)
    for i, h in enumerate(halves):
        first[i][2].wait_recv()
        first[i][3].wait_recv()
        second_start(i, 3, wrap(h.p + 2, 4))

    def gate_up(i, v):
        h = halves[i]
        at = h.group(v)
        lhs[...] = xs[i][at].reshape(160, 2048)

        @pl.loop(0, 6)
        def _(j):
            cols = pl.ds(pl.multiple_of(j * 256, 256), 256)
            part = dot(lhs[...], wgu[pl.ds(i * 2048, 2048), cols])
            place = at + (every, cols)
            acc[place] = acc[place] + part.reshape(4, 40, 256)

    loads[0].wait()
    loads[1].wait()
    for i, h in enumerate(halves):
        gate_up(i, h.q)
    for g in range(4):
        for i, h in enumerate(halves):
            u = (h.p, wrap(h.p - 1, 4), wrap(h.p + 1, 4), wrap(h.p + 2, 4))[g]
            second_pass(i, g, u)
    for i, h in enumerate(halves):
        gate_up(i, wrap(h.q - 1, 4))
        gate_up(i, wrap(h.q + 1, 4))
    for i, h in enumerate(halves):
        for g in range(4):
            second[i][g][2].wait_recv()
            second[i][g][3].wait_recv()
        gate_up(i, wrap(h.q + 2, 4))

    @pl.loop(0, 16)
    def _(n):
        at = (n // 4, n % 4)
        gate = acc[at + (every, pl.ds(0, 768))]
        up = acc[at + (every, pl.ds(768, 768))]
        hid[at] = (gate * jax.nn.sigmoid(gate) * up).astype(BF16)

    loads[2].wait()

    def down(i, v):
        at = halves[i].group(v)
        lhs[:, pl.ds(0, 768)] = hid[at].reshape(160, 768)

        @pl.loop(0, 8)
        def _(j):
            start = pl.multiple_of(j * 256, 256)
            part = dot(lhs[:, pl.ds(0, 768)], wd[:, pl.ds(i * 2048 + start, 256)])
            os[i][at + (every, pl.ds(start, 256))] = part.reshape(4, 40, 256).astype(BF16)

    def send(src, dst, i, stage, k, device):
        c = remote(src, dst, s_send.at[i, stage, k], s_recv.at[i, stage, k], device)
        c.start()
        sent.append(c)
        return c

    def ring_far(i, stage, chunk, ahead, behind, step):
        return [
            send(chunk(2, lo), ahead, i, stage, 0, step(1)),
            send(chunk(2, hi), behind, i, stage, 1, step(-1)),
        ]

    def add_into(ref, at, other, other_at):
        ref[at] = (ref[at].astype(F32) + other[other_at].astype(F32)).astype(BF16)

    stage_one = [None, None]
    for i, h in enumerate(halves):
        down(i, wrap(h.q + 2, 4))
        o, at = os[i], h.group(wrap(h.q + 2, 4))
        stage_one[i] = [
            send(o.at[at + (every, lo)], far.at[i, 0], i, 0, 0, h.two(1)),
            send(o.at[at + (every, hi)], far.at[i, 1], i, 0, 1, h.two(-1)),
        ]
    for i, h in enumerate(halves):
        o = os[i]
        down(i, wrap(h.q + 1, 4))
        at = h.group(wrap(h.q + 1, 4))
        stage_one[i].append(
            send(o.at[at + (every, hi)], near.at[i, 0, :, :, hi], i, 0, 2, h.two(1))
        )
        down(i, wrap(h.q - 1, 4))
        at = h.group(wrap(h.q - 1, 4))
        stage_one[i].append(
            send(o.at[at + (every, lo)], near.at[i, 1, :, :, lo], i, 0, 3, h.two(-1))
        )
    for i, h in enumerate(halves):
        down(i, h.q)
    for i, h in enumerate(halves):
        o = os[i]
        stage_one[i][0].wait_recv()
        at = h.group(wrap(h.q + 1, 4)) + (every, lo)
        add_into(o, at, far, (i, 0))
        stage_one[i].append(send(o.at[at], near.at[i, 0, :, :, lo], i, 0, 4, h.two(1)))
        stage_one[i][1].wait_recv()
        at = h.group(wrap(h.q - 1, 4)) + (every, hi)
        add_into(o, at, far, (i, 1))
        stage_one[i].append(send(o.at[at], near.at[i, 1, :, :, hi], i, 0, 5, h.two(-1)))

    stage_two = [None, None]
    for i, h in enumerate(halves):
        for c in stage_one[i][2:]:
            c.wait_recv()

        def total(u):
            mine = os[i][h.unit(u, h.q)].astype(F32)
            tot[i, u] = (mine + near[i, 0, u].astype(F32) + near[i, 1, u].astype(F32)).astype(BF16)

        opposite, ahead, behind = wrap(h.p + 2, 4), wrap(h.p + 1, 4), wrap(h.p - 1, 4)
        total(opposite)
        stage_two[i] = [
            send(tot.at[i, opposite, :, lo], far2.at[i, 0], i, 1, 0, h.one(1)),
            send(tot.at[i, opposite, :, hi], far2.at[i, 1], i, 1, 1, h.one(-1)),
        ]
        total(ahead)
        total(behind)
        stage_two[i].append(send(tot.at[i, ahead, :, hi], near2.at[i, 0, :, hi], i, 1, 2, h.one(1)))
        stage_two[i].append(
            send(tot.at[i, behind, :, lo], near2.at[i, 1, :, lo], i, 1, 3, h.one(-1))
        )
        total(h.p)
    for i, h in enumerate(halves):
        ahead, behind = wrap(h.p + 1, 4), wrap(h.p - 1, 4)
        stage_two[i][0].wait_recv()
        add_into(tot, (i, ahead, every, lo), far2, (i, 0))
        stage_two[i].append(send(tot.at[i, ahead, :, lo], near2.at[i, 0, :, lo], i, 1, 4, h.one(1)))
        stage_two[i][1].wait_recv()
        add_into(tot, (i, behind, every, hi), far2, (i, 1))
        stage_two[i].append(
            send(tot.at[i, behind, :, hi], near2.at[i, 1, :, hi], i, 1, 5, h.one(-1))
        )
    ends = []
    for i, h in enumerate(halves):
        for c in stage_two[i][2:]:
            c.wait_recv()
        final = (
            tot[i, h.p].astype(F32) + near2[i, 0].astype(F32) + near2[i, 1].astype(F32)
        ).astype(BF16)
        ends.append(final)

    across = (((0,), (0,)), ((), ()))
    back = lax.dot_general(pick_a[...], ends[0], across, preferred_element_type=F32)
    back = back + lax.dot_general(pick_b[...], ends[1], across, preferred_element_type=F32)
    go[...] = back.astype(BF16).reshape(8, 16, 2048)
    sends = []
    for d in range(1, 8):
        peer = lax.rem(exp + d, 8)
        c = remote(go.at[peer], rback.at[exp], r_send.at[d], r_recv.at[d], {"exp": peer})
        c.start()
        sends.append(c)
    rback[pl.ds(exp, 1)] = go[pl.ds(exp, 1)]
    for c in sends:
        c.wait_recv()
    flat = rback[...].reshape(128, 2048)
    g = gates[...]
    for i in range(2):
        cols = pl.ds(i * 2048, 2048)
        mix = g[:, 0:1] * dot(fetch[i, 0], flat) + g[:, 1:2] * dot(fetch[i, 1], flat)
        out[:, cols] = (stream[:, cols] + mix).astype(BF16)
    for c in sends + sent:
        c.wait_send()


def expert_layer(normed, stream, gates, expert_ids, w_gate, w_up, w_down):
    flat_ids = expert_ids.reshape(-1)
    hits = (flat_ids[:, None] == jnp.arange(8, dtype=jnp.int32)[None, :]).astype(jnp.int32)
    earlier = jnp.cumsum(hits, axis=0) - hits
    slot = jnp.sum(earlier * hits, axis=1)
    target = (flat_ids * 16 + slot).reshape(16, 2)
    places = jnp.arange(128, dtype=jnp.int32)
    first = target[:, 0][:, None] == places[None, :]
    both = first | (target[:, 1][:, None] == places[None, :])
    spread_a = both.T.astype(BF16)
    spread_b = jnp.roll(spread_a, 8, axis=0)
    fetch_a = jnp.stack([first, both & ~first]).astype(BF16)
    fetch = jnp.stack([fetch_a, jnp.roll(fetch_a, 8, axis=2)])
    pick = np.zeros((2, 40, 128), np.float32)
    for j in range(8):
        for s in range(5):
            pick[0, j * 5 + s, j * 16 + s] = 1.0
            pick[1, j * 5 + s, j * 16 + 8 + s] = 1.0
    pick_a, pick_b = jnp.asarray(pick[0], BF16), jnp.asarray(pick[1], BF16)
    vmem = pl.BlockSpec(memory_space=pltpu.VMEM)
    anywhere = pl.BlockSpec(memory_space=pl.ANY)
    dma = pltpu.SemaphoreType.DMA
    return pl.pallas_call(
        moe_kernel,
        out_shape=jax.ShapeDtypeStruct((16, 4096), BF16),
        in_specs=[vmem] * 8 + [anywhere] * 3,
        out_specs=vmem,
        scratch_shapes=[
            pltpu.VMEM((8, 16, 2048), BF16),
            pltpu.VMEM((8, 16, 2048), BF16),
            pltpu.VMEM((8, 16, 2048), BF16),
            pltpu.VMEM((4, 4, 40, 2048), BF16),
            pltpu.VMEM((4, 4, 40, 2048), BF16),
            pltpu.VMEM((4096, 1536), BF16),
            pltpu.VMEM((768, 4096), BF16),
            pltpu.VMEM((160, 2048), BF16),
            pltpu.VMEM((4, 4, 40, 1536), F32),
            pltpu.VMEM((4, 4, 40, 768), BF16),
            pltpu.VMEM((4, 4, 40, 2048), BF16),
            pltpu.VMEM((4, 4, 40, 2048), BF16),
            pltpu.VMEM((2, 2, 4, 40, 1024), BF16),
            pltpu.VMEM((2, 2, 4, 40, 2048), BF16),
            pltpu.VMEM((2, 4, 40, 2048), BF16),
            pltpu.VMEM((2, 2, 40, 1024), BF16),
            pltpu.VMEM((2, 2, 40, 2048), BF16),
            dma((3,)),
            dma((8,)),
            dma((8,)),
            dma((2, 5, 4)),
            dma((2, 5, 4)),
            dma((2, 2, 6)),
            dma((2, 2, 6)),
            dma((8,)),
            dma((8,)),
        ],
        compiler_params=pltpu.CompilerParams(
            collective_id=1, has_side_effects=True, vmem_limit_bytes=VMEM_LIMIT
        ),
        cost_estimate=pl.CostEstimate(flops=12_000_000_000, bytes_accessed=19_000_000, transcendentals=0),
    )(normed, stream, gates, spread_a, spread_b, pick_a, pick_b, fetch, w_gate, w_up, w_down)


LOG2E = 1.4426950408889634


def mixer_kernel(
    mixer_in,
    gate_in,
    conv_weight,
    conv_bias,
    x_proj,
    dt_proj,
    dt_bias,
    decay_rate,
    skip,
    out_proj,
    residual,
    gain,
    router,
    expert_ids,
    stream_out,
    normed_out,
    gates_out,
    rim,
    padded,
    conv_out,
    part,
    parts,
    proj,
    bc_v,
    bc_s,
    step_t,
    drive_t,
    cum_t,
    y_t,
    rate_t,
    enter_t,
    fin_own,
    fin_y,
    sum_y,
    fin_x,
    sum_x,
    opg,
    ga,
    zs,
    rz,
    ms,
    mo,
    h_sem,
    a_send,
    a_recv,
    b_send,
    b_recv,
    o_send,
    o_recv,
    c_send,
    c_recv,
    g_send,
    g_recv,
    z_send,
    z_recv,
    m_send,
    m_recv,
    l_sem,
):
    ctx, exp = lax.axis_index("ctx"), lax.axis_index("exp")
    mx, my = ctx // 4, ctx % 4
    every = slice(None)

    def along_x(d):
        return {"ctx": wrap(mx + d, 4) * 4 + my}

    def along_y(d):
        return {"ctx": mx * 4 + wrap(my + d, 4)}

    def peer(d):
        return {"exp": lax.rem(exp + d, 8)}

    behind, ahead = {"ctx": lax.rem(ctx + 15, 16)}, {"ctx": lax.rem(ctx + 1, 16)}
    greet(
        [behind, ahead]
        + [along_x(d) for d in (1, 2, -1)]
        + [along_y(d) for d in (1, 2, -1)]
        + [peer(d) for d in range(1, 8)]
    )
    sent = []

    def send(src, dst, ss, rs, device):
        c = remote(src, dst, ss, rs, device)
        c.start()
        sent.append(c)
        return c

    halo = send(mixer_in.at[pl.ds(112, 16)], rim, h_sem.at[0], h_sem.at[1], ahead)
    columns = [
        send(out_proj, opg.at[my], o_send.at[0], o_recv.at[0], along_y(1)),
        send(out_proj, opg.at[my], o_send.at[1], o_recv.at[1], along_y(-1)),
    ]
    opg[pl.ds(my, 1)] = out_proj[...][None]
    padded[pl.ds(8, 128), :] = mixer_in[...].astype(F32)
    for g in range(8):
        rate_t[pl.ds(g, 16, stride=8), :] = decay_rate[:, g * 128 : (g + 1) * 128] * (-LOG2E)
    halo.wait_recv()
    keep = jnp.where(ctx > 0, 1.0, 0.0).astype(F32)
    padded[pl.ds(0, 8), :] = rim[pl.ds(0, 16), :].astype(F32)[8:] * keep
    for g in range(8):
        cols = pl.ds(g * 128, 128)
        total = conv_bias[:, cols] + conv_weight[0:1, cols] * padded[pl.ds(5, 128), cols]
        for k in range(1, 4):
            total = total + conv_weight[k : k + 1, cols] * padded[pl.ds(5 + k, 128), cols]
        conv_out[:, cols] = (total * jax.nn.sigmoid(total)).astype(BF16)

    part[...] = dot(conv_out[...], x_proj[...]).reshape(8, 16, 544)
    scatter = [
        send(part.at[lax.rem(exp + d, 8)], parts.at[exp], a_send.at[d], a_recv.at[d], peer(d))
        for d in range(1, 8)
    ]
    parts[pl.ds(exp, 1)] = part[pl.ds(exp, 1)]
    for c in scatter:
        c.wait_recv()
    total = parts[0]
    for j in range(1, 8):
        total = total + parts[j]
    proj[pl.ds(exp, 1)] = total[None]
    gather = [
        send(proj.at[exp], proj.at[exp], b_send.at[d], b_recv.at[d], peer(d)) for d in range(1, 8)
    ]
    top, low = pl.ds(0, 512), pl.ds(512, 512)
    left, right = wrap(my - 1, 4), wrap(my + 1, 4)
    columns[0].wait_recv()
    columns.append(
        send(opg.at[left, top], opg.at[left, top], o_send.at[2], o_recv.at[2], along_y(1))
    )
    columns[1].wait_recv()
    columns.append(
        send(opg.at[right, low], opg.at[right, low], o_send.at[3], o_recv.at[3], along_y(-1))
    )
    for c in gather:
        c.wait_recv()
    bc_v[:, pl.ds(0, 32)] = proj[:, :, pl.ds(512, 32)].reshape(128, 32)
    scalars = pltpu.make_async_copy(bc_v, bc_s, l_sem.at[0])
    scalars.start()
    step_low = proj[:, :, pl.ds(0, 512)].reshape(128, 512).astype(BF16)
    for j in range(4):
        cols = pl.ds(j * 256, 256)
        raw = dot(step_low, dt_proj[:, cols]) + dt_bias[:, cols]
        step = jnp.maximum(raw, 0.0) + jnp.log1p(jnp.exp(-jnp.abs(raw)))
        drive = step * conv_out[:, cols].astype(F32)
        for i in range(2):
            rows = pl.ds(j * 2 + i, 128, stride=8)
            step_t[rows, :] = step[:, i * 128 : (i + 1) * 128]
            drive_t[rows, :] = drive[:, i * 128 : (i + 1) * 128]
    scalars.wait()

    rates = [rate_t[pl.ds(n * 8, 8), :] for n in range(16)]
    zero = jnp.zeros((8, 128), F32)

    def scan_step(t, carry):
        states, running = carry
        rows = pl.ds(pl.multiple_of(t * 8, 8), 8)
        s, d = step_t[rows, :], drive_t[rows, :]
        outs = [zero, zero]
        after = []
        for n in range(16):
            h = jnp.exp2(rates[n] * s) * states[n] + bc_s[t, n] * d
            outs[n % 2] = outs[n % 2] + bc_s[t, 16 + n] * h
            after.append(h)
        running = running + s
        y_t[rows, :] = outs[0] + outs[1]
        cum_t[rows, :] = running
        return (tuple(after), running)

    states, running = lax.fori_loop(0, 128, scan_step, ((zero,) * 16, zero), unroll=2)

    def exchange(finals, total, fin, sums, place, base, step):
        for n in range(16):
            fin_own[base // 6, pl.ds(n * 8, 8), :] = finals[n].astype(BF16)
        sums[pl.ds(place, 1)] = total[None]
        fin[pl.ds(place, 1)] = fin_own[base // 6][None]
        moves = []
        for k, d in enumerate((1, -1, 2)):
            s, r = base + 2 * k, base + 2 * k + 1
            moves.append(
                send(fin_own.at[base // 6], fin.at[place], c_send.at[s], c_recv.at[s], step(d))
            )
            moves.append(send(sums.at[place], sums.at[place], c_send.at[r], c_recv.at[r], step(d)))
        for c in moves:
            c.wait_recv()

    exchange(states, running, fin_y, sum_y, my, 0, along_y)
    before, row_total = zero, zero
    for v in range(4):
        before = before + jnp.where(v < my, 1.0, 0.0).astype(F32) * sum_y[v]
        row_total = row_total + sum_y[v]
    row_final = []
    for n in range(16):
        entering, whole = zero, zero
        for v in range(4):
            own = fin_y[v, pl.ds(n * 8, 8), :].astype(F32)
            decay = jnp.exp2(rates[n] * sum_y[v])
            entering = jnp.where(v < my, decay * entering + own, entering)
            whole = decay * whole + own
        enter_t[pl.ds(n * 8, 8), :] = entering
        row_final.append(whole)
    exchange(row_final, row_total, fin_x, sum_x, mx, 6, along_x)
    for n in range(16):
        entering = zero
        for u in range(4):
            own = fin_x[u, pl.ds(n * 8, 8), :].astype(F32)
            decay = jnp.exp2(rates[n] * sum_x[u])
            entering = jnp.where(u < mx, decay * entering + own, entering)
        rows = pl.ds(n * 8, 8)
        enter_t[rows, :] = enter_t[rows, :] + jnp.exp2(rates[n] * before) * entering

    def add_entering(t, carry):
        rows = pl.ds(pl.multiple_of(t * 8, 8), 8)
        c = cum_t[rows, :]
        outs = [y_t[rows, :], zero]
        for n in range(16):
            outs[n % 2] = outs[n % 2] + bc_s[t, 16 + n] * (jnp.exp2(rates[n] * c) * entered[n])
        y_t[rows, :] = outs[0] + outs[1]
        return carry

    entered = [enter_t[pl.ds(n * 8, 8), :] for n in range(16)]
    moves = []
    for half in range(2):
        lax.fori_loop(half * 64, half * 64 + 64, add_entering, 0, unroll=2)
        rows = pl.ds(half * 64, 64)
        for g in range(8):
            cols = pl.ds(g * 128, 128)
            y = y_t[pl.ds(half * 512 + g, 64, stride=8), :]
            y = y + skip[:, cols] * conv_out[rows, cols].astype(F32)
            z = gate_in[rows, cols].astype(F32)
            ga[pl.ds(mx, 1), rows, cols] = (y * (z * jax.nn.sigmoid(z))).astype(BF16)[None]
        place = ga.at[mx, rows]
        for k, d in enumerate((1, -1)):
            s = half * 2 + k
            moves.append(send(place, place, g_send.at[s], g_recv.at[s], along_x(d)))

    def project(u):
        for v in range(4):
            cols = pl.ds(v * 256, 256)
            out = dot(ga[u], opg[v])
            zs[pl.ds(u, 1), :, :, cols] = out.astype(BF16).reshape(1, 8, 16, 256)
        rz[pl.ds(u, 1), pl.ds(exp, 1)] = zs[pl.ds(u, 1), pl.ds(exp, 1)]

    def scatter_group(k, u):
        return [
            send(zs.at[u, lax.rem(exp + d, 8)], rz.at[u, exp], z_send.at[k, d], z_recv.at[k, d], peer(d))
            for d in range(1, 8)
        ]

    for c in columns[2:]:
        c.wait_recv()
    left, right, far = wrap(mx - 1, 4), wrap(mx + 1, 4), wrap(mx + 2, 4)
    top, low = pl.ds(0, 64), pl.ds(64, 64)
    project(mx)
    groups = [scatter_group(0, mx)]
    moves[0].wait_recv()
    moves.append(send(ga.at[left, top], ga.at[left, top], g_send.at[4], g_recv.at[4], along_x(1)))
    moves[1].wait_recv()
    moves[3].wait_recv()
    moves.append(send(ga.at[right, low], ga.at[right, low], g_send.at[5], g_recv.at[5], along_x(-1)))
    moves[2].wait_recv()
    for k, u in ((1, left), (2, right)):
        project(u)
        groups.append(scatter_group(k, u))
    moves[4].wait_recv()
    moves[5].wait_recv()
    project(far)
    groups.append(scatter_group(3, far))
    backs = []
    for k, (u, d) in enumerate(((mx, 0), (left, -1), (right, 1), (far, 2))):
        for c in groups[k]:
            c.wait_recv()
        total = rz[u, 0].astype(F32)
        for j in range(1, 8):
            total = total + rz[u, j].astype(F32)
        if d == 0:
            mo[pl.ds(mx, 1)] = total[None]
        else:
            ms[k - 1] = total
            backs.append(send(ms.at[k - 1], mo.at[mx], m_send.at[k], m_recv.at[k], along_x(d)))
    for c in backs:
        c.wait_recv()

    squares = jnp.zeros((16, 1), F32)
    for u in range(4):
        cols = pl.ds(u * 1024, 1024)
        rows = residual[:, cols].astype(F32) + mo[u]
        stream_out[:, cols] = rows
        squares = squares + jnp.sum(rows * rows, axis=1, keepdims=True)
    scale = lax.rsqrt(squares * (1.0 / 4096.0) + 1e-06)
    logits = jnp.zeros((16, 8), F32)
    for u in range(4):
        cols = pl.ds(u * 1024, 1024)
        rows = (stream_out[:, cols] * scale * gain[:, cols]).astype(BF16)
        normed_out[:, cols] = rows
        logits = logits + dot(rows, router[cols, :])
    ids = expert_ids[...]
    lanes = lax.broadcasted_iota(jnp.int32, (16, 8), 1)
    signs = jnp.where(ids[:, 0:1] == lanes, 1.0, 0.0) - jnp.where(ids[:, 1:2] == lanes, 1.0, 0.0)
    first = jax.nn.sigmoid(jnp.sum(logits * signs, axis=1, keepdims=True))
    gates_out[:, 0:1] = first
    gates_out[:, 1:2] = 1.0 - first
    for c in sent:
        c.wait_send()


def mixer_layer(
    mixer_in,
    gate_in,
    conv_weight,
    conv_bias,
    x_proj,
    dt_proj,
    dt_bias,
    decay_rate,
    skip,
    out_proj,
    residual,
    gain,
    router,
    expert_ids,
):
    vmem = pl.BlockSpec(memory_space=pltpu.VMEM)
    dma = pltpu.SemaphoreType.DMA
    return pl.pallas_call(
        mixer_kernel,
        out_shape=[
            jax.ShapeDtypeStruct((16, 4096), F32),
            jax.ShapeDtypeStruct((16, 4096), BF16),
            jax.ShapeDtypeStruct((16, 2), F32),
        ],
        in_specs=[vmem] * 14,
        out_specs=[vmem] * 3,
        scratch_shapes=[
            pltpu.VMEM((16, 1024), BF16),
            pltpu.VMEM((136, 1024), F32),
            pltpu.VMEM((128, 1024), BF16),
            pltpu.VMEM((8, 16, 544), F32),
            pltpu.VMEM((8, 16, 544), F32),
            pltpu.VMEM((8, 16, 544), F32),
            pltpu.VMEM((128, 128), F32),
            pltpu.SMEM((128, 128), F32),
            pltpu.VMEM((1024, 128), F32),
            pltpu.VMEM((1024, 128), F32),
            pltpu.VMEM((1024, 128), F32),
            pltpu.VMEM((1024, 128), F32),
            pltpu.VMEM((128, 128), F32),
            pltpu.VMEM((128, 128), F32),
            pltpu.VMEM((2, 128, 128), BF16),
            pltpu.VMEM((4, 128, 128), BF16),
            pltpu.VMEM((4, 8, 128), F32),
            pltpu.VMEM((4, 128, 128), BF16),
            pltpu.VMEM((4, 8, 128), F32),
            pltpu.VMEM((4, 1024, 256), BF16),
            pltpu.VMEM((4, 128, 1024), BF16),
            pltpu.VMEM((4, 8, 16, 1024), BF16),
            pltpu.VMEM((4, 8, 16, 1024), BF16),
            pltpu.VMEM((3, 16, 1024), F32),
            pltpu.VMEM((4, 16, 1024), F32),
            dma((2,)),
            dma((8,)),
            dma((8,)),
            dma((8,)),
            dma((8,)),
            dma((4,)),
            dma((4,)),
            dma((12,)),
            dma((12,)),
            dma((6,)),
            dma((6,)),
            dma((4, 8)),
            dma((4, 8)),
            dma((4,)),
            dma((4,)),
            dma((1,)),
        ],
        compiler_params=pltpu.CompilerParams(
            collective_id=0, has_side_effects=True, vmem_limit_bytes=VMEM_LIMIT
        ),
        cost_estimate=pl.CostEstimate(flops=1_500_000_000, bytes_accessed=5_000_000, transcendentals=0),
    )(
        mixer_in,
        gate_in,
        conv_weight,
        conv_bias[None],
        x_proj,
        dt_proj,
        dt_bias[None],
        decay_rate,
        skip[None],
        out_proj,
        residual,
        gain[None],
        router,
        expert_ids,
    )


def shards(
    mixer_in,
    gate_in,
    conv_weight,
    conv_bias,
    x_proj,
    dt_proj,
    dt_bias,
    decay_rate,
    skip,
    out_proj,
    residual,
    gain,
    router,
    w_gate,
    w_up,
    w_down,
    expert_ids,
):
    stream, normed, gates = mixer_layer(
        mixer_in,
        gate_in,
        conv_weight,
        conv_bias,
        x_proj,
        dt_proj,
        dt_bias,
        decay_rate,
        skip,
        out_proj,
        residual,
        gain,
        router,
        expert_ids,
    )
    return expert_layer(normed, stream, gates, expert_ids, w_gate, w_up, w_down)


def solution(mesh):
    in_specs = (
        P("ctx", "exp"),
        P("ctx", "exp"),
        P(None, "exp"),
        P("exp"),
        P("exp", None),
        P(None, "exp"),
        P("exp"),
        P(None, "exp"),
        P("exp"),
        P("exp", "ctx"),
        P(("ctx", "exp"), None),
        P(),
        P(),
        P("exp", None, "ctx"),
        P("exp", None, "ctx"),
        P("exp", "ctx", None),
        P(("ctx", "exp"), None),
    )
    out_specs = P(("ctx", "exp"), None)
    return jax.shard_map(shards, mesh=mesh, in_specs=in_specs, out_specs=out_specs, check_vma=False)
```

```python
import jax
import jax.numpy as jnp
import numpy as np
from jax import lax
from jax.experimental import pallas as pl
from jax.experimental.pallas import tpu as pltpu
from jax.sharding import PartitionSpec as P

F32 = jnp.float32
BF16 = jnp.bfloat16
VMEM_LIMIT = 60 * 1024 * 1024


def remote(src, dst, send_sem, recv_sem, device):
    return pltpu.make_async_remote_copy(
        src_ref=src,
        dst_ref=dst,
        send_sem=send_sem,
        recv_sem=recv_sem,
        device_id=device,
        device_id_type=pl.DeviceIdType.MESH,
    )


def greet(devices):
    barrier = pltpu.get_barrier_semaphore()
    for device in devices:
        pl.semaphore_signal(barrier, inc=1, device_id=device, device_id_type=pl.DeviceIdType.MESH)
    pl.semaphore_wait(barrier, len(devices))


def wrap(index, count):
    return lax.rem(index + count, count)


def dot(a, b):
    return jnp.dot(a, b, preferred_element_type=F32)


def dot_t(a, b):
    return lax.dot_general(a, b, (((1,), (1,)), ((), ())), preferred_element_type=F32)


class Half:
    def __init__(self, half, mx, my):
        self.half = half
        self.mx, self.my = mx, my
        self.p, self.q = (mx, my) if half == 0 else (my, mx)

    def one(self, step):
        p = wrap(self.p + step, 4)
        return {"ctx": p * 4 + self.my if self.half == 0 else self.mx * 4 + p}

    def two(self, step):
        q = wrap(self.q + step, 4)
        return {"ctx": self.mx * 4 + q if self.half == 0 else q * 4 + self.my}

    def unit(self, u, v):
        return (u, v) if self.half == 0 else (v, u)

    def group(self, v):
        return (slice(None), v) if self.half == 0 else (v, slice(None))


LOG2E = 1.4426950408889634

INPUTS = (
    "mixer_in",
    "gate_in",
    "conv_weight",
    "conv_bias",
    "x_proj",
    "dt_proj",
    "dt_bias",
    "decay_rate",
    "skip",
    "out_proj",
    "residual",
    "gain",
    "router",
    "expert_ids",
    "w_gate",
    "w_up",
    "w_down",
    "pick_a",
    "pick_b",
)

SCRATCH = {
    "stream": pltpu.VMEM((16, 4096), F32),
    "normed": pltpu.VMEM((16, 4096), BF16),
    "spread": pltpu.VMEM((2, 128, 16), BF16),
    "fetch": pltpu.VMEM((2, 2, 128, 16), BF16),
    "rim": pltpu.VMEM((16, 1024), BF16),
    "padded": pltpu.VMEM((136, 1024), F32),
    "conv_out": pltpu.VMEM((128, 1024), BF16),
    "part": pltpu.VMEM((8, 16, 544), F32),
    "parts": pltpu.VMEM((8, 16, 544), F32),
    "low_rank": pltpu.VMEM((8, 16, 512), BF16),
    "maps": pltpu.VMEM((8, 16, 128), F32),
    "bc_s": pltpu.SMEM((8, 16, 128), F32),
    "step_t": pltpu.VMEM((1024, 128), F32),
    "drive_t": pltpu.VMEM((1024, 128), F32),
    "cum_t": pltpu.VMEM((1024, 128), F32),
    "y_t": pltpu.VMEM((1024, 128), F32),
    "rate_t": pltpu.VMEM((128, 128), F32),
    "enter_t": pltpu.VMEM((128, 128), F32),
    "fin_own": pltpu.VMEM((2, 128, 128), BF16),
    "fin_y": pltpu.VMEM((4, 128, 128), BF16),
    "sum_y": pltpu.VMEM((4, 8, 128), F32),
    "fin_x": pltpu.VMEM((4, 128, 128), BF16),
    "sum_x": pltpu.VMEM((4, 8, 128), F32),
    "opg": pltpu.VMEM((4, 1024, 256), BF16),
    "ga": pltpu.VMEM((4, 128, 1024), BF16),
    "zs": pltpu.VMEM((4, 8, 16, 1024), BF16),
    "rz": pltpu.VMEM((4, 8, 16, 1024), BF16),
    "ms": pltpu.VMEM((3, 16, 1024), F32),
    "mo": pltpu.VMEM((4, 16, 1024), F32),
    "h_sem": pltpu.SemaphoreType.DMA((2,)),
    "a_send": pltpu.SemaphoreType.DMA((8,)),
    "a_recv": pltpu.SemaphoreType.DMA((8,)),
    "b_send": pltpu.SemaphoreType.DMA((16,)),
    "b_recv": pltpu.SemaphoreType.DMA((16,)),
    "o_send": pltpu.SemaphoreType.DMA((4,)),
    "o_recv": pltpu.SemaphoreType.DMA((4,)),
    "c_send": pltpu.SemaphoreType.DMA((12,)),
    "c_recv": pltpu.SemaphoreType.DMA((12,)),
    "g_send": pltpu.SemaphoreType.DMA((6,)),
    "g_recv": pltpu.SemaphoreType.DMA((6,)),
    "z_send": pltpu.SemaphoreType.DMA((4, 8)),
    "z_recv": pltpu.SemaphoreType.DMA((4, 8)),
    "m_send": pltpu.SemaphoreType.DMA((4,)),
    "m_recv": pltpu.SemaphoreType.DMA((4,)),
    "l_sem": pltpu.SemaphoreType.DMA((1,)),
    "go": pltpu.VMEM((8, 16, 2048), BF16),
    "rcv": pltpu.VMEM((8, 16, 2048), BF16),
    "rback": pltpu.VMEM((8, 16, 2048), BF16),
    "xa": pltpu.VMEM((4, 4, 40, 2048), BF16),
    "xb": pltpu.VMEM((4, 4, 40, 2048), BF16),
    "wgu": pltpu.VMEM((4096, 1536), BF16),
    "wd": pltpu.VMEM((768, 4096), BF16),
    "lhs": pltpu.VMEM((160, 2048), BF16),
    "acc": pltpu.VMEM((4, 4, 40, 1536), F32),
    "hid": pltpu.VMEM((4, 4, 40, 768), BF16),
    "oa": pltpu.VMEM((4, 4, 40, 2048), BF16),
    "ob": pltpu.VMEM((4, 4, 40, 2048), BF16),
    "far": pltpu.VMEM((2, 2, 4, 40, 1024), BF16),
    "near": pltpu.VMEM((2, 2, 4, 40, 2048), BF16),
    "tot": pltpu.VMEM((2, 4, 40, 2048), BF16),
    "far2": pltpu.VMEM((2, 2, 40, 1024), BF16),
    "near2": pltpu.VMEM((2, 2, 40, 2048), BF16),
    "w_sem": pltpu.SemaphoreType.DMA((3,)),
    "d_send": pltpu.SemaphoreType.DMA((8,)),
    "d_recv": pltpu.SemaphoreType.DMA((8,)),
    "u_send": pltpu.SemaphoreType.DMA((2, 5, 4)),
    "u_recv": pltpu.SemaphoreType.DMA((2, 5, 4)),
    "s_send": pltpu.SemaphoreType.DMA((2, 2, 6)),
    "s_recv": pltpu.SemaphoreType.DMA((2, 2, 6)),
    "r_send": pltpu.SemaphoreType.DMA((8,)),
    "r_recv": pltpu.SemaphoreType.DMA((8,)),
}


def mixer(r, ctx, exp, mx, my):
    mixer_in = r["mixer_in"]
    gate_in = r["gate_in"]
    conv_weight = r["conv_weight"]
    conv_bias = r["conv_bias"]
    x_proj = r["x_proj"]
    dt_proj = r["dt_proj"]
    dt_bias = r["dt_bias"]
    decay_rate = r["decay_rate"]
    skip = r["skip"]
    out_proj = r["out_proj"]
    residual = r["residual"]
    gain = r["gain"]
    router = r["router"]
    expert_ids = r["expert_ids"]
    stream = r["stream"]
    normed = r["normed"]
    rim = r["rim"]
    padded = r["padded"]
    conv_out = r["conv_out"]
    part = r["part"]
    parts = r["parts"]
    low_rank = r["low_rank"]
    maps = r["maps"]
    bc_s = r["bc_s"]
    step_t = r["step_t"]
    drive_t = r["drive_t"]
    cum_t = r["cum_t"]
    y_t = r["y_t"]
    rate_t = r["rate_t"]
    enter_t = r["enter_t"]
    fin_own = r["fin_own"]
    fin_y = r["fin_y"]
    sum_y = r["sum_y"]
    fin_x = r["fin_x"]
    sum_x = r["sum_x"]
    opg = r["opg"]
    ga = r["ga"]
    zs = r["zs"]
    rz = r["rz"]
    ms = r["ms"]
    mo = r["mo"]
    h_sem = r["h_sem"]
    a_send = r["a_send"]
    a_recv = r["a_recv"]
    b_send = r["b_send"]
    b_recv = r["b_recv"]
    o_send = r["o_send"]
    o_recv = r["o_recv"]
    c_send = r["c_send"]
    c_recv = r["c_recv"]
    g_send = r["g_send"]
    g_recv = r["g_recv"]
    z_send = r["z_send"]
    z_recv = r["z_recv"]
    m_send = r["m_send"]
    m_recv = r["m_recv"]
    l_sem = r["l_sem"]
    every = slice(None)

    def along_x(d):
        return {"ctx": wrap(mx + d, 4) * 4 + my}

    def along_y(d):
        return {"ctx": mx * 4 + wrap(my + d, 4)}

    def peer(d):
        return {"exp": lax.rem(exp + d, 8)}

    ahead = {"ctx": lax.rem(ctx + 1, 16)}
    sent = []

    def send(src, dst, ss, rs, device):
        c = remote(src, dst, ss, rs, device)
        c.start()
        sent.append(c)
        return c

    halo = send(mixer_in.at[pl.ds(112, 16)], rim, h_sem.at[0], h_sem.at[1], ahead)
    columns = [
        send(out_proj, opg.at[my], o_send.at[0], o_recv.at[0], along_y(1)),
        send(out_proj, opg.at[my], o_send.at[1], o_recv.at[1], along_y(-1)),
    ]
    opg[pl.ds(my, 1)] = out_proj[...][None]
    padded[pl.ds(8, 128), :] = mixer_in[...].astype(F32)
    for g in range(8):
        rate_t[pl.ds(g, 16, stride=8), :] = decay_rate[:, g * 128 : (g + 1) * 128] * (-LOG2E)
    halo.wait_recv()
    keep = jnp.where(ctx > 0, 1.0, 0.0).astype(F32)
    padded[pl.ds(0, 8), :] = rim[pl.ds(0, 16), :].astype(F32)[8:] * keep
    for g in range(8):
        cols = pl.ds(g * 128, 128)
        total = conv_bias[:, cols] + conv_weight[0:1, cols] * padded[pl.ds(5, 128), cols]
        for k in range(1, 4):
            total = total + conv_weight[k : k + 1, cols] * padded[pl.ds(5 + k, 128), cols]
        conv_out[:, cols] = (total * jax.nn.sigmoid(total)).astype(BF16)

    part[...] = dot_t(conv_out[...], x_proj[...]).reshape(8, 16, 544)
    scatter = [
        send(part.at[lax.rem(exp + d, 8)], parts.at[exp], a_send.at[d], a_recv.at[d], peer(d))
        for d in range(1, 8)
    ]
    parts[pl.ds(exp, 1)] = part[pl.ds(exp, 1)]
    for c in scatter:
        c.wait_recv()
    total = parts[0]
    for j in range(1, 8):
        total = total + parts[j]
    low_rank[pl.ds(exp, 1)] = total[:, :512].astype(BF16)[None]
    maps[pl.ds(exp, 1), :, pl.ds(0, 32)] = total[:, 512:][None]
    gather = []
    for d in range(1, 8):
        for k, ref in enumerate((low_rank, maps)):
            s = 2 * d + k
            gather.append(send(ref.at[exp], ref.at[exp], b_send.at[s], b_recv.at[s], peer(d)))
    top, low = pl.ds(0, 512), pl.ds(512, 512)
    left, right = wrap(my - 1, 4), wrap(my + 1, 4)
    columns[0].wait_recv()
    columns.append(
        send(opg.at[left, top], opg.at[left, top], o_send.at[2], o_recv.at[2], along_y(1))
    )
    columns[1].wait_recv()
    columns.append(
        send(opg.at[right, low], opg.at[right, low], o_send.at[3], o_recv.at[3], along_y(-1))
    )
    for c in gather:
        c.wait_recv()
    scalars = pltpu.make_async_copy(maps, bc_s, l_sem.at[0])
    scalars.start()
    step_low = low_rank[...].reshape(128, 512)
    for j in range(4):
        cols = pl.ds(j * 256, 256)
        raw = dot(step_low, dt_proj[:, cols]) + dt_bias[:, cols]
        step = jnp.maximum(raw, 0.0) + jnp.log1p(jnp.exp(-jnp.abs(raw)))
        drive = step * conv_out[:, cols].astype(F32)
        for i in range(2):
            rows = pl.ds(j * 2 + i, 128, stride=8)
            step_t[rows, :] = step[:, i * 128 : (i + 1) * 128]
            drive_t[rows, :] = drive[:, i * 128 : (i + 1) * 128]
    scalars.wait()

    rates = [rate_t[pl.ds(n * 8, 8), :] for n in range(16)]
    zero = jnp.zeros((8, 128), F32)

    def scan_step(t, carry):
        states, running = carry
        rows = pl.ds(pl.multiple_of(t * 8, 8), 8)
        s, d = step_t[rows, :], drive_t[rows, :]
        outs = [zero, zero]
        after = []
        for n in range(16):
            h = jnp.exp2(rates[n] * s) * states[n] + bc_s[t // 16, t % 16, n] * d
            outs[n % 2] = outs[n % 2] + bc_s[t // 16, t % 16, 16 + n] * h
            after.append(h)
        running = running + s
        y_t[rows, :] = outs[0] + outs[1]
        cum_t[rows, :] = running
        return (tuple(after), running)

    states, running = lax.fori_loop(0, 128, scan_step, ((zero,) * 16, zero), unroll=2)

    def exchange(finals, total, fin, sums, place, base, step):
        for n in range(16):
            fin_own[base // 6, pl.ds(n * 8, 8), :] = finals[n].astype(BF16)
        sums[pl.ds(place, 1)] = total[None]
        fin[pl.ds(place, 1)] = fin_own[base // 6][None]
        moves = []
        for k, d in enumerate((1, -1, 2)):
            s, r = base + 2 * k, base + 2 * k + 1
            moves.append(
                send(fin_own.at[base // 6], fin.at[place], c_send.at[s], c_recv.at[s], step(d))
            )
            moves.append(send(sums.at[place], sums.at[place], c_send.at[r], c_recv.at[r], step(d)))
        for c in moves:
            c.wait_recv()

    exchange(states, running, fin_y, sum_y, my, 0, along_y)
    before, row_total = zero, zero
    for v in range(4):
        before = before + jnp.where(v < my, 1.0, 0.0).astype(F32) * sum_y[v]
        row_total = row_total + sum_y[v]
    row_final = []
    for n in range(16):
        entering, whole = zero, zero
        for v in range(4):
            own = fin_y[v, pl.ds(n * 8, 8), :].astype(F32)
            decay = jnp.exp2(rates[n] * sum_y[v])
            entering = jnp.where(v < my, decay * entering + own, entering)
            whole = decay * whole + own
        enter_t[pl.ds(n * 8, 8), :] = entering
        row_final.append(whole)
    exchange(row_final, row_total, fin_x, sum_x, mx, 6, along_x)
    for n in range(16):
        entering = zero
        for u in range(4):
            own = fin_x[u, pl.ds(n * 8, 8), :].astype(F32)
            decay = jnp.exp2(rates[n] * sum_x[u])
            entering = jnp.where(u < mx, decay * entering + own, entering)
        rows = pl.ds(n * 8, 8)
        enter_t[rows, :] = enter_t[rows, :] + jnp.exp2(rates[n] * before) * entering

    def add_entering(t, carry):
        rows = pl.ds(pl.multiple_of(t * 8, 8), 8)
        c = cum_t[rows, :]
        outs = [y_t[rows, :], zero]
        for n in range(16):
            outs[n % 2] = outs[n % 2] + bc_s[t // 16, t % 16, 16 + n] * (jnp.exp2(rates[n] * c) * entered[n])
        y_t[rows, :] = outs[0] + outs[1]
        return carry

    entered = [enter_t[pl.ds(n * 8, 8), :] for n in range(16)]
    moves = []
    for half in range(2):
        lax.fori_loop(half * 64, half * 64 + 64, add_entering, 0, unroll=2)
        rows = pl.ds(half * 64, 64)
        for g in range(8):
            cols = pl.ds(g * 128, 128)
            y = y_t[pl.ds(half * 512 + g, 64, stride=8), :]
            y = y + skip[:, cols] * conv_out[rows, cols].astype(F32)
            z = gate_in[rows, cols].astype(F32)
            ga[pl.ds(mx, 1), rows, cols] = (y * (z * jax.nn.sigmoid(z))).astype(BF16)[None]
        place = ga.at[mx, rows]
        for k, d in enumerate((1, -1)):
            s = half * 2 + k
            moves.append(send(place, place, g_send.at[s], g_recv.at[s], along_x(d)))

    def project(u):
        for v in range(4):
            cols = pl.ds(v * 256, 256)
            out = dot(ga[u], opg[v])
            zs[pl.ds(u, 1), :, :, cols] = out.astype(BF16).reshape(1, 8, 16, 256)
        rz[pl.ds(u, 1), pl.ds(exp, 1)] = zs[pl.ds(u, 1), pl.ds(exp, 1)]

    def scatter_group(k, u):
        return [
            send(zs.at[u, lax.rem(exp + d, 8)], rz.at[u, exp], z_send.at[k, d], z_recv.at[k, d], peer(d))
            for d in range(1, 8)
        ]

    for c in columns[2:]:
        c.wait_recv()
    left, right, far = wrap(mx - 1, 4), wrap(mx + 1, 4), wrap(mx + 2, 4)
    top, low = pl.ds(0, 64), pl.ds(64, 64)
    project(mx)
    groups = [scatter_group(0, mx)]
    moves[0].wait_recv()
    moves.append(send(ga.at[left, top], ga.at[left, top], g_send.at[4], g_recv.at[4], along_x(1)))
    moves[1].wait_recv()
    moves[3].wait_recv()
    moves.append(send(ga.at[right, low], ga.at[right, low], g_send.at[5], g_recv.at[5], along_x(-1)))
    moves[2].wait_recv()
    for k, u in ((1, left), (2, right)):
        project(u)
        groups.append(scatter_group(k, u))
    moves[4].wait_recv()
    moves[5].wait_recv()
    project(far)
    groups.append(scatter_group(3, far))
    backs = []
    for k, (u, d) in enumerate(((mx, 0), (left, -1), (right, 1), (far, 2))):
        for c in groups[k]:
            c.wait_recv()
        total = rz[u, 0].astype(F32)
        for j in range(1, 8):
            total = total + rz[u, j].astype(F32)
        if d == 0:
            mo[pl.ds(mx, 1)] = total[None]
        else:
            ms[k - 1] = total
            backs.append(send(ms.at[k - 1], mo.at[mx], m_send.at[k], m_recv.at[k], along_x(d)))
    for c in backs:
        c.wait_recv()

    squares = jnp.zeros((16, 1), F32)
    for u in range(4):
        cols = pl.ds(u * 1024, 1024)
        rows = residual[:, cols].astype(F32) + mo[u]
        stream[:, cols] = rows
        squares = squares + jnp.sum(rows * rows, axis=1, keepdims=True)
    scale = lax.rsqrt(squares * (1.0 / 4096.0) + 1e-06)
    logits = jnp.zeros((8, 16), F32)
    for u in range(4):
        cols = pl.ds(u * 1024, 1024)
        rows = (stream[:, cols] * scale * gain[:, cols]).astype(BF16)
        normed[:, cols] = rows
        logits = logits + dot_t(router[:, cols], rows)
    ids = expert_ids[...]
    lanes = lax.broadcasted_iota(jnp.int32, (8, 16), 0)
    signs = jnp.where(ids[0:1] == lanes, 1.0, 0.0) - jnp.where(ids[1:2] == lanes, 1.0, 0.0)
    first = jax.nn.sigmoid(jnp.sum(logits * signs, axis=0, keepdims=True))
    return first, sent


def experts(r, gate_row, sent, out, exp, mx, my, halves, loads):
    pick_a = r["pick_a"]
    pick_b = r["pick_b"]
    stream = r["stream"]
    normed = r["normed"]
    spread = r["spread"]
    fetch = r["fetch"]
    go = r["go"]
    rcv = r["rcv"]
    rback = r["rback"]
    xa = r["xa"]
    xb = r["xb"]
    wgu = r["wgu"]
    wd = r["wd"]
    lhs = r["lhs"]
    acc = r["acc"]
    hid = r["hid"]
    oa = r["oa"]
    ob = r["ob"]
    far = r["far"]
    near = r["near"]
    tot = r["tot"]
    far2 = r["far2"]
    near2 = r["near2"]
    d_send = r["d_send"]
    d_recv = r["d_recv"]
    u_send = r["u_send"]
    u_recv = r["u_recv"]
    s_send = r["s_send"]
    s_recv = r["s_recv"]
    r_send = r["r_send"]
    r_recv = r["r_recv"]
    xs, os = (xa, xb), (oa, ob)
    lo, hi = pl.ds(0, 1024), pl.ds(1024, 1024)
    every = slice(None)

    rows = normed[...]
    packed = dot(spread[0], rows[:, :2048]) + dot(spread[1], rows[:, 2048:])
    go[...] = packed.astype(BF16).reshape(8, 16, 2048)
    sends = []
    for d in range(1, 8):
        peer = lax.rem(exp + d, 8)
        c = remote(go.at[peer], rcv.at[exp], d_send.at[d], d_recv.at[d], {"exp": peer})
        c.start()
        sends.append(c)
    rcv[pl.ds(exp, 1)] = go[pl.ds(exp, 1)]
    acc[...] = jnp.zeros_like(acc)
    for c in sends:
        c.wait_recv()
    flat = rcv[...].reshape(128, 2048)
    xa[pl.ds(mx, 1), pl.ds(my, 1)] = dot(pick_a[...], flat).astype(BF16)[None, None]
    xb[pl.ds(mx, 1), pl.ds(my, 1)] = dot(pick_b[...], flat).astype(BF16)[None, None]
    for c in sends:
        c.wait_send()

    def push(h, x, at, cols, g, k, device):
        place = x.at[at + (every, cols)] if cols is not None else x.at[at]
        c = remote(place, place, u_send.at[h, g, k], u_recv.at[h, g, k], device)
        c.start()
        sent.append(c)
        return c

    first, second = [], [[None] * 4, [None] * 4]

    def second_start(i, g, u):
        h, x = halves[i], xs[i]
        at = h.unit(u, h.q)
        second[i][g] = [
            push(i, x, at, None, g + 1, 0, h.two(1)),
            push(i, x, at, None, g + 1, 1, h.two(-1)),
        ]

    def second_pass(i, g, u):
        h, x = halves[i], xs[i]
        second[i][g][0].wait_recv()
        a = push(i, x, h.unit(u, wrap(h.q - 1, 4)), lo, g + 1, 2, h.two(1))
        second[i][g][1].wait_recv()
        b = push(i, x, h.unit(u, wrap(h.q + 1, 4)), hi, g + 1, 3, h.two(-1))
        second[i][g] += [a, b]

    for i, (h, x) in enumerate(zip(halves, xs)):
        at = h.unit(h.p, h.q)
        first.append(
            [push(i, x, at, None, 0, 0, h.one(1)), push(i, x, at, None, 0, 1, h.one(-1))]
        )
    for i, h in enumerate(halves):
        second_start(i, 0, h.p)
    for i, (h, x) in enumerate(zip(halves, xs)):
        left, right = wrap(h.p - 1, 4), wrap(h.p + 1, 4)
        first[i][0].wait_recv()
        first[i].append(push(i, x, h.unit(left, h.q), lo, 0, 2, h.one(1)))
        first[i][1].wait_recv()
        first[i].append(push(i, x, h.unit(right, h.q), hi, 0, 3, h.one(-1)))
        second_start(i, 1, left)
        second_start(i, 2, right)
    for i, h in enumerate(halves):
        first[i][2].wait_recv()
        first[i][3].wait_recv()
        second_start(i, 3, wrap(h.p + 2, 4))

    def gate_up(i, v):
        h = halves[i]
        at = h.group(v)
        lhs[...] = xs[i][at].reshape(160, 2048)

        @pl.loop(0, 6)
        def _(j):
            cols = pl.ds(pl.multiple_of(j * 256, 256), 256)
            part = dot(lhs[...], wgu[pl.ds(i * 2048, 2048), cols])
            place = at + (every, cols)
            acc[place] = acc[place] + part.reshape(4, 40, 256)

    loads[0].wait()
    loads[1].wait()
    for i, h in enumerate(halves):
        gate_up(i, h.q)
    for g in range(4):
        for i, h in enumerate(halves):
            u = (h.p, wrap(h.p - 1, 4), wrap(h.p + 1, 4), wrap(h.p + 2, 4))[g]
            second_pass(i, g, u)
    for i, h in enumerate(halves):
        gate_up(i, wrap(h.q - 1, 4))
        gate_up(i, wrap(h.q + 1, 4))
    for i, h in enumerate(halves):
        for g in range(4):
            second[i][g][2].wait_recv()
            second[i][g][3].wait_recv()
        gate_up(i, wrap(h.q + 2, 4))

    @pl.loop(0, 16)
    def _(n):
        at = (n // 4, n % 4)
        gate = acc[at + (every, pl.ds(0, 768))]
        up = acc[at + (every, pl.ds(768, 768))]
        hid[at] = (gate * jax.nn.sigmoid(gate) * up).astype(BF16)

    loads[2].wait()

    def down(i, v):
        at = halves[i].group(v)
        lhs[:, pl.ds(0, 768)] = hid[at].reshape(160, 768)

        @pl.loop(0, 8)
        def _(j):
            start = pl.multiple_of(j * 256, 256)
            part = dot(lhs[:, pl.ds(0, 768)], wd[:, pl.ds(i * 2048 + start, 256)])
            os[i][at + (every, pl.ds(start, 256))] = part.reshape(4, 40, 256).astype(BF16)

    def send(src, dst, i, stage, k, device):
        c = remote(src, dst, s_send.at[i, stage, k], s_recv.at[i, stage, k], device)
        c.start()
        sent.append(c)
        return c

    def ring_far(i, stage, chunk, ahead, behind, step):
        return [
            send(chunk(2, lo), ahead, i, stage, 0, step(1)),
            send(chunk(2, hi), behind, i, stage, 1, step(-1)),
        ]

    def add_into(ref, at, other, other_at):
        ref[at] = (ref[at].astype(F32) + other[other_at].astype(F32)).astype(BF16)

    stage_one = [None, None]
    for i, h in enumerate(halves):
        down(i, wrap(h.q + 2, 4))
        o, at = os[i], h.group(wrap(h.q + 2, 4))
        stage_one[i] = [
            send(o.at[at + (every, lo)], far.at[i, 0], i, 0, 0, h.two(1)),
            send(o.at[at + (every, hi)], far.at[i, 1], i, 0, 1, h.two(-1)),
        ]
    for i, h in enumerate(halves):
        o = os[i]
        down(i, wrap(h.q + 1, 4))
        at = h.group(wrap(h.q + 1, 4))
        stage_one[i].append(
            send(o.at[at + (every, hi)], near.at[i, 0, :, :, hi], i, 0, 2, h.two(1))
        )
        down(i, wrap(h.q - 1, 4))
        at = h.group(wrap(h.q - 1, 4))
        stage_one[i].append(
            send(o.at[at + (every, lo)], near.at[i, 1, :, :, lo], i, 0, 3, h.two(-1))
        )
    for i, h in enumerate(halves):
        down(i, h.q)
    for i, h in enumerate(halves):
        o = os[i]
        stage_one[i][0].wait_recv()
        at = h.group(wrap(h.q + 1, 4)) + (every, lo)
        add_into(o, at, far, (i, 0))
        stage_one[i].append(send(o.at[at], near.at[i, 0, :, :, lo], i, 0, 4, h.two(1)))
        stage_one[i][1].wait_recv()
        at = h.group(wrap(h.q - 1, 4)) + (every, hi)
        add_into(o, at, far, (i, 1))
        stage_one[i].append(send(o.at[at], near.at[i, 1, :, :, hi], i, 0, 5, h.two(-1)))

    stage_two = [None, None]
    for i, h in enumerate(halves):
        for c in stage_one[i][2:]:
            c.wait_recv()

        def total(u):
            mine = os[i][h.unit(u, h.q)].astype(F32)
            tot[i, u] = (mine + near[i, 0, u].astype(F32) + near[i, 1, u].astype(F32)).astype(BF16)

        opposite, ahead, behind = wrap(h.p + 2, 4), wrap(h.p + 1, 4), wrap(h.p - 1, 4)
        total(opposite)
        stage_two[i] = [
            send(tot.at[i, opposite, :, lo], far2.at[i, 0], i, 1, 0, h.one(1)),
            send(tot.at[i, opposite, :, hi], far2.at[i, 1], i, 1, 1, h.one(-1)),
        ]
        total(ahead)
        total(behind)
        stage_two[i].append(send(tot.at[i, ahead, :, hi], near2.at[i, 0, :, hi], i, 1, 2, h.one(1)))
        stage_two[i].append(
            send(tot.at[i, behind, :, lo], near2.at[i, 1, :, lo], i, 1, 3, h.one(-1))
        )
        total(h.p)
    for i, h in enumerate(halves):
        ahead, behind = wrap(h.p + 1, 4), wrap(h.p - 1, 4)
        stage_two[i][0].wait_recv()
        add_into(tot, (i, ahead, every, lo), far2, (i, 0))
        stage_two[i].append(send(tot.at[i, ahead, :, lo], near2.at[i, 0, :, lo], i, 1, 4, h.one(1)))
        stage_two[i][1].wait_recv()
        add_into(tot, (i, behind, every, hi), far2, (i, 1))
        stage_two[i].append(
            send(tot.at[i, behind, :, hi], near2.at[i, 1, :, hi], i, 1, 5, h.one(-1))
        )
    ends = []
    for i, h in enumerate(halves):
        for c in stage_two[i][2:]:
            c.wait_recv()
        final = (
            tot[i, h.p].astype(F32) + near2[i, 0].astype(F32) + near2[i, 1].astype(F32)
        ).astype(BF16)
        ends.append(final)

    across = (((0,), (0,)), ((), ()))
    back = lax.dot_general(pick_a[...], ends[0], across, preferred_element_type=F32)
    back = back + lax.dot_general(pick_b[...], ends[1], across, preferred_element_type=F32)
    go[...] = back.astype(BF16).reshape(8, 16, 2048)
    sends = []
    for d in range(1, 8):
        peer = lax.rem(exp + d, 8)
        c = remote(go.at[peer], rback.at[exp], r_send.at[d], r_recv.at[d], {"exp": peer})
        c.start()
        sends.append(c)
    rback[pl.ds(exp, 1)] = go[pl.ds(exp, 1)]
    for c in sends:
        c.wait_recv()
    flat = rback[...].reshape(128, 2048)
    eye = lax.broadcasted_iota(jnp.int32, (16, 16), 0) == lax.broadcasted_iota(
        jnp.int32, (16, 16), 1
    )
    gate = jnp.sum(jnp.where(eye, jnp.broadcast_to(gate_row, (16, 16)), 0.0), axis=1, keepdims=True)
    for i in range(2):
        cols = pl.ds(i * 2048, 2048)
        pair = [
            lax.dot_general(fetch[i, k], flat, across, preferred_element_type=F32)
            for k in range(2)
        ]
        mix = gate * pair[0] + (1.0 - gate) * pair[1]
        out[:, cols] = (stream[:, cols] + mix).astype(BF16)
    for c in sends + sent:
        c.wait_send()


def token_places(ids, spread, fetch):
    experts_of = lax.broadcasted_iota(jnp.int32, (8, 16), 0)
    hits = [ids[k : k + 1] == experts_of for k in range(2)]
    either = jnp.where(hits[0] | hits[1], 1.0, 0.0).astype(BF16)
    before = lax.broadcasted_iota(jnp.int32, (16, 16), 0) < lax.broadcasted_iota(
        jnp.int32, (16, 16), 1
    )
    earlier = dot(either, jnp.where(before, 1.0, 0.0).astype(BF16))
    rows = lax.broadcasted_iota(jnp.int32, (128, 16), 0).astype(F32)
    for half in range(2):
        found = []
        for k in range(2):
            slot = jnp.sum(jnp.where(hits[k], earlier, 0.0), axis=0, keepdims=True)
            place = ids[k : k + 1].astype(F32) * 16.0 + slot + half * 8.0
            found.append(jnp.where(rows == place, 1.0, 0.0))
            fetch[half, k] = found[k].astype(BF16)
        spread[half] = (found[0] + found[1]).astype(BF16)


def block_kernel(*refs):
    names = INPUTS + ("out",) + tuple(SCRATCH)
    r = dict(zip(names, refs, strict=True))
    ctx, exp = lax.axis_index("ctx"), lax.axis_index("exp")
    mx, my = ctx // 4, ctx % 4
    halves = (Half(0, mx, my), Half(1, mx, my))
    wgu, wd, w_sem = r["wgu"], r["wd"], r["w_sem"]
    loads = [
        pltpu.make_async_copy(r["w_gate"].at[0], wgu.at[:, pl.ds(0, 768)], w_sem.at[0]),
        pltpu.make_async_copy(r["w_up"].at[0], wgu.at[:, pl.ds(768, 768)], w_sem.at[1]),
        pltpu.make_async_copy(r["w_down"].at[0], wd, w_sem.at[2]),
    ]
    for load in loads:
        load.start()
    greet(
        [{"ctx": lax.rem(ctx + 15, 16)}, {"ctx": lax.rem(ctx + 1, 16)}]
        + [h.one(d) for h in halves for d in (1, 2, -1)]
        + [{"exp": lax.rem(exp + d, 8)} for d in range(1, 8)]
    )
    token_places(r["expert_ids"][...], r["spread"], r["fetch"])
    first, sent = mixer(r, ctx, exp, mx, my)
    experts(r, first, sent, r["out"], exp, mx, my, halves, loads)


def shards(
    mixer_in,
    gate_in,
    conv_weight,
    conv_bias,
    x_proj,
    dt_proj,
    dt_bias,
    decay_rate,
    skip,
    out_proj,
    residual,
    gain,
    router,
    w_gate,
    w_up,
    w_down,
    expert_ids,
):
    pick = np.zeros((2, 40, 128), np.float32)
    for j in range(8):
        for s in range(5):
            pick[0, j * 5 + s, j * 16 + s] = 1.0
            pick[1, j * 5 + s, j * 16 + 8 + s] = 1.0
    vmem = pl.BlockSpec(memory_space=pltpu.VMEM)
    anywhere = pl.BlockSpec(memory_space=pl.ANY)
    return pl.pallas_call(
        block_kernel,
        out_shape=jax.ShapeDtypeStruct((16, 4096), BF16),
        in_specs=[anywhere if name.startswith("w_") else vmem for name in INPUTS],
        out_specs=vmem,
        scratch_shapes=list(SCRATCH.values()),
        compiler_params=pltpu.CompilerParams(
            collective_id=0, has_side_effects=True, vmem_limit_bytes=VMEM_LIMIT
        ),
        cost_estimate=pl.CostEstimate(
            flops=13_500_000_000, bytes_accessed=24_000_000, transcendentals=0
        ),
    )(
        mixer_in,
        gate_in,
        conv_weight,
        conv_bias[None],
        x_proj.T,
        dt_proj,
        dt_bias[None],
        decay_rate,
        skip[None],
        out_proj,
        residual,
        gain[None],
        router.T,
        expert_ids.T,
        w_gate,
        w_up,
        w_down,
        jnp.asarray(pick[0], BF16),
        jnp.asarray(pick[1], BF16),
    )


def solution(mesh):
    in_specs = (
        P("ctx", "exp"),
        P("ctx", "exp"),
        P(None, "exp"),
        P("exp"),
        P("exp", None),
        P(None, "exp"),
        P("exp"),
        P(None, "exp"),
        P("exp"),
        P("exp", "ctx"),
        P(("ctx", "exp"), None),
        P(),
        P(),
        P("exp", None, "ctx"),
        P("exp", None, "ctx"),
        P("exp", "ctx", None),
        P(("ctx", "exp"), None),
    )
    out_specs = P(("ctx", "exp"), None)
    return jax.shard_map(shards, mesh=mesh, in_specs=in_specs, out_specs=out_specs, check_vma=False)
```

```python
import jax
import jax.numpy as jnp
import numpy as np
from jax import lax
from jax.experimental import pallas as pl
from jax.experimental.pallas import tpu as pltpu
from jax.sharding import PartitionSpec as P

F32 = jnp.float32
BF16 = jnp.bfloat16
VMEM_LIMIT = 60 * 1024 * 1024


def remote(src, dst, send_sem, recv_sem, device):
    return pltpu.make_async_remote_copy(
        src_ref=src,
        dst_ref=dst,
        send_sem=send_sem,
        recv_sem=recv_sem,
        device_id=device,
        device_id_type=pl.DeviceIdType.MESH,
    )


def greet(devices):
    barrier = pltpu.get_barrier_semaphore()
    for device in devices:
        pl.semaphore_signal(barrier, inc=1, device_id=device, device_id_type=pl.DeviceIdType.MESH)
    pl.semaphore_wait(barrier, len(devices))


def wrap(index, count):
    return lax.rem(index + count, count)


def dot(a, b):
    return jnp.dot(a, b, preferred_element_type=F32)


def dot_t(a, b):
    return lax.dot_general(a, b, (((1,), (1,)), ((), ())), preferred_element_type=F32)


class Half:
    def __init__(self, half, mx, my):
        self.half = half
        self.mx, self.my = mx, my
        self.p, self.q = (mx, my) if half == 0 else (my, mx)

    def one(self, step):
        p = wrap(self.p + step, 4)
        return {"ctx": p * 4 + self.my if self.half == 0 else self.mx * 4 + p}

    def two(self, step):
        q = wrap(self.q + step, 4)
        return {"ctx": self.mx * 4 + q if self.half == 0 else q * 4 + self.my}

    def unit(self, u, v):
        return (u, v) if self.half == 0 else (v, u)

    def group(self, v):
        return (slice(None), v) if self.half == 0 else (v, slice(None))


LOG2E = 1.4426950408889634

INPUTS = (
    "mixer_in",
    "gate_in",
    "conv_weight",
    "conv_bias",
    "x_proj",
    "dt_proj",
    "dt_bias",
    "decay_rate",
    "skip",
    "out_proj",
    "residual",
    "gain",
    "router",
    "expert_ids",
    "w_gate",
    "w_up",
    "w_down",
    "pick",
)

SCRATCH = {
    "stream": pltpu.VMEM((16, 4096), F32),
    "normed": pltpu.VMEM((16, 4096), BF16),
    "spread": pltpu.VMEM((3, 128, 16), BF16),
    "fetch": pltpu.VMEM((3, 2, 128, 16), BF16),
    "rim": pltpu.VMEM((16, 1024), BF16),
    "padded": pltpu.VMEM((136, 1024), F32),
    "conv_out": pltpu.VMEM((128, 1024), BF16),
    "part": pltpu.VMEM((8, 16, 544), BF16),
    "parts": pltpu.VMEM((8, 16, 544), BF16),
    "low_rank": pltpu.VMEM((8, 16, 512), BF16),
    "maps": pltpu.VMEM((8, 16, 128), F32),
    "bc_s": pltpu.SMEM((8, 16, 128), F32),
    "step_t": pltpu.VMEM((1024, 128), F32),
    "drive_t": pltpu.VMEM((1024, 128), F32),
    "cum_t": pltpu.VMEM((1024, 128), F32),
    "y_t": pltpu.VMEM((1024, 128), F32),
    "rate_t": pltpu.VMEM((128, 128), F32),
    "enter_t": pltpu.VMEM((128, 128), F32),
    "fin_own": pltpu.VMEM((2, 128, 128), BF16),
    "fin_y": pltpu.VMEM((4, 128, 128), BF16),
    "sum_y": pltpu.VMEM((4, 8, 128), F32),
    "fin_x": pltpu.VMEM((4, 128, 128), BF16),
    "sum_x": pltpu.VMEM((4, 8, 128), F32),
    "opg": pltpu.VMEM((4, 1024, 256), BF16),
    "ga": pltpu.VMEM((4, 128, 1024), BF16),
    "zs": pltpu.VMEM((4, 8, 16, 1024), BF16),
    "rz": pltpu.VMEM((4, 8, 16, 1024), BF16),
    "ms": pltpu.VMEM((3, 16, 1024), BF16),
    "mo": pltpu.VMEM((4, 16, 1024), BF16),
    "h_sem": pltpu.SemaphoreType.DMA((2,)),
    "a_send": pltpu.SemaphoreType.DMA((8,)),
    "a_recv": pltpu.SemaphoreType.DMA((8,)),
    "b_send": pltpu.SemaphoreType.DMA((16,)),
    "b_recv": pltpu.SemaphoreType.DMA((16,)),
    "o_send": pltpu.SemaphoreType.DMA((4,)),
    "o_recv": pltpu.SemaphoreType.DMA((4,)),
    "c_send": pltpu.SemaphoreType.DMA((12,)),
    "c_recv": pltpu.SemaphoreType.DMA((12,)),
    "g_send": pltpu.SemaphoreType.DMA((6,)),
    "g_recv": pltpu.SemaphoreType.DMA((6,)),
    "z_send": pltpu.SemaphoreType.DMA((4, 8)),
    "z_recv": pltpu.SemaphoreType.DMA((4, 8)),
    "m_send": pltpu.SemaphoreType.DMA((4,)),
    "m_recv": pltpu.SemaphoreType.DMA((4,)),
    "l_sem": pltpu.SemaphoreType.DMA((1,)),
    "go": pltpu.VMEM((2, 8, 16, 768), BF16),
    "rcv": pltpu.VMEM((2, 8, 16, 768), BF16),
    "rback": pltpu.VMEM((2, 8, 16, 768), BF16),
    "xa": pltpu.VMEM((4, 4, 40, 2048), BF16),
    "xb": pltpu.VMEM((4, 4, 40, 2048), BF16),
    "wgu": pltpu.VMEM((4096, 1536), BF16),
    "wd": pltpu.VMEM((768, 4096), BF16),
    "lhs": pltpu.VMEM((160, 2048), BF16),
    "acc": pltpu.VMEM((4, 4, 40, 1536), F32),
    "hid": pltpu.VMEM((4, 4, 40, 768), BF16),
    "oa": pltpu.VMEM((4, 4, 40, 2048), BF16),
    "ob": pltpu.VMEM((4, 4, 40, 2048), BF16),
    "far": pltpu.VMEM((2, 2, 4, 40, 1024), BF16),
    "near": pltpu.VMEM((2, 2, 4, 40, 2048), BF16),
    "tot": pltpu.VMEM((2, 4, 40, 2048), BF16),
    "far2": pltpu.VMEM((2, 2, 40, 1024), BF16),
    "near2": pltpu.VMEM((2, 2, 40, 2048), BF16),
    "w_sem": pltpu.SemaphoreType.DMA((3,)),
    "d_send": pltpu.SemaphoreType.DMA((2, 8)),
    "d_recv": pltpu.SemaphoreType.DMA((2, 8)),
    "u_send": pltpu.SemaphoreType.DMA((2, 5, 4)),
    "u_recv": pltpu.SemaphoreType.DMA((2, 5, 4)),
    "s_send": pltpu.SemaphoreType.DMA((2, 24)),
    "s_recv": pltpu.SemaphoreType.DMA((2, 24)),
    "r_send": pltpu.SemaphoreType.DMA((2, 8)),
    "r_recv": pltpu.SemaphoreType.DMA((2, 8)),
}


def mixer(r, ctx, exp, mx, my):
    mixer_in = r["mixer_in"]
    gate_in = r["gate_in"]
    conv_weight = r["conv_weight"]
    conv_bias = r["conv_bias"]
    x_proj = r["x_proj"]
    dt_proj = r["dt_proj"]
    dt_bias = r["dt_bias"]
    decay_rate = r["decay_rate"]
    skip = r["skip"]
    out_proj = r["out_proj"]
    residual = r["residual"]
    gain = r["gain"]
    router = r["router"]
    expert_ids = r["expert_ids"]
    stream = r["stream"]
    normed = r["normed"]
    rim = r["rim"]
    padded = r["padded"]
    conv_out = r["conv_out"]
    part = r["part"]
    parts = r["parts"]
    low_rank = r["low_rank"]
    maps = r["maps"]
    bc_s = r["bc_s"]
    step_t = r["step_t"]
    drive_t = r["drive_t"]
    cum_t = r["cum_t"]
    y_t = r["y_t"]
    rate_t = r["rate_t"]
    enter_t = r["enter_t"]
    fin_own = r["fin_own"]
    fin_y = r["fin_y"]
    sum_y = r["sum_y"]
    fin_x = r["fin_x"]
    sum_x = r["sum_x"]
    opg = r["opg"]
    ga = r["ga"]
    zs = r["zs"]
    rz = r["rz"]
    ms = r["ms"]
    mo = r["mo"]
    h_sem = r["h_sem"]
    a_send = r["a_send"]
    a_recv = r["a_recv"]
    b_send = r["b_send"]
    b_recv = r["b_recv"]
    o_send = r["o_send"]
    o_recv = r["o_recv"]
    c_send = r["c_send"]
    c_recv = r["c_recv"]
    g_send = r["g_send"]
    g_recv = r["g_recv"]
    z_send = r["z_send"]
    z_recv = r["z_recv"]
    m_send = r["m_send"]
    m_recv = r["m_recv"]
    l_sem = r["l_sem"]
    every = slice(None)

    def along_x(d):
        return {"ctx": wrap(mx + d, 4) * 4 + my}

    def along_y(d):
        return {"ctx": mx * 4 + wrap(my + d, 4)}

    def peer(d):
        return {"exp": lax.rem(exp + d, 8)}

    ahead = {"ctx": lax.rem(ctx + 1, 16)}
    sent = []

    def send(src, dst, ss, rs, device):
        c = remote(src, dst, ss, rs, device)
        c.start()
        sent.append(c)
        return c

    halo = send(mixer_in.at[pl.ds(112, 16)], rim, h_sem.at[0], h_sem.at[1], ahead)
    columns = [
        send(out_proj, opg.at[my], o_send.at[0], o_recv.at[0], along_y(1)),
        send(out_proj, opg.at[my], o_send.at[1], o_recv.at[1], along_y(-1)),
    ]
    opg[pl.ds(my, 1)] = out_proj[...][None]
    padded[pl.ds(8, 128), :] = mixer_in[...].astype(F32)
    for g in range(8):
        rate_t[pl.ds(g, 16, stride=8), :] = decay_rate[:, g * 128 : (g + 1) * 128] * (-LOG2E)

    def convolve(start, rows):
        for g in range(8):
            cols = pl.ds(g * 128, 128)
            total = conv_bias[:, cols]
            for k in range(4):
                taps = conv_weight[k : k + 1, cols]
                total = total + taps * padded[pl.ds(start + 5 + k, rows), cols]
            conv_out[pl.ds(start, rows), cols] = (total * jax.nn.sigmoid(total)).astype(BF16)

    convolve(16, 112)
    halo.wait_recv()
    keep = jnp.where(ctx > 0, 1.0, 0.0).astype(F32)
    padded[pl.ds(0, 8), :] = rim[pl.ds(0, 16), :].astype(F32)[8:] * keep
    convolve(0, 16)

    part[...] = dot_t(conv_out[...], x_proj[...]).astype(BF16).reshape(8, 16, 544)
    scatter = [
        send(part.at[lax.rem(exp + d, 8)], parts.at[exp], a_send.at[d], a_recv.at[d], peer(d))
        for d in range(1, 8)
    ]
    parts[pl.ds(exp, 1)] = part[pl.ds(exp, 1)]
    for c in scatter:
        c.wait_recv()
    total = parts[0].astype(F32)
    for j in range(1, 8):
        total = total + parts[j].astype(F32)
    low_rank[pl.ds(exp, 1)] = total[:, :512].astype(BF16)[None]
    maps[pl.ds(exp, 1), :, pl.ds(0, 32)] = total[:, 512:][None]
    gather = []
    for d in range(1, 8):
        for k, ref in enumerate((low_rank, maps)):
            s = 2 * d + k
            gather.append(send(ref.at[exp], ref.at[exp], b_send.at[s], b_recv.at[s], peer(d)))
    for c in gather:
        c.wait_recv()
    top, low = pl.ds(0, 512), pl.ds(512, 512)
    left, right = wrap(my - 1, 4), wrap(my + 1, 4)
    columns[0].wait_recv()
    columns.append(
        send(opg.at[left, top], opg.at[left, top], o_send.at[2], o_recv.at[2], along_y(1))
    )
    columns[1].wait_recv()
    columns.append(
        send(opg.at[right, low], opg.at[right, low], o_send.at[3], o_recv.at[3], along_y(-1))
    )
    scalars = pltpu.make_async_copy(maps, bc_s, l_sem.at[0])
    scalars.start()
    step_low = low_rank[...].reshape(128, 512)
    for j in range(4):
        cols = pl.ds(j * 256, 256)
        raw = dot(step_low, dt_proj[:, cols]) + dt_bias[:, cols]
        step = jnp.maximum(raw, 0.0) + jnp.log1p(jnp.exp(-jnp.abs(raw)))
        drive = step * conv_out[:, cols].astype(F32)
        for i in range(2):
            rows = pl.ds(j * 2 + i, 128, stride=8)
            step_t[rows, :] = step[:, i * 128 : (i + 1) * 128]
            drive_t[rows, :] = drive[:, i * 128 : (i + 1) * 128]
    scalars.wait()

    rates = [rate_t[pl.ds(n * 8, 8), :] for n in range(16)]
    zero = jnp.zeros((8, 128), F32)

    def scan_step(t, carry):
        states, running = carry
        rows = pl.ds(pl.multiple_of(t * 8, 8), 8)
        s, d = step_t[rows, :], drive_t[rows, :]
        outs = [zero, zero]
        after = []
        for n in range(16):
            h = jnp.exp2(rates[n] * s) * states[n] + bc_s[t // 16, t % 16, n] * d
            outs[n % 2] = outs[n % 2] + bc_s[t // 16, t % 16, 16 + n] * h
            after.append(h)
        running = running + s
        y_t[rows, :] = outs[0] + outs[1]
        cum_t[rows, :] = running
        return (tuple(after), running)

    states, running = lax.fori_loop(0, 128, scan_step, ((zero,) * 16, zero), unroll=2)

    def exchange(finals, total, fin, sums, place, base, step):
        for n in range(16):
            fin_own[base // 6, pl.ds(n * 8, 8), :] = finals[n].astype(BF16)
        sums[pl.ds(place, 1)] = total[None]
        fin[pl.ds(place, 1)] = fin_own[base // 6][None]
        moves = []
        for k, d in enumerate((1, -1, 2)):
            s, r = base + 2 * k, base + 2 * k + 1
            moves.append(
                send(fin_own.at[base // 6], fin.at[place], c_send.at[s], c_recv.at[s], step(d))
            )
            moves.append(send(sums.at[place], sums.at[place], c_send.at[r], c_recv.at[r], step(d)))
        for c in moves:
            c.wait_recv()

    exchange(states, running, fin_y, sum_y, my, 0, along_y)
    before, row_total = zero, zero
    for v in range(4):
        before = before + jnp.where(v < my, 1.0, 0.0).astype(F32) * sum_y[v]
        row_total = row_total + sum_y[v]
    row_final = []
    for n in range(16):
        entering, whole = zero, zero
        for v in range(4):
            own = fin_y[v, pl.ds(n * 8, 8), :].astype(F32)
            decay = jnp.exp2(rates[n] * sum_y[v])
            entering = jnp.where(v < my, decay * entering + own, entering)
            whole = decay * whole + own
        enter_t[pl.ds(n * 8, 8), :] = entering
        row_final.append(whole)
    exchange(row_final, row_total, fin_x, sum_x, mx, 6, along_x)
    for n in range(16):
        entering = zero
        for u in range(4):
            own = fin_x[u, pl.ds(n * 8, 8), :].astype(F32)
            decay = jnp.exp2(rates[n] * sum_x[u])
            entering = jnp.where(u < mx, decay * entering + own, entering)
        rows = pl.ds(n * 8, 8)
        enter_t[rows, :] = enter_t[rows, :] + jnp.exp2(rates[n] * before) * entering

    def add_entering(t, carry):
        rows = pl.ds(pl.multiple_of(t * 8, 8), 8)
        c = cum_t[rows, :]
        outs = [y_t[rows, :], zero]
        for n in range(16):
            outs[n % 2] = outs[n % 2] + bc_s[t // 16, t % 16, 16 + n] * (jnp.exp2(rates[n] * c) * entered[n])
        y_t[rows, :] = outs[0] + outs[1]
        return carry

    entered = [enter_t[pl.ds(n * 8, 8), :] for n in range(16)]
    moves = []
    for half in range(2):
        lax.fori_loop(half * 64, half * 64 + 64, add_entering, 0, unroll=2)
        rows = pl.ds(half * 64, 64)
        for g in range(8):
            cols = pl.ds(g * 128, 128)
            y = y_t[pl.ds(half * 512 + g, 64, stride=8), :]
            y = y + skip[:, cols] * conv_out[rows, cols].astype(F32)
            z = gate_in[rows, cols].astype(F32)
            ga[pl.ds(mx, 1), rows, cols] = (y * (z * jax.nn.sigmoid(z))).astype(BF16)[None]
        place = ga.at[mx, rows]
        for k, d in enumerate((1, -1)):
            s = half * 2 + k
            moves.append(send(place, place, g_send.at[s], g_recv.at[s], along_x(d)))

    def project(u):
        for v in range(4):
            cols = pl.ds(v * 256, 256)
            out = dot(ga[u], opg[v])
            zs[pl.ds(u, 1), :, :, cols] = out.astype(BF16).reshape(1, 8, 16, 256)
        rz[pl.ds(u, 1), pl.ds(exp, 1)] = zs[pl.ds(u, 1), pl.ds(exp, 1)]

    def scatter_group(k, u):
        return [
            send(zs.at[u, lax.rem(exp + d, 8)], rz.at[u, exp], z_send.at[k, d], z_recv.at[k, d], peer(d))
            for d in range(1, 8)
        ]

    for c in columns[2:]:
        c.wait_recv()
    left, right, far = wrap(mx - 1, 4), wrap(mx + 1, 4), wrap(mx + 2, 4)
    top, low = pl.ds(0, 64), pl.ds(64, 64)
    project(mx)
    groups = [scatter_group(0, mx)]
    moves[0].wait_recv()
    moves.append(send(ga.at[left, top], ga.at[left, top], g_send.at[4], g_recv.at[4], along_x(1)))
    moves[1].wait_recv()
    moves[3].wait_recv()
    moves.append(send(ga.at[right, low], ga.at[right, low], g_send.at[5], g_recv.at[5], along_x(-1)))
    moves[2].wait_recv()
    for k, u in ((1, left), (2, right)):
        project(u)
        groups.append(scatter_group(k, u))
    moves[4].wait_recv()
    moves[5].wait_recv()
    project(far)
    groups.append(scatter_group(3, far))
    backs = []
    for k, (u, d) in enumerate(((mx, 0), (left, -1), (right, 1), (far, 2))):
        for c in groups[k]:
            c.wait_recv()
        total = rz[u, 0].astype(F32)
        for j in range(1, 8):
            total = total + rz[u, j].astype(F32)
        if d == 0:
            mo[pl.ds(mx, 1)] = total.astype(BF16)[None]
        else:
            ms[k - 1] = total.astype(BF16)
            backs.append(send(ms.at[k - 1], mo.at[mx], m_send.at[k], m_recv.at[k], along_x(d)))
    for c in backs:
        c.wait_recv()

    squares = jnp.zeros((16, 1), F32)
    for u in range(4):
        cols = pl.ds(u * 1024, 1024)
        rows = residual[:, cols].astype(F32) + mo[u].astype(F32)
        stream[:, cols] = rows
        squares = squares + jnp.sum(rows * rows, axis=1, keepdims=True)
    scale = lax.rsqrt(squares * (1.0 / 4096.0) + 1e-06)
    logits = jnp.zeros((8, 16), F32)
    for u in range(4):
        cols = pl.ds(u * 1024, 1024)
        rows = (stream[:, cols] * scale * gain[:, cols]).astype(BF16)
        normed[:, cols] = rows
        logits = logits + dot_t(router[:, cols], rows)
    ids = expert_ids[...]
    lanes = lax.broadcasted_iota(jnp.int32, (8, 16), 0)
    signs = jnp.where(ids[0:1] == lanes, 1.0, 0.0) - jnp.where(ids[1:2] == lanes, 1.0, 0.0)
    first = jax.nn.sigmoid(jnp.sum(logits * signs, axis=0, keepdims=True))
    return first, sent


def experts(r, gate_row, sent, out, exp, mx, my, halves, loads):
    pick = r["pick"]
    stream = r["stream"]
    normed = r["normed"]
    spread = r["spread"]
    fetch = r["fetch"]
    go = r["go"]
    rcv = r["rcv"]
    rback = r["rback"]
    xa = r["xa"]
    xb = r["xb"]
    wgu = r["wgu"]
    wd = r["wd"]
    lhs = r["lhs"]
    acc = r["acc"]
    hid = r["hid"]
    oa = r["oa"]
    ob = r["ob"]
    far = r["far"]
    near = r["near"]
    tot = r["tot"]
    far2 = r["far2"]
    near2 = r["near2"]
    d_send = r["d_send"]
    d_recv = r["d_recv"]
    u_send = r["u_send"]
    u_recv = r["u_recv"]
    s_send = r["s_send"]
    s_recv = r["s_recv"]
    r_send = r["r_send"]
    r_recv = r["r_recv"]
    xs, os = (xa, xb), (oa, ob)
    lo, hi = pl.ds(0, 1024), pl.ds(1024, 1024)
    every = slice(None)

    windows = (0, 768, 1280)

    def all_to_all(half, into, ss, rs):
        moves = []
        for d in range(1, 8):
            peer = lax.rem(exp + d, 8)
            src, dst = go.at[half, peer], into.at[half, exp]
            c = remote(src, dst, ss.at[half, d], rs.at[half, d], {"exp": peer})
            c.start()
            moves.append(c)
        into[half, pl.ds(exp, 1)] = go[half, pl.ds(exp, 1)]
        sent.extend(moves)
        return moves

    dispatch = []
    for i in range(2):
        packed = jnp.zeros((128, 768), F32)
        for k, w in enumerate(windows):
            packed = packed + dot(spread[k], normed[:, pl.ds(i * 2048 + w, 768)])
        go[i] = packed.astype(BF16).reshape(8, 16, 768)
        dispatch.append(all_to_all(i, rcv, d_send, d_recv))
    acc[...] = jnp.zeros_like(acc)

    def push(h, x, at, cols, g, k, device):
        place = x.at[at + (every, cols)] if cols is not None else x.at[at]
        c = remote(place, place, u_send.at[h, g, k], u_recv.at[h, g, k], device)
        c.start()
        sent.append(c)
        return c

    first, second = [], [[None] * 4, [None] * 4]
    steps = [[wrap(h.p + d, 4) for d in (0, -1, 1, 2)] for h in halves]

    def second_start(i, g):
        h, x = halves[i], xs[i]
        at = h.unit(steps[i][g], h.q)
        second[i][g] = [
            push(i, x, at, None, g + 1, 0, h.two(1)),
            push(i, x, at, None, g + 1, 1, h.two(-1)),
        ]

    def second_pass(i, g):
        h, x, u = halves[i], xs[i], steps[i][g]
        second[i][g][0].wait_recv()
        a = push(i, x, h.unit(u, wrap(h.q - 1, 4)), lo, g + 1, 2, h.two(1))
        second[i][g][1].wait_recv()
        b = push(i, x, h.unit(u, wrap(h.q + 1, 4)), hi, g + 1, 3, h.two(-1))
        second[i][g] += [a, b]

    for i, (h, x) in enumerate(zip(halves, xs)):
        for c in dispatch[i]:
            c.wait_recv()
        flat = rcv[i].reshape(128, 768)
        for k, w in enumerate(windows):
            block = dot(pick[k], flat).astype(BF16)[None, None]
            x[pl.ds(mx, 1), pl.ds(my, 1), :, pl.ds(w, 768)] = block
        at = h.unit(h.p, h.q)
        first.append(
            [push(i, x, at, None, 0, 0, h.one(1)), push(i, x, at, None, 0, 1, h.one(-1))]
        )
        second_start(i, 0)
    for i, (h, x) in enumerate(zip(halves, xs)):
        first[i][0].wait_recv()
        first[i].append(push(i, x, h.unit(steps[i][1], h.q), lo, 0, 2, h.one(1)))
        first[i][1].wait_recv()
        first[i].append(push(i, x, h.unit(steps[i][2], h.q), hi, 0, 3, h.one(-1)))
    second_start(0, 1)
    second_start(1, 1)
    for i in range(2):
        first[i][2].wait_recv()
        first[i][3].wait_recv()
        second_start(i, 2)
        second_start(i, 3)

    def gate_up(i, v):
        at = halves[i].group(v)
        lhs[...] = xs[i][at].reshape(160, 2048)
        for j in range(6):
            cols = pl.ds(j * 256, 256)
            part = dot(lhs[...], wgu[pl.ds(i * 2048, 2048), cols])
            place = at + (every, cols)
            acc[place] = acc[place] + part.reshape(4, 40, 256)

    loads[0].wait()
    loads[1].wait()
    gate_up(0, halves[0].q)
    second_pass(0, 0)
    second_pass(1, 0)
    gate_up(1, halves[1].q)
    for g in range(1, 4):
        second_pass(0, g)
        second_pass(1, g)
    for i, h in enumerate(halves):
        gate_up(i, wrap(h.q - 1, 4))
        gate_up(i, wrap(h.q + 1, 4))
    for i, h in enumerate(halves):
        for g in range(4):
            second[i][g][2].wait_recv()
            second[i][g][3].wait_recv()
        gate_up(i, wrap(h.q + 2, 4))

    @pl.loop(0, 16)
    def _(n):
        at = (n // 4, n % 4)
        gate = acc[at + (every, pl.ds(0, 768))]
        up = acc[at + (every, pl.ds(768, 768))]
        hid[at] = (gate * jax.nn.sigmoid(gate) * up).astype(BF16)

    loads[2].wait()

    def down(i, v):
        at = halves[i].group(v)
        lhs[:, pl.ds(0, 768)] = hid[at].reshape(160, 768)
        for j in range(8):
            part = dot(lhs[:, pl.ds(0, 768)], wd[:, pl.ds(i * 2048 + j * 256, 256)])
            os[i][at + (every, pl.ds(j * 256, 256))] = part.reshape(4, 40, 256).astype(BF16)

    def send(src, dst, i, k, device):
        c = remote(src, dst, s_send.at[i, k], s_recv.at[i, k], device)
        c.start()
        sent.append(c)
        return c

    def add_into(ref, at, other, other_at):
        ref[at] = (ref[at].astype(F32) + other[other_at].astype(F32)).astype(BF16)

    order = [[wrap(h.p + d, 4) for d in (2, 1, -1, 0)] for h in halves]
    fars, nears, adds, lasts = [[], []], [[], []], [[], []], [[], []]
    for i, h in enumerate(halves):
        v = wrap(h.q + 2, 4)
        down(i, v)
        for k, u in enumerate(order[i]):
            at = h.unit(u, v)
            fars[i].append(
                [
                    send(os[i].at[at + (every, lo)], far.at[i, 0, u], i, k, h.two(1)),
                    send(os[i].at[at + (every, hi)], far.at[i, 1, u], i, 4 + k, h.two(-1)),
                ]
            )
    for i, h in enumerate(halves):
        for v, d, cols, b in ((wrap(h.q + 1, 4), 1, hi, 0), (wrap(h.q - 1, 4), -1, lo, 1)):
            down(i, v)
            src = os[i].at[h.group(v) + (every, cols)]
            nears[i].append(send(src, near.at[i, b, :, :, cols], i, 8 + b, h.two(d)))
    down(0, halves[0].q)
    for k in range(4):
        for i, h in enumerate(halves):
            u, moves = order[i][k], []
            for b, d, cols in ((0, 1, lo), (1, -1, hi)):
                fars[i][k][b].wait_recv()
                at = h.unit(u, wrap(h.q + d, 4)) + (every, cols)
                add_into(os[i], at, far, (i, b, u))
                dst = near.at[i, b, u, :, cols]
                moves.append(send(os[i].at[at], dst, i, 10 + 4 * b + k, h.two(d)))
            adds[i].append(moves)
    down(1, halves[1].q)
    for i in range(2):
        for c in nears[i]:
            c.wait_recv()
    for k in range(4):
        for i, h in enumerate(halves):
            u = order[i][k]
            for c in adds[i][k]:
                c.wait_recv()
            mine = os[i][h.unit(u, h.q)].astype(F32)
            mine = mine + near[i, 0, u].astype(F32) + near[i, 1, u].astype(F32)
            tot[i, u] = mine.astype(BF16)
            if k == 0:
                lasts[i].append(send(tot.at[i, u, :, lo], far2.at[i, 0], i, 18, h.one(1)))
                lasts[i].append(send(tot.at[i, u, :, hi], far2.at[i, 1], i, 19, h.one(-1)))
            if k == 1:
                lasts[i].append(send(tot.at[i, u, :, hi], near2.at[i, 0, :, hi], i, 20, h.one(1)))
            if k == 2:
                lasts[i].append(send(tot.at[i, u, :, lo], near2.at[i, 1, :, lo], i, 21, h.one(-1)))
    for i, h in enumerate(halves):
        for b, d, cols in ((0, 1, lo), (1, -1, hi)):
            u = order[i][1 + b]
            lasts[i][b].wait_recv()
            add_into(tot, (i, u, every, cols), far2, (i, b))
            dst = near2.at[i, b, :, cols]
            lasts[i].append(send(tot.at[i, u, :, cols], dst, i, 22 + b, h.one(d)))

    across = (((0,), (0,)), ((), ()))
    returns = []
    for i, h in enumerate(halves):
        for c in lasts[i][2:]:
            c.wait_recv()
        final = tot[i, h.p].astype(F32) + near2[i, 0].astype(F32) + near2[i, 1].astype(F32)
        final = final.astype(BF16)
        back = jnp.zeros((128, 768), F32)
        for k, w in enumerate(windows):
            block = final[:, w : w + 768]
            back = back + lax.dot_general(pick[k], block, across, preferred_element_type=F32)
        for c in dispatch[i]:
            c.wait_send()
        go[i] = back.astype(BF16).reshape(8, 16, 768)
        returns.append(all_to_all(i, rback, r_send, r_recv))
    eye = lax.broadcasted_iota(jnp.int32, (16, 16), 0) == lax.broadcasted_iota(
        jnp.int32, (16, 16), 1
    )
    gate = jnp.sum(jnp.where(eye, jnp.broadcast_to(gate_row, (16, 16)), 0.0), axis=1, keepdims=True)
    for i in range(2):
        for c in returns[i]:
            c.wait_recv()
        flat = rback[i].reshape(128, 768)
        for j, w in enumerate(windows):
            cols = pl.ds(i * 2048 + w, 768)
            pair = [
                lax.dot_general(fetch[j, k], flat, across, preferred_element_type=F32)
                for k in range(2)
            ]
            mix = gate * pair[0] + (1.0 - gate) * pair[1]
            out[:, cols] = (stream[:, cols] + mix).astype(BF16)
    early = dispatch[0] + dispatch[1]
    for c in sent:
        if not any(c is other for other in early):
            c.wait_send()


def token_places(ids, spread, fetch):
    experts_of = lax.broadcasted_iota(jnp.int32, (8, 16), 0)
    hits = [ids[k : k + 1] == experts_of for k in range(2)]
    either = jnp.where(hits[0] | hits[1], 1.0, 0.0).astype(BF16)
    before = lax.broadcasted_iota(jnp.int32, (16, 16), 0) < lax.broadcasted_iota(
        jnp.int32, (16, 16), 1
    )
    earlier = dot(either, jnp.where(before, 1.0, 0.0).astype(BF16))
    rows = lax.broadcasted_iota(jnp.int32, (128, 16), 0).astype(F32)
    for j in range(3):
        found = []
        for k in range(2):
            slot = jnp.sum(jnp.where(hits[k], earlier, 0.0), axis=0, keepdims=True)
            place = ids[k : k + 1].astype(F32) * 16.0 + slot + j * 5.0
            found.append(jnp.where(rows == place, 1.0, 0.0))
            fetch[j, k] = found[k].astype(BF16)
        spread[j] = (found[0] + found[1]).astype(BF16)


def block_kernel(*refs):
    names = INPUTS + ("out",) + tuple(SCRATCH)
    r = dict(zip(names, refs, strict=True))
    ctx, exp = lax.axis_index("ctx"), lax.axis_index("exp")
    mx, my = ctx // 4, ctx % 4
    halves = (Half(0, mx, my), Half(1, mx, my))
    wgu, wd, w_sem = r["wgu"], r["wd"], r["w_sem"]
    loads = [
        pltpu.make_async_copy(r["w_gate"].at[0], wgu.at[:, pl.ds(0, 768)], w_sem.at[0]),
        pltpu.make_async_copy(r["w_up"].at[0], wgu.at[:, pl.ds(768, 768)], w_sem.at[1]),
        pltpu.make_async_copy(r["w_down"].at[0], wd, w_sem.at[2]),
    ]
    for load in loads:
        load.start()
    greet(
        [{"ctx": lax.rem(ctx + 15, 16)}, {"ctx": lax.rem(ctx + 1, 16)}]
        + [h.one(d) for h in halves for d in (1, 2, -1)]
        + [{"exp": lax.rem(exp + d, 8)} for d in range(1, 8)]
    )
    token_places(r["expert_ids"][...], r["spread"], r["fetch"])
    first, sent = mixer(r, ctx, exp, mx, my)
    experts(r, first, sent, r["out"], exp, mx, my, halves, loads)


def shards(
    mixer_in,
    gate_in,
    conv_weight,
    conv_bias,
    x_proj,
    dt_proj,
    dt_bias,
    decay_rate,
    skip,
    out_proj,
    residual,
    gain,
    router,
    w_gate,
    w_up,
    w_down,
    expert_ids,
):
    pick = np.zeros((3, 40, 128), np.float32)
    for w in range(3):
        for j in range(8):
            for s in range(5):
                pick[w, j * 5 + s, j * 16 + w * 5 + s] = 1.0
    vmem = pl.BlockSpec(memory_space=pltpu.VMEM)
    anywhere = pl.BlockSpec(memory_space=pl.ANY)
    return pl.pallas_call(
        block_kernel,
        out_shape=jax.ShapeDtypeStruct((16, 4096), BF16),
        in_specs=[anywhere if name.startswith("w_") else vmem for name in INPUTS],
        out_specs=vmem,
        scratch_shapes=list(SCRATCH.values()),
        compiler_params=pltpu.CompilerParams(
            collective_id=0, has_side_effects=True, vmem_limit_bytes=VMEM_LIMIT
        ),
        cost_estimate=pl.CostEstimate(
            flops=13_500_000_000, bytes_accessed=24_000_000, transcendentals=0
        ),
    )(
        mixer_in,
        gate_in,
        conv_weight,
        conv_bias[None],
        x_proj.T,
        dt_proj,
        dt_bias[None],
        decay_rate,
        skip[None],
        out_proj,
        residual,
        gain[None],
        router.T,
        expert_ids.T,
        w_gate,
        w_up,
        w_down,
        jnp.asarray(pick, BF16),
    )


def solution(mesh):
    in_specs = (
        P("ctx", "exp"),
        P("ctx", "exp"),
        P(None, "exp"),
        P("exp"),
        P("exp", None),
        P(None, "exp"),
        P("exp"),
        P(None, "exp"),
        P("exp"),
        P("exp", "ctx"),
        P(("ctx", "exp"), None),
        P(),
        P(),
        P("exp", None, "ctx"),
        P("exp", None, "ctx"),
        P("exp", "ctx", None),
        P(("ctx", "exp"), None),
    )
    out_specs = P(("ctx", "exp"), None)
    return jax.shard_map(shards, mesh=mesh, in_specs=in_specs, out_specs=out_specs, check_vma=False)
```

```python
import jax
import jax.numpy as jnp
import numpy as np
from jax import lax
from jax.experimental import pallas as pl
from jax.experimental.pallas import tpu as pltpu
from jax.sharding import PartitionSpec as P

F32 = jnp.float32
BF16 = jnp.bfloat16
VMEM_LIMIT = 60 * 1024 * 1024


def remote(src, dst, send_sem, recv_sem, device):
    return pltpu.make_async_remote_copy(
        src_ref=src,
        dst_ref=dst,
        send_sem=send_sem,
        recv_sem=recv_sem,
        device_id=device,
        device_id_type=pl.DeviceIdType.MESH,
    )


def greet(devices):
    barrier = pltpu.get_barrier_semaphore()
    for device in devices:
        pl.semaphore_signal(barrier, inc=1, device_id=device, device_id_type=pl.DeviceIdType.MESH)
    return lambda: pl.semaphore_wait(barrier, len(devices))


def settle(view, sem):
    pltpu.make_async_copy(view, view, sem).wait()


def wrap(index, count):
    return lax.rem(index + count, count)


def dot(a, b):
    return jnp.dot(a, b, preferred_element_type=F32)


def dot_t(a, b):
    return lax.dot_general(a, b, (((1,), (1,)), ((), ())), preferred_element_type=F32)


class Half:
    def __init__(self, half, mx, my):
        self.half = half
        self.mx, self.my = mx, my
        self.p, self.q = (mx, my) if half == 0 else (my, mx)

    def one(self, step):
        p = wrap(self.p + step, 4)
        return {"ctx": p * 4 + self.my if self.half == 0 else self.mx * 4 + p}

    def two(self, step):
        q = wrap(self.q + step, 4)
        return {"ctx": self.mx * 4 + q if self.half == 0 else q * 4 + self.my}

    def unit(self, u, v):
        return (u, v) if self.half == 0 else (v, u)

    def group(self, v):
        return (slice(None), v) if self.half == 0 else (v, slice(None))


LOG2E = 1.4426950408889634

INPUTS = (
    "mixer_in",
    "gate_in",
    "conv_weight",
    "conv_bias",
    "x_proj",
    "dt_proj",
    "dt_bias",
    "decay_rate",
    "skip",
    "out_proj",
    "residual",
    "gain",
    "router",
    "expert_ids",
    "w_gate",
    "w_up",
    "w_down",
    "pick",
)

SCRATCH = {
    "stream": pltpu.VMEM((16, 4096), F32),
    "result": pltpu.VMEM((16, 4096), BF16),
    "e_sem": pltpu.SemaphoreType.DMA((2,)),
    "normed": pltpu.VMEM((16, 4096), BF16),
    "spread": pltpu.VMEM((3, 128, 16), BF16),
    "fetch": pltpu.VMEM((3, 2, 128, 16), BF16),
    "rim": pltpu.VMEM((16, 1024), BF16),
    "padded": pltpu.VMEM((136, 1024), F32),
    "conv_out": pltpu.VMEM((128, 1024), BF16),
    "part": pltpu.VMEM((8, 16, 544), BF16),
    "parts": pltpu.VMEM((8, 16, 544), BF16),
    "low_rank": pltpu.VMEM((8, 16, 512), BF16),
    "maps": pltpu.VMEM((8, 16, 128), F32),
    "bc_s": pltpu.SMEM((8, 16, 128), F32),
    "step_t": pltpu.VMEM((1024, 128), F32),
    "drive_t": pltpu.VMEM((1024, 128), F32),
    "cum_t": pltpu.VMEM((1024, 128), F32),
    "y_t": pltpu.VMEM((1024, 128), F32),
    "rate_t": pltpu.VMEM((128, 128), F32),
    "enter_t": pltpu.VMEM((128, 128), F32),
    "fin_own": pltpu.VMEM((2, 128, 128), BF16),
    "fin_y": pltpu.VMEM((4, 128, 128), BF16),
    "sum_y": pltpu.VMEM((4, 8, 128), F32),
    "fin_x": pltpu.VMEM((4, 128, 128), BF16),
    "sum_x": pltpu.VMEM((4, 8, 128), F32),
    "opg": pltpu.VMEM((4, 1024, 256), BF16),
    "ga": pltpu.VMEM((4, 128, 1024), BF16),
    "zs": pltpu.VMEM((4, 8, 16, 1024), BF16),
    "rz": pltpu.VMEM((4, 8, 16, 1024), BF16),
    "ms": pltpu.VMEM((3, 16, 1024), BF16),
    "mo": pltpu.VMEM((4, 16, 1024), BF16),
    "h_sem": pltpu.SemaphoreType.DMA((2,)),
    "a_sem": pltpu.SemaphoreType.DMA((2,)),
    "b_sem": pltpu.SemaphoreType.DMA((4,)),
    "o_send": pltpu.SemaphoreType.DMA((1,)),
    "o_recv": pltpu.SemaphoreType.DMA((3,)),
    "c_send": pltpu.SemaphoreType.DMA((2, 2)),
    "c_recv": pltpu.SemaphoreType.DMA((2, 2)),
    "g_send": pltpu.SemaphoreType.DMA((1,)),
    "g_recv": pltpu.SemaphoreType.DMA((5,)),
    "z_send": pltpu.SemaphoreType.DMA((1,)),
    "z_recv": pltpu.SemaphoreType.DMA((4,)),
    "m_sem": pltpu.SemaphoreType.DMA((2,)),
    "l_sem": pltpu.SemaphoreType.DMA((1,)),
    "go": pltpu.VMEM((2, 8, 16, 768), BF16),
    "rcv": pltpu.VMEM((2, 8, 16, 768), BF16),
    "rback": pltpu.VMEM((2, 8, 16, 768), BF16),
    "xa": pltpu.VMEM((4, 4, 40, 2048), BF16),
    "xb": pltpu.VMEM((4, 4, 40, 2048), BF16),
    "wgu": pltpu.VMEM((4096, 1536), BF16),
    "wd": pltpu.VMEM((768, 4096), BF16),
    "lhs": pltpu.VMEM((4, 40, 2048), BF16),
    "lhs_down": pltpu.VMEM((6, 40, 768), BF16),
    "acc": pltpu.VMEM((4, 4, 40, 1536), F32),
    "hid": pltpu.VMEM((4, 4, 40, 768), BF16),
    "oa": pltpu.VMEM((4, 4, 40, 2048), BF16),
    "ob": pltpu.VMEM((4, 4, 40, 2048), BF16),
    "far": pltpu.VMEM((2, 2, 4, 40, 1024), BF16),
    "near": pltpu.VMEM((2, 2, 4, 40, 2048), BF16),
    "tot": pltpu.VMEM((2, 4, 40, 2048), BF16),
    "far2": pltpu.VMEM((2, 2, 40, 1024), BF16),
    "near2": pltpu.VMEM((2, 2, 40, 2048), BF16),
    "w_sem": pltpu.SemaphoreType.DMA((3,)),
    "d_send": pltpu.SemaphoreType.DMA((2,)),
    "d_recv": pltpu.SemaphoreType.DMA((2,)),
    "u_send": pltpu.SemaphoreType.DMA((2, 3)),
    "u_recv": pltpu.SemaphoreType.DMA((2, 8)),
    "s_send": pltpu.SemaphoreType.DMA((2, 2)),
    "s_recv": pltpu.SemaphoreType.DMA((2, 11)),
    "r_send": pltpu.SemaphoreType.DMA((2,)),
    "r_recv": pltpu.SemaphoreType.DMA((2,)),
}


def mixer(r, ctx, exp, mx, my, arrive):
    mixer_in = r["mixer_in"]
    gate_in = r["gate_in"]
    conv_weight = r["conv_weight"]
    conv_bias = r["conv_bias"]
    x_proj = r["x_proj"]
    dt_proj = r["dt_proj"]
    dt_bias = r["dt_bias"]
    decay_rate = r["decay_rate"]
    skip = r["skip"]
    out_proj = r["out_proj"]
    residual = r["residual"]
    gain = r["gain"]
    router = r["router"]
    expert_ids = r["expert_ids"]
    stream = r["stream"]
    normed = r["normed"]
    rim = r["rim"]
    padded = r["padded"]
    conv_out = r["conv_out"]
    part = r["part"]
    parts = r["parts"]
    low_rank = r["low_rank"]
    maps = r["maps"]
    bc_s = r["bc_s"]
    step_t = r["step_t"]
    drive_t = r["drive_t"]
    cum_t = r["cum_t"]
    y_t = r["y_t"]
    rate_t = r["rate_t"]
    enter_t = r["enter_t"]
    fin_own = r["fin_own"]
    fin_y = r["fin_y"]
    sum_y = r["sum_y"]
    fin_x = r["fin_x"]
    sum_x = r["sum_x"]
    opg = r["opg"]
    ga = r["ga"]
    zs = r["zs"]
    rz = r["rz"]
    ms = r["ms"]
    mo = r["mo"]
    h_sem = r["h_sem"]
    a_sem = r["a_sem"]
    b_sem = r["b_sem"]
    o_send = r["o_send"]
    o_recv = r["o_recv"]
    c_send = r["c_send"]
    c_recv = r["c_recv"]
    g_send = r["g_send"]
    g_recv = r["g_recv"]
    z_send = r["z_send"]
    z_recv = r["z_recv"]
    m_sem = r["m_sem"]
    l_sem = r["l_sem"]
    every = slice(None)

    def along_x(d):
        return {"ctx": wrap(mx + d, 4) * 4 + my}

    def along_y(d):
        return {"ctx": mx * 4 + wrap(my + d, 4)}

    def peer(d):
        return {"exp": lax.rem(exp + d, 8)}

    ahead = {"ctx": lax.rem(ctx + 1, 16)}

    def send(src, dst, ss, rs, device):
        remote(src, dst, ss, rs, device).start()

    padded[pl.ds(8, 128), :] = mixer_in[...].astype(F32)
    for g in range(8):
        rate_t[pl.ds(g, 16, stride=8), :] = decay_rate[:, g * 128 : (g + 1) * 128] * (-LOG2E)

    def convolve(start, rows):
        for g in range(8):
            cols = pl.ds(g * 128, 128)
            total = conv_bias[:, cols]
            for k in range(4):
                taps = conv_weight[k : k + 1, cols]
                total = total + taps * padded[pl.ds(start + 5 + k, rows), cols]
            conv_out[pl.ds(start, rows), cols] = (total * jax.nn.sigmoid(total)).astype(BF16)

    def channel_sums(start, rows):
        sums = dot_t(conv_out[pl.ds(start, rows), :], x_proj[...]).astype(BF16)
        part[pl.ds(start // 16, rows // 16)] = sums.reshape(rows // 16, 16, 544)

    convolve(16, 112)

    arrive()
    send(mixer_in.at[pl.ds(112, 16)], rim, h_sem.at[0], h_sem.at[1], ahead)
    send(out_proj, opg.at[my], o_send.at[0], o_recv.at[0], along_y(1))
    send(out_proj, opg.at[my], o_send.at[0], o_recv.at[1], along_y(-1))
    opg[pl.ds(my, 1)] = out_proj[...][None]
    channel_sums(16, 112)
    settle(rim, h_sem.at[1])
    keep = jnp.where(ctx > 0, 1.0, 0.0).astype(F32)
    padded[pl.ds(0, 8), :] = rim[pl.ds(0, 16), :].astype(F32)[8:] * keep
    convolve(0, 16)
    channel_sums(0, 16)

    for d in range(1, 8):
        src = part.at[lax.rem(exp + d, 8)]
        send(src, parts.at[exp], a_sem.at[0], a_sem.at[1], peer(d))
    parts[pl.ds(exp, 1)] = part[pl.ds(exp, 1)]
    settle(parts.at[pl.ds(0, 7)], a_sem.at[1])
    total = parts[0].astype(F32)
    for j in range(1, 8):
        total = total + parts[j].astype(F32)
    low_rank[pl.ds(exp, 1)] = total[:, :512].astype(BF16)[None]
    maps[pl.ds(exp, 1), :, pl.ds(0, 32)] = total[:, 512:][None]
    for d in range(1, 8):
        for k, ref in enumerate((low_rank, maps)):
            send(ref.at[exp], ref.at[exp], b_sem.at[k], b_sem.at[2 + k], peer(d))
    settle(low_rank.at[pl.ds(0, 7)], b_sem.at[2])
    settle(maps.at[pl.ds(0, 7)], b_sem.at[3])
    top, low = pl.ds(0, 512), pl.ds(512, 512)
    left, right = wrap(my - 1, 4), wrap(my + 1, 4)
    settle(opg.at[0], o_recv.at[0])
    send(opg.at[left, top], opg.at[left, top], o_send.at[0], o_recv.at[2], along_y(1))
    settle(opg.at[0], o_recv.at[1])
    send(opg.at[right, low], opg.at[right, low], o_send.at[0], o_recv.at[2], along_y(-1))
    scalars = pltpu.make_async_copy(maps, bc_s, l_sem.at[0])
    scalars.start()
    step_low = low_rank[...].reshape(128, 512)
    for j in range(4):
        cols = pl.ds(j * 256, 256)
        raw = dot(step_low, dt_proj[:, cols]) + dt_bias[:, cols]
        step = jnp.maximum(raw, 0.0) + jnp.log1p(jnp.exp(-jnp.abs(raw)))
        drive = step * conv_out[:, cols].astype(F32)
        for i in range(2):
            rows = pl.ds(j * 2 + i, 128, stride=8)
            step_t[rows, :] = step[:, i * 128 : (i + 1) * 128]
            drive_t[rows, :] = drive[:, i * 128 : (i + 1) * 128]
    scalars.wait()

    rates = [rate_t[pl.ds(n * 8, 8), :] for n in range(16)]
    zero = jnp.zeros((8, 128), F32)

    def scan_step(t, carry):
        states, running = carry
        rows = pl.ds(pl.multiple_of(t * 8, 8), 8)
        s, d = step_t[rows, :], drive_t[rows, :]
        outs = [zero, zero]
        after = []
        for n in range(16):
            h = jnp.exp2(rates[n] * s) * states[n] + bc_s[t // 16, t % 16, n] * d
            outs[n % 2] = outs[n % 2] + bc_s[t // 16, t % 16, 16 + n] * h
            after.append(h)
        running = running + s
        y_t[rows, :] = outs[0] + outs[1]
        cum_t[rows, :] = running
        return (tuple(after), running)

    states, running = lax.fori_loop(0, 128, scan_step, ((zero,) * 16, zero), unroll=2)

    def exchange(finals, total, fin, sums, place, base, step):
        for n in range(16):
            fin_own[base, pl.ds(n * 8, 8), :] = finals[n].astype(BF16)
        sums[pl.ds(place, 1)] = total[None]
        fin[pl.ds(place, 1)] = fin_own[base][None]
        for d in (1, -1, 2):
            send(fin_own.at[base], fin.at[place], c_send.at[0, base], c_recv.at[0, base], step(d))
            send(sums.at[place], sums.at[place], c_send.at[1, base], c_recv.at[1, base], step(d))
        settle(fin.at[pl.ds(0, 3)], c_recv.at[0, base])
        settle(sums.at[pl.ds(0, 3)], c_recv.at[1, base])

    exchange(states, running, fin_y, sum_y, my, 0, along_y)
    before, row_total = zero, zero
    for v in range(4):
        before = before + jnp.where(v < my, 1.0, 0.0).astype(F32) * sum_y[v]
        row_total = row_total + sum_y[v]
    row_final = []
    for n in range(16):
        entering, whole = zero, zero
        for v in range(4):
            own = fin_y[v, pl.ds(n * 8, 8), :].astype(F32)
            decay = jnp.exp2(rates[n] * sum_y[v])
            entering = jnp.where(v < my, decay * entering + own, entering)
            whole = decay * whole + own
        enter_t[pl.ds(n * 8, 8), :] = entering
        row_final.append(whole)
    exchange(row_final, row_total, fin_x, sum_x, mx, 1, along_x)
    for n in range(16):
        entering = zero
        for u in range(4):
            own = fin_x[u, pl.ds(n * 8, 8), :].astype(F32)
            decay = jnp.exp2(rates[n] * sum_x[u])
            entering = jnp.where(u < mx, decay * entering + own, entering)
        rows = pl.ds(n * 8, 8)
        enter_t[rows, :] = enter_t[rows, :] + jnp.exp2(rates[n] * before) * entering

    def add_entering(t, carry):
        rows = pl.ds(pl.multiple_of(t * 8, 8), 8)
        c = cum_t[rows, :]
        outs = [y_t[rows, :], zero]
        for n in range(16):
            outs[n % 2] = outs[n % 2] + bc_s[t // 16, t % 16, 16 + n] * (jnp.exp2(rates[n] * c) * entered[n])
        y_t[rows, :] = outs[0] + outs[1]
        return carry

    entered = [enter_t[pl.ds(n * 8, 8), :] for n in range(16)]
    for half in range(2):
        lax.fori_loop(half * 64, half * 64 + 64, add_entering, 0, unroll=2)
        rows = pl.ds(half * 64, 64)
        for g in range(8):
            cols = pl.ds(g * 128, 128)
            y = y_t[pl.ds(half * 512 + g, 64, stride=8), :]
            y = y + skip[:, cols] * conv_out[rows, cols].astype(F32)
            z = gate_in[rows, cols].astype(F32)
            ga[pl.ds(mx, 1), rows, cols] = (y * (z * jax.nn.sigmoid(z))).astype(BF16)[None]
        place = ga.at[mx, rows]
        for k, d in enumerate((1, -1)):
            s = half * 2 + k
            send(place, place, g_send.at[0], g_recv.at[s], along_x(d))

    def project(u):
        for v in range(4):
            cols = pl.ds(v * 256, 256)
            out = dot(ga[u], opg[v])
            zs[pl.ds(u, 1), :, :, cols] = out.astype(BF16).reshape(1, 8, 16, 256)
        rz[pl.ds(u, 1), pl.ds(exp, 1)] = zs[pl.ds(u, 1), pl.ds(exp, 1)]

    def scatter_group(k, u):
        for d in range(1, 8):
            src = zs.at[u, lax.rem(exp + d, 8)]
            send(src, rz.at[u, exp], z_send.at[0], z_recv.at[k], peer(d))

    settle(opg.at[0], o_recv.at[2])
    left, right, far = wrap(mx - 1, 4), wrap(mx + 1, 4), wrap(mx + 2, 4)
    top, low = pl.ds(0, 64), pl.ds(64, 64)
    project(mx)
    scatter_group(0, mx)
    settle(ga.at[0, top], g_recv.at[0])
    send(ga.at[left, top], ga.at[left, top], g_send.at[0], g_recv.at[4], along_x(1))
    settle(ga.at[0, top], g_recv.at[1])
    settle(ga.at[0, top], g_recv.at[3])
    send(ga.at[right, low], ga.at[right, low], g_send.at[0], g_recv.at[4], along_x(-1))
    settle(ga.at[0, top], g_recv.at[2])
    for k, u in ((1, left), (2, right)):
        project(u)
        scatter_group(k, u)
    settle(ga.at[0], g_recv.at[4])
    project(far)
    scatter_group(3, far)
    for k, (u, d) in enumerate(((mx, 0), (left, -1), (right, 1), (far, 2))):
        settle(rz.at[0, pl.ds(0, 7)], z_recv.at[k])
        total = rz[u, 0].astype(F32)
        for j in range(1, 8):
            total = total + rz[u, j].astype(F32)
        if d == 0:
            mo[pl.ds(mx, 1)] = total.astype(BF16)[None]
        else:
            ms[k - 1] = total.astype(BF16)
            send(ms.at[k - 1], mo.at[mx], m_sem.at[0], m_sem.at[1], along_x(d))
    settle(mo.at[pl.ds(0, 3)], m_sem.at[1])

    squares = jnp.zeros((16, 1), F32)
    for u in range(4):
        cols = pl.ds(u * 1024, 1024)
        rows = residual[:, cols].astype(F32) + mo[u].astype(F32)
        stream[:, cols] = rows
        squares = squares + jnp.sum(rows * rows, axis=1, keepdims=True)
    scale = lax.rsqrt(squares * (1.0 / 4096.0) + 1e-06)
    logits = jnp.zeros((8, 16), F32)
    for u in range(4):
        cols = pl.ds(u * 1024, 1024)
        rows = (stream[:, cols] * scale * gain[:, cols]).astype(BF16)
        normed[:, cols] = rows
        logits = logits + dot_t(router[:, cols], rows)
    ids = expert_ids[...]
    lanes = lax.broadcasted_iota(jnp.int32, (8, 16), 0)
    signs = jnp.where(ids[0:1] == lanes, 1.0, 0.0) - jnp.where(ids[1:2] == lanes, 1.0, 0.0)
    first = jax.nn.sigmoid(jnp.sum(logits * signs, axis=0, keepdims=True))

    def drain():
        settle(rim, h_sem.at[0])
        settle(opg.at[pl.ds(0, 3)], o_send.at[0])
        settle(parts.at[pl.ds(0, 7)], a_sem.at[0])
        settle(low_rank.at[pl.ds(0, 7)], b_sem.at[0])
        settle(maps.at[pl.ds(0, 7)], b_sem.at[1])
        for base, (fin, sums) in enumerate(((fin_y, sum_y), (fin_x, sum_x))):
            settle(fin.at[pl.ds(0, 3)], c_send.at[0, base])
            settle(sums.at[pl.ds(0, 3)], c_send.at[1, base])
        settle(ga.at[pl.ds(0, 3)], g_send.at[0])
        settle(rz.at[:, pl.ds(0, 7)], z_send.at[0])
        settle(mo.at[pl.ds(0, 3)], m_sem.at[0])

    return first, drain


def experts(r, gate_row, drain, out, exp, mx, my, halves, loads):
    pick = r["pick"]
    result = r["result"]
    e_sem = r["e_sem"]
    stream = r["stream"]
    normed = r["normed"]
    spread = r["spread"]
    fetch = r["fetch"]
    go = r["go"]
    rcv = r["rcv"]
    rback = r["rback"]
    xa = r["xa"]
    xb = r["xb"]
    wgu = r["wgu"]
    wd = r["wd"]
    lhs = r["lhs"]
    lhs_down = r["lhs_down"]
    acc = r["acc"]
    hid = r["hid"]
    oa = r["oa"]
    ob = r["ob"]
    far = r["far"]
    near = r["near"]
    tot = r["tot"]
    far2 = r["far2"]
    near2 = r["near2"]
    d_send = r["d_send"]
    d_recv = r["d_recv"]
    u_send = r["u_send"]
    u_recv = r["u_recv"]
    s_send = r["s_send"]
    s_recv = r["s_recv"]
    r_send = r["r_send"]
    r_recv = r["r_recv"]
    xs, os = (xa, xb), (oa, ob)
    lo, hi = pl.ds(0, 1024), pl.ds(1024, 1024)
    every = slice(None)

    windows = (0, 768, 1280)

    def all_to_all(half, into, ss, rs):
        for d in range(1, 8):
            peer = lax.rem(exp + d, 8)
            src, dst = go.at[half, peer], into.at[half, exp]
            remote(src, dst, ss.at[half], rs.at[half], {"exp": peer}).start()
        into[half, pl.ds(exp, 1)] = go[half, pl.ds(exp, 1)]

    for i in range(2):
        packed = jnp.zeros((128, 768), F32)
        for k, w in enumerate(windows):
            packed = packed + dot(spread[k], normed[:, pl.ds(i * 2048 + w, 768)])
        go[i] = packed.astype(BF16).reshape(8, 16, 768)
        all_to_all(i, rcv, d_send, d_recv)
    acc[...] = jnp.zeros_like(acc)

    def push(i, at, cols, ss, rs, device):
        place = xs[i].at[at + (every, cols)] if cols is not None else xs[i].at[at]
        remote(place, place, u_send.at[i, ss], u_recv.at[i, rs], device).start()

    steps = [[wrap(h.p + d, 4) for d in (0, -1, 1, 2)] for h in halves]

    def second_start(i, g):
        h = halves[i]
        at = h.unit(steps[i][g], h.q)
        push(i, at, None, 1, 3 + g, h.two(1))
        push(i, at, None, 1, 3 + g, h.two(-1))

    def second_pass(i, g):
        h, u = halves[i], steps[i][g]
        settle(xs[i].at[0, pl.ds(0, 2)], u_recv.at[i, 3 + g])
        push(i, h.unit(u, wrap(h.q - 1, 4)), lo, 2, 7, h.two(1))
        push(i, h.unit(u, wrap(h.q + 1, 4)), hi, 2, 7, h.two(-1))

    for i, (h, x) in enumerate(zip(halves, xs)):
        settle(rcv.at[i, pl.ds(0, 7)], d_recv.at[i])
        flat = rcv[i].reshape(128, 768)
        for k, w in enumerate(windows):
            block = dot(pick[k], flat).astype(BF16)[None, None]
            x[pl.ds(mx, 1), pl.ds(my, 1), :, pl.ds(w, 768)] = block
        at = h.unit(h.p, h.q)
        push(i, at, None, 0, 0, h.one(1))
        push(i, at, None, 0, 1, h.one(-1))
        if i == 0:
            second_start(0, 0)
    for i, (h, x) in enumerate(zip(halves, xs)):
        settle(x.at[0, 0], u_recv.at[i, 0])
        push(i, h.unit(steps[i][1], h.q), lo, 0, 2, h.one(1))
        settle(x.at[0, 0], u_recv.at[i, 1])
        push(i, h.unit(steps[i][2], h.q), hi, 0, 2, h.one(-1))
        if i == 0:
            second_start(1, 0)
    second_start(0, 1)
    second_start(1, 1)
    for i in range(2):
        settle(xs[i].at[0, 0], u_recv.at[i, 2])
        second_start(i, 2)
        second_start(i, 3)

    def gate_up(i, units):
        for n, at in enumerate(units):
            lhs[n] = xs[i][at]
        for j in range(6):
            cols = pl.ds(j * 256, 256)
            part = dot(lhs[...].reshape(160, 2048), wgu[pl.ds(i * 2048, 2048), cols])
            for n, at in enumerate(units):
                place = at + (every, cols)
                acc[place] = acc[place] + part[n * 40 : (n + 1) * 40]

    def line(i, v):
        return [halves[i].unit(u, v) for u in steps[i]]

    def beside(i, gs):
        h = halves[i]
        return [h.unit(steps[i][g], wrap(h.q + d, 4)) for g in gs for d in (-1, 1)]

    loads[0].wait()
    loads[1].wait()
    gate_up(0, line(0, halves[0].q))
    second_pass(0, 0)
    second_pass(1, 0)
    gate_up(1, line(1, halves[1].q))
    second_pass(0, 1)
    second_pass(1, 1)
    gate_up(0, beside(0, (0, 1)))
    second_pass(0, 2)
    second_pass(1, 2)
    gate_up(1, beside(1, (0, 1)))
    second_pass(0, 3)
    second_pass(1, 3)
    gate_up(0, beside(0, (2, 3)))
    gate_up(1, beside(1, (2, 3)))

    def activate(units):
        for at in units:
            gate = acc[at + (every, pl.ds(0, 768))]
            up = acc[at + (every, pl.ds(768, 768))]
            hid[at] = (gate * jax.nn.sigmoid(gate) * up).astype(BF16)

    def down(i, units):
        count = len(units)
        for n, at in enumerate(units):
            lhs_down[n] = hid[at]
        for j in range(8):
            cols = pl.ds(j * 256, 256)
            rows = lhs_down[pl.ds(0, count)].reshape(count * 40, 768)
            part = dot(rows, wd[:, pl.ds(i * 2048 + j * 256, 256)]).astype(BF16)
            for n, at in enumerate(units):
                os[i][at + (every, cols)] = part[n * 40 : (n + 1) * 40]

    def send(src, dst, i, ss, rs, device):
        remote(src, dst, s_send.at[i, ss], s_recv.at[i, rs], device).start()

    def add_into(ref, at, other, other_at):
        ref[at] = (ref[at].astype(F32) + other[other_at].astype(F32)).astype(BF16)

    order = [[wrap(h.p + d, 4) for d in (2, 1, -1, 0)] for h in halves]

    def send_near(i, ks):
        h = halves[i]
        sides = ((wrap(h.q + 1, 4), 1, hi, 0), (wrap(h.q - 1, 4), -1, lo, 1))
        down(i, [h.unit(order[i][k], v) for v, _, _, _ in sides for k in ks])
        for v, d, cols, b in sides:
            for k in ks:
                u = order[i][k]
                src, dst = os[i].at[h.unit(u, v) + (every, cols)], near.at[i, b, u, :, cols]
                send(src, dst, i, 0, 4, h.two(d))

    xx, yy = [wrap(mx + d, 4) for d in (0, 1, -1)], [wrap(my + d, 4) for d in (0, 1, -1)]
    activate([(u, v) for u in xx for v in yy])
    loads[2].wait()
    for i in range(2):
        send_near(i, (1, 2, 3))
    for i, h in enumerate(halves):
        settle(xs[i].at[0], u_recv.at[i, 7])
        gate_up(i, line(i, wrap(h.q + 2, 4)))
    fx, fy = wrap(mx + 2, 4), wrap(my + 2, 4)
    activate([(fx, v) for v in yy] + [(u, fy) for u in xx] + [(fx, fy)])
    for i, h in enumerate(halves):
        v = wrap(h.q + 2, 4)
        down(i, [h.unit(u, v) for u in order[i]])
        for k, u in enumerate(order[i]):
            at = h.unit(u, v)
            send(os[i].at[at + (every, lo)], far.at[i, 0, u], i, 0, k, h.two(1))
            send(os[i].at[at + (every, hi)], far.at[i, 1, u], i, 0, k, h.two(-1))
    for i in range(2):
        send_near(i, (0,))
    down(0, line(0, halves[0].q))
    for k in range(4):
        for i, h in enumerate(halves):
            u = order[i][k]
            settle(xs[i].at[0, 0], s_recv.at[i, k])
            for b, d, cols in ((0, 1, lo), (1, -1, hi)):
                at = h.unit(u, wrap(h.q + d, 4)) + (every, cols)
                add_into(os[i], at, far, (i, b, u))
                send(os[i].at[at], near.at[i, b, u, :, cols], i, 0, 5 + k, h.two(d))
    down(1, line(1, halves[1].q))
    for i in range(2):
        settle(xs[i].at[0], s_recv.at[i, 4])
    for k in range(4):
        for i, h in enumerate(halves):
            u = order[i][k]
            settle(xs[i].at[0, 0], s_recv.at[i, 5 + k])
            mine = os[i][h.unit(u, h.q)].astype(F32)
            mine = mine + near[i, 0, u].astype(F32) + near[i, 1, u].astype(F32)
            tot[i, u] = mine.astype(BF16)
            if k == 0:
                send(tot.at[i, u, :, lo], far2.at[i, 0], i, 1, 9, h.one(1))
                send(tot.at[i, u, :, hi], far2.at[i, 1], i, 1, 9, h.one(-1))
            if k == 1:
                send(tot.at[i, u, :, hi], near2.at[i, 0, :, hi], i, 1, 10, h.one(1))
            if k == 2:
                send(tot.at[i, u, :, lo], near2.at[i, 1, :, lo], i, 1, 10, h.one(-1))
    for i, h in enumerate(halves):
        settle(xs[i].at[0, 0], s_recv.at[i, 9])
        for b, d, cols in ((0, 1, lo), (1, -1, hi)):
            u = order[i][1 + b]
            add_into(tot, (i, u, every, cols), far2, (i, b))
            send(tot.at[i, u, :, cols], near2.at[i, b, :, cols], i, 1, 10, h.one(d))

    across = (((0,), (0,)), ((), ()))
    for i, h in enumerate(halves):
        settle(xs[i].at[0, pl.ds(0, 2)], s_recv.at[i, 10])
        final = tot[i, h.p].astype(F32) + near2[i, 0].astype(F32) + near2[i, 1].astype(F32)
        final = final.astype(BF16)
        back = jnp.zeros((128, 768), F32)
        for k, w in enumerate(windows):
            block = final[:, w : w + 768]
            back = back + lax.dot_general(pick[k], block, across, preferred_element_type=F32)
        settle(rcv.at[i, pl.ds(0, 7)], d_send.at[i])
        go[i] = back.astype(BF16).reshape(8, 16, 768)
        all_to_all(i, rback, r_send, r_recv)
    eye = lax.broadcasted_iota(jnp.int32, (16, 16), 0) == lax.broadcasted_iota(
        jnp.int32, (16, 16), 1
    )
    gate = jnp.sum(jnp.where(eye, jnp.broadcast_to(gate_row, (16, 16)), 0.0), axis=1, keepdims=True)
    stores = []
    for i in range(2):
        settle(rback.at[i, pl.ds(0, 7)], r_recv.at[i])
        flat = rback[i].reshape(128, 768)
        for j, w in enumerate(windows):
            cols = pl.ds(i * 2048 + w, 768)
            pair = [
                lax.dot_general(fetch[j, k], flat, across, preferred_element_type=F32)
                for k in range(2)
            ]
            mix = gate * pair[0] + (1.0 - gate) * pair[1]
            result[:, cols] = (stream[:, cols] + mix).astype(BF16)
        cols = pl.ds(i * 2048, 2048)
        stores.append(pltpu.make_async_copy(result.at[:, cols], out.at[:, cols], e_sem.at[i]))
        stores[i].start()
    drain()
    for i in range(2):
        settle(rback.at[i, pl.ds(0, 7)], r_send.at[i])
        settle(xs[i].at[0, pl.ds(0, 3)], u_send.at[i, 0])
        settle(xs[i].at[pl.ds(0, 2)], u_send.at[i, 1])
        settle(xs[i].at[0], u_send.at[i, 2])
        settle(xs[i].at[pl.ds(0, 3)], s_send.at[i, 0])
        settle(xs[i].at[0, pl.ds(0, 3)], s_send.at[i, 1])
    for c in stores:
        c.wait()


def token_places(ids, spread, fetch):
    experts_of = lax.broadcasted_iota(jnp.int32, (8, 16), 0)
    hits = [ids[k : k + 1] == experts_of for k in range(2)]
    either = jnp.where(hits[0] | hits[1], 1.0, 0.0).astype(BF16)
    before = lax.broadcasted_iota(jnp.int32, (16, 16), 0) < lax.broadcasted_iota(
        jnp.int32, (16, 16), 1
    )
    earlier = dot(either, jnp.where(before, 1.0, 0.0).astype(BF16))
    rows = lax.broadcasted_iota(jnp.int32, (128, 16), 0).astype(F32)
    for j in range(3):
        found = []
        for k in range(2):
            slot = jnp.sum(jnp.where(hits[k], earlier, 0.0), axis=0, keepdims=True)
            place = ids[k : k + 1].astype(F32) * 16.0 + slot + j * 5.0
            found.append(jnp.where(rows == place, 1.0, 0.0))
            fetch[j, k] = found[k].astype(BF16)
        spread[j] = (found[0] + found[1]).astype(BF16)


def block_kernel(*refs):
    names = INPUTS + ("out",) + tuple(SCRATCH)
    r = dict(zip(names, refs, strict=True))
    ctx, exp = lax.axis_index("ctx"), lax.axis_index("exp")
    mx, my = ctx // 4, ctx % 4
    halves = (Half(0, mx, my), Half(1, mx, my))
    wgu, wd, w_sem = r["wgu"], r["wd"], r["w_sem"]
    loads = [
        pltpu.make_async_copy(r["w_gate"].at[0], wgu.at[:, pl.ds(0, 768)], w_sem.at[0]),
        pltpu.make_async_copy(r["w_up"].at[0], wgu.at[:, pl.ds(768, 768)], w_sem.at[1]),
        pltpu.make_async_copy(r["w_down"].at[0], wd, w_sem.at[2]),
    ]
    for load in loads:
        load.start()
    arrive = greet(
        [{"ctx": lax.rem(ctx + 15, 16)}, {"ctx": lax.rem(ctx + 1, 16)}]
        + [h.one(d) for h in halves for d in (1, 2, -1)]
        + [{"exp": lax.rem(exp + d, 8)} for d in range(1, 8)]
    )
    token_places(r["expert_ids"][...], r["spread"], r["fetch"])
    gate_row, drain = mixer(r, ctx, exp, mx, my, arrive)
    experts(r, gate_row, drain, r["out"], exp, mx, my, halves, loads)


def shards(
    mixer_in,
    gate_in,
    conv_weight,
    conv_bias,
    x_proj,
    dt_proj,
    dt_bias,
    decay_rate,
    skip,
    out_proj,
    residual,
    gain,
    router,
    w_gate,
    w_up,
    w_down,
    expert_ids,
):
    pick = np.zeros((3, 40, 128), np.float32)
    for w in range(3):
        for j in range(8):
            for s in range(5):
                pick[w, j * 5 + s, j * 16 + w * 5 + s] = 1.0
    vmem = pl.BlockSpec(memory_space=pltpu.VMEM)
    anywhere = pl.BlockSpec(memory_space=pl.ANY)
    return pl.pallas_call(
        block_kernel,
        out_shape=jax.ShapeDtypeStruct((16, 4096), BF16),
        in_specs=[anywhere if name.startswith("w_") else vmem for name in INPUTS],
        out_specs=anywhere,
        scratch_shapes=list(SCRATCH.values()),
        compiler_params=pltpu.CompilerParams(
            collective_id=0, has_side_effects=True, vmem_limit_bytes=VMEM_LIMIT
        ),
        cost_estimate=pl.CostEstimate(
            flops=13_500_000_000, bytes_accessed=24_000_000, transcendentals=0
        ),
    )(
        mixer_in,
        gate_in,
        conv_weight,
        conv_bias[None],
        x_proj.T,
        dt_proj,
        dt_bias[None],
        decay_rate,
        skip[None],
        out_proj,
        residual,
        gain[None],
        router.T,
        expert_ids.T,
        w_gate,
        w_up,
        w_down,
        jnp.asarray(pick, BF16),
    )


def solution(mesh):
    in_specs = (
        P("ctx", "exp"),
        P("ctx", "exp"),
        P(None, "exp"),
        P("exp"),
        P("exp", None),
        P(None, "exp"),
        P("exp"),
        P(None, "exp"),
        P("exp"),
        P("exp", "ctx"),
        P(("ctx", "exp"), None),
        P(),
        P(),
        P("exp", None, "ctx"),
        P("exp", None, "ctx"),
        P("exp", "ctx", None),
        P(("ctx", "exp"), None),
    )
    out_specs = P(("ctx", "exp"), None)
    return jax.shard_map(shards, mesh=mesh, in_specs=in_specs, out_specs=out_specs, check_vma=False)
```

```python
import types

import jax
import jax.numpy as jnp
import numpy as np
from jax import lax
from jax.experimental import pallas as pl
from jax.experimental.pallas import tpu as pltpu
from jax.sharding import PartitionSpec as P

F32 = jnp.float32
BF16 = jnp.bfloat16
VMEM_LIMIT = 60 * 1024 * 1024


def remote(src, dst, send_sem, recv_sem, device):
    return pltpu.make_async_remote_copy(
        src_ref=src,
        dst_ref=dst,
        send_sem=send_sem,
        recv_sem=recv_sem,
        device_id=device,
        device_id_type=pl.DeviceIdType.MESH,
    )


def greet(devices):
    barrier = pltpu.get_barrier_semaphore()
    for device in devices:
        pl.semaphore_signal(barrier, inc=1, device_id=device, device_id_type=pl.DeviceIdType.MESH)
    return lambda: pl.semaphore_wait(barrier, len(devices))


def settle(view, sem):
    pltpu.make_async_copy(view, view, sem).wait()


def wrap(index, count):
    return lax.rem(index + count, count)


def dot(a, b):
    return jnp.dot(a, b, preferred_element_type=F32)


def dot_t(a, b):
    return lax.dot_general(a, b, (((1,), (1,)), ((), ())), preferred_element_type=F32)


class Half:
    def __init__(self, half, mx, my):
        self.half = half
        self.mx, self.my = mx, my
        self.p, self.q = (mx, my) if half == 0 else (my, mx)

    def one(self, step):
        p = wrap(self.p + step, 4)
        return {"ctx": p * 4 + self.my if self.half == 0 else self.mx * 4 + p}

    def two(self, step):
        q = wrap(self.q + step, 4)
        return {"ctx": self.mx * 4 + q if self.half == 0 else q * 4 + self.my}

    def unit(self, u, v):
        return (u, v) if self.half == 0 else (v, u)

    def group(self, v):
        return (slice(None), v) if self.half == 0 else (v, slice(None))


LOG2E = 1.4426950408889634

INPUTS = (
    "mixer_in",
    "gate_in",
    "conv_weight",
    "conv_bias",
    "x_proj",
    "dt_proj",
    "dt_bias",
    "decay_rate",
    "skip",
    "out_proj",
    "residual",
    "gain",
    "router",
    "expert_ids",
    "w_gate",
    "w_up",
    "w_down",
    "pick",
)

SCRATCH = dict(
    stream=pltpu.VMEM((16, 4096), F32),
    result=pltpu.VMEM((16, 4096), BF16),
    e_sem=pltpu.SemaphoreType.DMA((2,)),
    normed=pltpu.VMEM((16, 4096), BF16),
    spread=pltpu.VMEM((3, 128, 16), BF16),
    fetch=pltpu.VMEM((3, 2, 128, 16), BF16),
    rim=pltpu.VMEM((16, 1024), BF16),
    padded=pltpu.VMEM((136, 1024), F32),
    conv_out=pltpu.VMEM((128, 1024), BF16),
    part=pltpu.VMEM((8, 16, 544), BF16),
    parts=pltpu.VMEM((8, 16, 544), BF16),
    low_rank=pltpu.VMEM((8, 16, 512), BF16),
    maps=pltpu.VMEM((8, 16, 128), F32),
    bc_s=pltpu.SMEM((8, 16, 128), F32),
    step_t=pltpu.VMEM((1024, 128), F32),
    drive_t=pltpu.VMEM((1024, 128), F32),
    cum_t=pltpu.VMEM((1024, 128), F32),
    y_t=pltpu.VMEM((1024, 128), F32),
    rate_t=pltpu.VMEM((128, 128), F32),
    enter_t=pltpu.VMEM((128, 128), F32),
    fin_own=pltpu.VMEM((2, 128, 128), BF16),
    fin_y=pltpu.VMEM((4, 128, 128), BF16),
    sum_y=pltpu.VMEM((4, 8, 128), F32),
    fin_x=pltpu.VMEM((4, 128, 128), BF16),
    sum_x=pltpu.VMEM((4, 8, 128), F32),
    opg=pltpu.VMEM((2, 4, 1024, 256), BF16),
    ga=pltpu.VMEM((2, 4, 64, 1024), BF16),
    zs=pltpu.VMEM((4, 4, 2, 16, 1024), BF16),
    pair=pltpu.VMEM((4, 4, 16, 1024), BF16),
    both=pltpu.VMEM((4, 4, 16, 1024), BF16),
    p_send=pltpu.SemaphoreType.DMA((1,)),
    p_recv=pltpu.SemaphoreType.DMA((4,)),
    rz=pltpu.VMEM((4, 4, 16, 1024), BF16),
    ms=pltpu.VMEM((3, 16, 1024), BF16),
    mo=pltpu.VMEM((4, 16, 1024), BF16),
    h_sem=pltpu.SemaphoreType.DMA((2,)),
    a_sem=pltpu.SemaphoreType.DMA((2,)),
    b_sem=pltpu.SemaphoreType.DMA((4,)),
    o_send=pltpu.SemaphoreType.DMA((2,)),
    o_recv=pltpu.SemaphoreType.DMA((2, 3)),
    c_send=pltpu.SemaphoreType.DMA((2, 2)),
    c_recv=pltpu.SemaphoreType.DMA((2, 2)),
    g_send=pltpu.SemaphoreType.DMA((2,)),
    g_recv=pltpu.SemaphoreType.DMA((2, 3)),
    z_send=pltpu.SemaphoreType.DMA((1,)),
    z_recv=pltpu.SemaphoreType.DMA((4,)),
    m_sem=pltpu.SemaphoreType.DMA((2,)),
    l_sem=pltpu.SemaphoreType.DMA((1,)),
    go=pltpu.VMEM((2, 8, 16, 768), BF16),
    rcv=pltpu.VMEM((2, 8, 16, 768), BF16),
    rback=pltpu.VMEM((2, 8, 16, 768), BF16),
    xa=pltpu.VMEM((4, 4, 40, 2048), BF16),
    xb=pltpu.VMEM((4, 4, 40, 2048), BF16),
    wgu=pltpu.VMEM((4096, 1536), BF16),
    wd=pltpu.VMEM((768, 4096), BF16),
    lhs=pltpu.VMEM((4, 40, 2048), BF16),
    lhs_down=pltpu.VMEM((6, 40, 768), BF16),
    acc=pltpu.VMEM((4, 4, 40, 1536), F32),
    hid=pltpu.VMEM((4, 4, 40, 768), BF16),
    oa=pltpu.VMEM((4, 4, 40, 2048), BF16),
    ob=pltpu.VMEM((4, 4, 40, 2048), BF16),
    far=pltpu.VMEM((2, 2, 4, 40, 1024), BF16),
    near=pltpu.VMEM((2, 2, 4, 40, 2048), BF16),
    tot=pltpu.VMEM((2, 4, 40, 2048), BF16),
    far2=pltpu.VMEM((2, 2, 40, 1024), BF16),
    near2=pltpu.VMEM((2, 2, 40, 2048), BF16),
    w_sem=pltpu.SemaphoreType.DMA((3,)),
    d_send=pltpu.SemaphoreType.DMA((2,)),
    d_recv=pltpu.SemaphoreType.DMA((2,)),
    u_send=pltpu.SemaphoreType.DMA((2, 3)),
    u_recv=pltpu.SemaphoreType.DMA((2, 8)),
    s_send=pltpu.SemaphoreType.DMA((2, 2)),
    s_recv=pltpu.SemaphoreType.DMA((2, 11)),
    r_send=pltpu.SemaphoreType.DMA((2,)),
    r_recv=pltpu.SemaphoreType.DMA((2,)),
)


def mixer(r, ctx, exp, mx, my, halves, arrive):
    mixer_in = r.mixer_in
    gate_in = r.gate_in
    conv_weight = r.conv_weight
    conv_bias = r.conv_bias
    x_proj = r.x_proj
    dt_proj = r.dt_proj
    dt_bias = r.dt_bias
    decay_rate = r.decay_rate
    skip = r.skip
    out_proj = r.out_proj
    residual = r.residual
    gain = r.gain
    router = r.router
    expert_ids = r.expert_ids
    stream = r.stream
    normed = r.normed
    rim = r.rim
    padded = r.padded
    conv_out = r.conv_out
    part = r.part
    parts = r.parts
    low_rank = r.low_rank
    maps = r.maps
    bc_s = r.bc_s
    step_t = r.step_t
    drive_t = r.drive_t
    cum_t = r.cum_t
    y_t = r.y_t
    rate_t = r.rate_t
    enter_t = r.enter_t
    fin_own = r.fin_own
    fin_y = r.fin_y
    sum_y = r.sum_y
    fin_x = r.fin_x
    sum_x = r.sum_x
    opg = r.opg
    ga = r.ga
    zs = r.zs
    pair = r.pair
    both = r.both
    p_send = r.p_send
    p_recv = r.p_recv
    rz = r.rz
    ms = r.ms
    mo = r.mo
    h_sem = r.h_sem
    a_sem = r.a_sem
    b_sem = r.b_sem
    o_send = r.o_send
    o_recv = r.o_recv
    c_send = r.c_send
    c_recv = r.c_recv
    g_send = r.g_send
    g_recv = r.g_recv
    z_send = r.z_send
    z_recv = r.z_recv
    m_sem = r.m_sem
    l_sem = r.l_sem
    every = slice(None)

    def along_x(d):
        return {"ctx": wrap(mx + d, 4) * 4 + my}

    def along_y(d):
        return {"ctx": mx * 4 + wrap(my + d, 4)}

    def peer(d):
        return {"exp": lax.rem(exp + d, 8)}

    ahead = {"ctx": lax.rem(ctx + 1, 16)}

    def send(src, dst, ss, rs, device):
        remote(src, dst, ss, rs, device).start()

    padded[pl.ds(8, 128), :] = mixer_in[...].astype(F32)
    for g in range(8):
        rate_t[pl.ds(g, 16, stride=8), :] = decay_rate[:, g * 128 : (g + 1) * 128] * (-LOG2E)

    def convolve(start, rows):
        for g in range(8):
            cols = pl.ds(g * 128, 128)
            total = conv_bias[:, cols]
            for k in range(4):
                taps = conv_weight[k : k + 1, cols]
                total = total + taps * padded[pl.ds(start + 5 + k, rows), cols]
            conv_out[pl.ds(start, rows), cols] = (total * jax.nn.sigmoid(total)).astype(BF16)

    def channel_sums(start, rows):
        sums = dot_t(conv_out[pl.ds(start, rows), :], x_proj[...]).astype(BF16)
        part[pl.ds(start // 16, rows // 16)] = sums.reshape(rows // 16, 16, 544)

    convolve(16, 112)

    arrive()
    send(mixer_in.at[pl.ds(112, 16)], rim, h_sem.at[0], h_sem.at[1], ahead)
    for i, h in enumerate(halves):
        send(out_proj, opg.at[i, h.q], o_send.at[i], o_recv.at[i, 0], h.two(1))
        send(out_proj, opg.at[i, h.q], o_send.at[i], o_recv.at[i, 1], h.two(-1))
        opg[i, pl.ds(h.q, 1)] = out_proj[...][None]
    channel_sums(16, 112)
    settle(rim, h_sem.at[1])
    keep = jnp.where(ctx > 0, 1.0, 0.0).astype(F32)
    padded[pl.ds(0, 8), :] = rim[pl.ds(0, 16), :].astype(F32)[8:] * keep
    convolve(0, 16)
    channel_sums(0, 16)

    for d in range(1, 8):
        src = part.at[lax.rem(exp + d, 8)]
        send(src, parts.at[exp], a_sem.at[0], a_sem.at[1], peer(d))
    parts[pl.ds(exp, 1)] = part[pl.ds(exp, 1)]
    settle(parts.at[pl.ds(0, 7)], a_sem.at[1])
    total = parts[0].astype(F32)
    for j in range(1, 8):
        total = total + parts[j].astype(F32)
    low_rank[pl.ds(exp, 1)] = total[:, :512].astype(BF16)[None]
    maps[pl.ds(exp, 1), :, pl.ds(0, 32)] = total[:, 512:][None]
    for d in range(1, 8):
        for k, ref in enumerate((low_rank, maps)):
            send(ref.at[exp], ref.at[exp], b_sem.at[k], b_sem.at[2 + k], peer(d))
    settle(low_rank.at[pl.ds(0, 7)], b_sem.at[2])
    settle(maps.at[pl.ds(0, 7)], b_sem.at[3])
    top, low = pl.ds(0, 512), pl.ds(512, 512)
    for i, h in enumerate(halves):
        for k, d, rows in ((0, 1, top), (1, -1, low)):
            settle(opg.at[0, 0], o_recv.at[i, k])
            place = opg.at[i, wrap(h.q - d, 4), rows]
            send(place, place, o_send.at[i], o_recv.at[i, 2], h.two(d))
    scalars = pltpu.make_async_copy(maps, bc_s, l_sem.at[0])
    scalars.start()
    step_low = low_rank[...].reshape(128, 512)
    for j in range(4):
        cols = pl.ds(j * 256, 256)
        raw = dot(step_low, dt_proj[:, cols]) + dt_bias[:, cols]
        step = jnp.maximum(raw, 0.0) + jnp.log1p(jnp.exp(-jnp.abs(raw)))
        drive = step * conv_out[:, cols].astype(F32)
        for i in range(2):
            rows = pl.ds(j * 2 + i, 128, stride=8)
            step_t[rows, :] = step[:, i * 128 : (i + 1) * 128]
            drive_t[rows, :] = drive[:, i * 128 : (i + 1) * 128]
    scalars.wait()

    rates = [rate_t[pl.ds(n * 8, 8), :] for n in range(16)]
    zero = jnp.zeros((8, 128), F32)

    def scan_step(t, carry):
        states, running = carry
        rows = pl.ds(pl.multiple_of(t * 8, 8), 8)
        s, d = step_t[rows, :], drive_t[rows, :]
        outs = [zero, zero]
        after = []
        for n in range(16):
            h = jnp.exp2(rates[n] * s) * states[n] + bc_s[t // 16, t % 16, n] * d
            outs[n % 2] = outs[n % 2] + bc_s[t // 16, t % 16, 16 + n] * h
            after.append(h)
        running = running + s
        y_t[rows, :] = outs[0] + outs[1]
        cum_t[rows, :] = running
        return (tuple(after), running)

    states, running = lax.fori_loop(0, 128, scan_step, ((zero,) * 16, zero), unroll=2)

    def exchange(finals, total, fin, sums, place, base, step):
        for n in range(16):
            fin_own[base, pl.ds(n * 8, 8), :] = finals[n].astype(BF16)
        sums[pl.ds(place, 1)] = total[None]
        fin[pl.ds(place, 1)] = fin_own[base][None]
        for d in (1, -1, 2):
            send(fin_own.at[base], fin.at[place], c_send.at[0, base], c_recv.at[0, base], step(d))
            send(sums.at[place], sums.at[place], c_send.at[1, base], c_recv.at[1, base], step(d))
        settle(fin.at[pl.ds(0, 3)], c_recv.at[0, base])
        settle(sums.at[pl.ds(0, 3)], c_recv.at[1, base])

    exchange(states, running, fin_y, sum_y, my, 0, along_y)
    before, row_total = zero, zero
    for v in range(4):
        before = before + jnp.where(v < my, 1.0, 0.0).astype(F32) * sum_y[v]
        row_total = row_total + sum_y[v]
    row_final = []
    for n in range(16):
        entering, whole = zero, zero
        for v in range(4):
            own = fin_y[v, pl.ds(n * 8, 8), :].astype(F32)
            decay = jnp.exp2(rates[n] * sum_y[v])
            entering = jnp.where(v < my, decay * entering + own, entering)
            whole = decay * whole + own
        enter_t[pl.ds(n * 8, 8), :] = entering
        row_final.append(whole)
    exchange(row_final, row_total, fin_x, sum_x, mx, 1, along_x)
    for n in range(16):
        entering = zero
        for u in range(4):
            own = fin_x[u, pl.ds(n * 8, 8), :].astype(F32)
            decay = jnp.exp2(rates[n] * sum_x[u])
            entering = jnp.where(u < mx, decay * entering + own, entering)
        rows = pl.ds(n * 8, 8)
        enter_t[rows, :] = enter_t[rows, :] + jnp.exp2(rates[n] * before) * entering

    def add_entering(t, carry):
        rows = pl.ds(pl.multiple_of(t * 8, 8), 8)
        c = cum_t[rows, :]
        outs = [y_t[rows, :], zero]
        for n in range(16):
            outs[n % 2] = outs[n % 2] + bc_s[t // 16, t % 16, 16 + n] * (jnp.exp2(rates[n] * c) * entered[n])
        y_t[rows, :] = outs[0] + outs[1]
        return carry

    entered = [enter_t[pl.ds(n * 8, 8), :] for n in range(16)]
    for half in range(2):
        lax.fori_loop(half * 64, half * 64 + 64, add_entering, 0, unroll=2)
        rows = pl.ds(half * 64, 64)
        for g in range(8):
            cols = pl.ds(g * 128, 128)
            y = y_t[pl.ds(half * 512 + g, 64, stride=8), :]
            y = y + skip[:, cols] * conv_out[rows, cols].astype(F32)
            z = gate_in[rows, cols].astype(F32)
            block = (y * (z * jax.nn.sigmoid(z))).astype(BF16)
            ga[half, pl.ds(halves[half].p, 1), :, cols] = block[None]
        place = ga.at[half, halves[half].p]
        for k, d in enumerate((1, -1)):
            send(place, place, g_send.at[half], g_recv.at[half, k], halves[half].one(d))

    hops = (0, -1, 1, 2)

    def project(i, k):
        rows = ga[i, wrap(halves[i].p + hops[k], 4)]
        for v in range(4):
            block = dot(rows, opg[i, v]).astype(BF16).reshape(2, 2, 16, 256)
            zs[k, pl.ds(2 * i, 2), :, :, pl.ds(v * 256, 256)] = block

    mz, core = exp // 2, exp % 2

    def pair_group(k):
        sibling = {"exp": 2 * mz + 1 - core}
        send(zs.at[k, :, 1 - core], pair.at[k], p_send.at[0], p_recv.at[k], sibling)

    def scatter_group(k):
        settle(pair.at[0], p_recv.at[k])
        own = zs[k, :, pl.ds(core, 1)].reshape(4, 16, 1024).astype(F32)
        both[k] = (own + pair[k].astype(F32)).astype(BF16)
        for d in (1, 3, 2):
            z = wrap(mz + d, 4)
            send(both.at[k, z], rz.at[k, mz], z_send.at[0], z_recv.at[k], {"exp": 2 * z + core})
        rz[k, pl.ds(mz, 1)] = both[k, pl.ds(mz, 1)]

    top, low = pl.ds(0, 32), pl.ds(32, 32)
    for i in range(2):
        settle(opg.at[0, 0], o_recv.at[i, 2])
        project(i, 0)
    pair_group(0)
    for i, h in enumerate(halves):
        for k, d, rows in ((0, 1, top), (1, -1, low)):
            settle(ga.at[0, 0], g_recv.at[i, k])
            place = ga.at[i, wrap(h.p - d, 4), rows]
            send(place, place, g_send.at[i], g_recv.at[i, 2], h.one(d))
    scatter_group(0)
    for k in (1, 2):
        project(0, k)
        project(1, k)
        pair_group(k)
    scatter_group(1)
    scatter_group(2)
    for i in range(2):
        settle(ga.at[0, 0], g_recv.at[i, 2])
        project(i, 3)
    pair_group(3)
    scatter_group(3)
    second = exp // 4
    place = mx + second * (my - mx)
    for k, d in enumerate(hops):
        settle(rz.at[0, pl.ds(0, 3)], z_recv.at[k])
        total = rz[k, 0].astype(F32)
        for j in range(1, 4):
            total = total + rz[k, j].astype(F32)
        if d == 0:
            mo[pl.ds(place, 1)] = total.astype(BF16)[None]
        else:
            ms[k - 1] = total.astype(BF16)
            near_x, near_y = along_x(d)["ctx"], along_y(d)["ctx"]
            device = {"ctx": near_x + second * (near_y - near_x)}
            send(ms.at[k - 1], mo.at[place], m_sem.at[0], m_sem.at[1], device)
    settle(mo.at[pl.ds(0, 3)], m_sem.at[1])

    squares = jnp.zeros((16, 1), F32)
    for u in range(4):
        cols = pl.ds(u * 1024, 1024)
        across = [mo[v, :, pl.ds(u * 256, 256)] for v in range(4)]
        mixed = jnp.where(second == 0, mo[u].astype(F32), jnp.concatenate(across, 1).astype(F32))
        rows = residual[:, cols].astype(F32) + mixed
        stream[:, cols] = rows
        squares = squares + jnp.sum(rows * rows, axis=1, keepdims=True)
    scale = lax.rsqrt(squares * (1.0 / 4096.0) + 1e-06)
    logits = jnp.zeros((8, 16), F32)
    for u in range(4):
        cols = pl.ds(u * 1024, 1024)
        rows = (stream[:, cols] * scale * gain[:, cols]).astype(BF16)
        normed[:, cols] = rows
        logits = logits + dot_t(router[:, cols], rows)
    ids = expert_ids[...]
    lanes = lax.broadcasted_iota(jnp.int32, (8, 16), 0)
    signs = jnp.where(ids[0:1] == lanes, 1.0, 0.0) - jnp.where(ids[1:2] == lanes, 1.0, 0.0)
    first = jax.nn.sigmoid(jnp.sum(logits * signs, axis=0, keepdims=True))

    def drain():
        settle(rim, h_sem.at[0])
        for i in range(2):
            settle(opg.at[0, pl.ds(0, 3)], o_send.at[i])
            settle(ga.at[0, pl.ds(0, 3)], g_send.at[i])
        settle(parts.at[pl.ds(0, 7)], a_sem.at[0])
        settle(low_rank.at[pl.ds(0, 7)], b_sem.at[0])
        settle(maps.at[pl.ds(0, 7)], b_sem.at[1])
        for base, (fin, sums) in enumerate(((fin_y, sum_y), (fin_x, sum_x))):
            settle(fin.at[pl.ds(0, 3)], c_send.at[0, base])
            settle(sums.at[pl.ds(0, 3)], c_send.at[1, base])
        settle(pair, p_send.at[0])
        settle(rz.at[:, pl.ds(0, 3)], z_send.at[0])
        settle(mo.at[pl.ds(0, 3)], m_sem.at[0])

    return first, drain


def experts(r, gate_row, drain, out, exp, mx, my, halves, loads):
    pick = r.pick
    result = r.result
    e_sem = r.e_sem
    stream = r.stream
    normed = r.normed
    spread = r.spread
    fetch = r.fetch
    go = r.go
    rcv = r.rcv
    rback = r.rback
    xa = r.xa
    xb = r.xb
    wgu = r.wgu
    wd = r.wd
    lhs = r.lhs
    lhs_down = r.lhs_down
    acc = r.acc
    hid = r.hid
    oa = r.oa
    ob = r.ob
    far = r.far
    near = r.near
    tot = r.tot
    far2 = r.far2
    near2 = r.near2
    d_send = r.d_send
    d_recv = r.d_recv
    u_send = r.u_send
    u_recv = r.u_recv
    s_send = r.s_send
    s_recv = r.s_recv
    r_send = r.r_send
    r_recv = r.r_recv
    xs, os = (xa, xb), (oa, ob)
    lo, hi = pl.ds(0, 1024), pl.ds(1024, 1024)
    every = slice(None)

    windows = (0, 768, 1280)

    def all_to_all(half, into, ss, rs):
        for d in range(1, 8):
            peer = lax.rem(exp + d, 8)
            src, dst = go.at[half, peer], into.at[half, exp]
            remote(src, dst, ss.at[half], rs.at[half], {"exp": peer}).start()
        into[half, pl.ds(exp, 1)] = go[half, pl.ds(exp, 1)]

    for i in range(2):
        packed = jnp.zeros((128, 768), F32)
        for k, w in enumerate(windows):
            packed = packed + dot(spread[k], normed[:, pl.ds(i * 2048 + w, 768)])
        go[i] = packed.astype(BF16).reshape(8, 16, 768)
        all_to_all(i, rcv, d_send, d_recv)
    acc[...] = jnp.zeros_like(acc)

    def push(i, at, cols, ss, rs, device):
        place = xs[i].at[at + (every, cols)] if cols is not None else xs[i].at[at]
        remote(place, place, u_send.at[i, ss], u_recv.at[i, rs], device).start()

    steps = [[wrap(h.p + d, 4) for d in (0, -1, 1, 2)] for h in halves]

    def second_start(i, g):
        h = halves[i]
        at = h.unit(steps[i][g], h.q)
        push(i, at, None, 1, 3 + g, h.two(1))
        push(i, at, None, 1, 3 + g, h.two(-1))

    def second_pass(i, g):
        h, u = halves[i], steps[i][g]
        settle(xs[i].at[0, pl.ds(0, 2)], u_recv.at[i, 3 + g])
        push(i, h.unit(u, wrap(h.q - 1, 4)), lo, 2, 7, h.two(1))
        push(i, h.unit(u, wrap(h.q + 1, 4)), hi, 2, 7, h.two(-1))

    for i, (h, x) in enumerate(zip(halves, xs)):
        settle(rcv.at[i, pl.ds(0, 7)], d_recv.at[i])
        flat = rcv[i].reshape(128, 768)
        for k, w in enumerate(windows):
            block = dot(pick[k], flat).astype(BF16)[None, None]
            x[pl.ds(mx, 1), pl.ds(my, 1), :, pl.ds(w, 768)] = block
        at = h.unit(h.p, h.q)
        push(i, at, None, 0, 0, h.one(1))
        push(i, at, None, 0, 1, h.one(-1))
        if i == 0:
            second_start(0, 0)
    for i, (h, x) in enumerate(zip(halves, xs)):
        settle(x.at[0, 0], u_recv.at[i, 0])
        push(i, h.unit(steps[i][1], h.q), lo, 0, 2, h.one(1))
        settle(x.at[0, 0], u_recv.at[i, 1])
        push(i, h.unit(steps[i][2], h.q), hi, 0, 2, h.one(-1))
        if i == 0:
            second_start(1, 0)
    second_start(0, 1)
    second_start(1, 1)
    for i in range(2):
        settle(xs[i].at[0, 0], u_recv.at[i, 2])
        second_start(i, 2)
        second_start(i, 3)

    def gate_up(i, units):
        for n, at in enumerate(units):
            lhs[n] = xs[i][at]
        for j in range(6):
            cols = pl.ds(j * 256, 256)
            part = dot(lhs[...].reshape(160, 2048), wgu[pl.ds(i * 2048, 2048), cols])
            for n, at in enumerate(units):
                place = at + (every, cols)
                acc[place] = acc[place] + part[n * 40 : (n + 1) * 40]

    def line(i, v):
        return [halves[i].unit(u, v) for u in steps[i]]

    def beside(i, gs):
        h = halves[i]
        return [h.unit(steps[i][g], wrap(h.q + d, 4)) for g in gs for d in (-1, 1)]

    loads[0].wait()
    loads[1].wait()
    gate_up(0, line(0, halves[0].q))
    second_pass(0, 0)
    second_pass(1, 0)
    gate_up(1, line(1, halves[1].q))
    second_pass(0, 1)
    second_pass(1, 1)
    gate_up(0, beside(0, (0, 1)))
    second_pass(0, 2)
    second_pass(1, 2)
    gate_up(1, beside(1, (0, 1)))
    second_pass(0, 3)
    second_pass(1, 3)
    gate_up(0, beside(0, (2, 3)))
    gate_up(1, beside(1, (2, 3)))

    def activate(units):
        for at in units:
            gate = acc[at + (every, pl.ds(0, 768))]
            up = acc[at + (every, pl.ds(768, 768))]
            hid[at] = (gate * jax.nn.sigmoid(gate) * up).astype(BF16)

    def down(i, units):
        count = len(units)
        for n, at in enumerate(units):
            lhs_down[n] = hid[at]
        for j in range(8):
            cols = pl.ds(j * 256, 256)
            rows = lhs_down[pl.ds(0, count)].reshape(count * 40, 768)
            part = dot(rows, wd[:, pl.ds(i * 2048 + j * 256, 256)]).astype(BF16)
            for n, at in enumerate(units):
                os[i][at + (every, cols)] = part[n * 40 : (n + 1) * 40]

    def send(src, dst, i, ss, rs, device):
        remote(src, dst, s_send.at[i, ss], s_recv.at[i, rs], device).start()

    def add_into(ref, at, other, other_at):
        ref[at] = (ref[at].astype(F32) + other[other_at].astype(F32)).astype(BF16)

    order = [[wrap(h.p + d, 4) for d in (2, 1, -1, 0)] for h in halves]

    def send_near(i, ks):
        h = halves[i]
        sides = ((wrap(h.q + 1, 4), 1, hi, 0), (wrap(h.q - 1, 4), -1, lo, 1))
        down(i, [h.unit(order[i][k], v) for v, _, _, _ in sides for k in ks])
        for v, d, cols, b in sides:
            for k in ks:
                u = order[i][k]
                src, dst = os[i].at[h.unit(u, v) + (every, cols)], near.at[i, b, u, :, cols]
                send(src, dst, i, 0, 4, h.two(d))

    xx, yy = [wrap(mx + d, 4) for d in (0, 1, -1)], [wrap(my + d, 4) for d in (0, 1, -1)]
    activate([(u, v) for u in xx for v in yy])
    loads[2].wait()
    for i in range(2):
        send_near(i, (1, 2, 3))
    for i, h in enumerate(halves):
        settle(xs[i].at[0], u_recv.at[i, 7])
        gate_up(i, line(i, wrap(h.q + 2, 4)))
    fx, fy = wrap(mx + 2, 4), wrap(my + 2, 4)
    activate([(fx, v) for v in yy] + [(u, fy) for u in xx] + [(fx, fy)])
    for i, h in enumerate(halves):
        v = wrap(h.q + 2, 4)
        down(i, [h.unit(u, v) for u in order[i]])
        for k, u in enumerate(order[i]):
            at = h.unit(u, v)
            send(os[i].at[at + (every, lo)], far.at[i, 0, u], i, 0, k, h.two(1))
            send(os[i].at[at + (every, hi)], far.at[i, 1, u], i, 0, k, h.two(-1))
    for i in range(2):
        send_near(i, (0,))
    down(0, line(0, halves[0].q))
    for k in range(4):
        for i, h in enumerate(halves):
            u = order[i][k]
            settle(xs[i].at[0, 0], s_recv.at[i, k])
            for b, d, cols in ((0, 1, lo), (1, -1, hi)):
                at = h.unit(u, wrap(h.q + d, 4)) + (every, cols)
                add_into(os[i], at, far, (i, b, u))
                send(os[i].at[at], near.at[i, b, u, :, cols], i, 0, 5 + k, h.two(d))
    down(1, line(1, halves[1].q))
    for i in range(2):
        settle(xs[i].at[0], s_recv.at[i, 4])
    for k in range(4):
        for i, h in enumerate(halves):
            u = order[i][k]
            settle(xs[i].at[0, 0], s_recv.at[i, 5 + k])
            mine = os[i][h.unit(u, h.q)].astype(F32)
            mine = mine + near[i, 0, u].astype(F32) + near[i, 1, u].astype(F32)
            tot[i, u] = mine.astype(BF16)
            if k == 0:
                send(tot.at[i, u, :, lo], far2.at[i, 0], i, 1, 9, h.one(1))
                send(tot.at[i, u, :, hi], far2.at[i, 1], i, 1, 9, h.one(-1))
            if k == 1:
                send(tot.at[i, u, :, hi], near2.at[i, 0, :, hi], i, 1, 10, h.one(1))
            if k == 2:
                send(tot.at[i, u, :, lo], near2.at[i, 1, :, lo], i, 1, 10, h.one(-1))
    for i, h in enumerate(halves):
        settle(xs[i].at[0, 0], s_recv.at[i, 9])
        for b, d, cols in ((0, 1, lo), (1, -1, hi)):
            u = order[i][1 + b]
            add_into(tot, (i, u, every, cols), far2, (i, b))
            send(tot.at[i, u, :, cols], near2.at[i, b, :, cols], i, 1, 10, h.one(d))

    across = (((0,), (0,)), ((), ()))
    for i, h in enumerate(halves):
        settle(xs[i].at[0, pl.ds(0, 2)], s_recv.at[i, 10])
        final = tot[i, h.p].astype(F32) + near2[i, 0].astype(F32) + near2[i, 1].astype(F32)
        final = final.astype(BF16)
        back = jnp.zeros((128, 768), F32)
        for k, w in enumerate(windows):
            block = final[:, w : w + 768]
            back = back + lax.dot_general(pick[k], block, across, preferred_element_type=F32)
        settle(rcv.at[i, pl.ds(0, 7)], d_send.at[i])
        go[i] = back.astype(BF16).reshape(8, 16, 768)
        all_to_all(i, rback, r_send, r_recv)
    eye = lax.broadcasted_iota(jnp.int32, (16, 16), 0) == lax.broadcasted_iota(
        jnp.int32, (16, 16), 1
    )
    gate = jnp.sum(jnp.where(eye, jnp.broadcast_to(gate_row, (16, 16)), 0.0), axis=1, keepdims=True)
    stores = []
    for i in range(2):
        settle(rback.at[i, pl.ds(0, 7)], r_recv.at[i])
        flat = rback[i].reshape(128, 768)
        for j, w in enumerate(windows):
            cols = pl.ds(i * 2048 + w, 768)
            pair = [
                lax.dot_general(fetch[j, k], flat, across, preferred_element_type=F32)
                for k in range(2)
            ]
            mix = gate * pair[0] + (1.0 - gate) * pair[1]
            result[:, cols] = (stream[:, cols] + mix).astype(BF16)
        cols = pl.ds(i * 2048, 2048)
        stores.append(pltpu.make_async_copy(result.at[:, cols], out.at[:, cols], e_sem.at[i]))
        stores[i].start()
    drain()
    for i in range(2):
        settle(rback.at[i, pl.ds(0, 7)], r_send.at[i])
        settle(xs[i].at[0, pl.ds(0, 3)], u_send.at[i, 0])
        settle(xs[i].at[pl.ds(0, 2)], u_send.at[i, 1])
        settle(xs[i].at[0], u_send.at[i, 2])
        settle(xs[i].at[pl.ds(0, 3)], s_send.at[i, 0])
        settle(xs[i].at[0, pl.ds(0, 3)], s_send.at[i, 1])
    for c in stores:
        c.wait()


def token_places(ids, spread, fetch):
    experts_of = lax.broadcasted_iota(jnp.int32, (8, 16), 0)
    hits = [ids[k : k + 1] == experts_of for k in range(2)]
    either = jnp.where(hits[0] | hits[1], 1.0, 0.0).astype(BF16)
    before = lax.broadcasted_iota(jnp.int32, (16, 16), 0) < lax.broadcasted_iota(
        jnp.int32, (16, 16), 1
    )
    earlier = dot(either, jnp.where(before, 1.0, 0.0).astype(BF16))
    rows = lax.broadcasted_iota(jnp.int32, (128, 16), 0).astype(F32)
    for j in range(3):
        found = []
        for k in range(2):
            slot = jnp.sum(jnp.where(hits[k], earlier, 0.0), axis=0, keepdims=True)
            place = ids[k : k + 1].astype(F32) * 16.0 + slot + j * 5.0
            found.append(jnp.where(rows == place, 1.0, 0.0))
            fetch[j, k] = found[k].astype(BF16)
        spread[j] = (found[0] + found[1]).astype(BF16)


def block_kernel(*refs):
    names = INPUTS + ("out",) + tuple(SCRATCH)
    r = types.SimpleNamespace(**dict(zip(names, refs, strict=True)))
    ctx, exp = lax.axis_index("ctx"), lax.axis_index("exp")
    mx, my = ctx // 4, ctx % 4
    halves = (Half(0, mx, my), Half(1, mx, my))
    wgu, wd, w_sem = r.wgu, r.wd, r.w_sem
    loads = [
        pltpu.make_async_copy(r.w_gate.at[0], wgu.at[:, pl.ds(0, 768)], w_sem.at[0]),
        pltpu.make_async_copy(r.w_up.at[0], wgu.at[:, pl.ds(768, 768)], w_sem.at[1]),
        pltpu.make_async_copy(r.w_down.at[0], wd, w_sem.at[2]),
    ]
    for load in loads:
        load.start()
    arrive = greet(
        [{"ctx": lax.rem(ctx + 15, 16)}, {"ctx": lax.rem(ctx + 1, 16)}]
        + [h.one(d) for h in halves for d in (1, 2, -1)]
        + [{"exp": lax.rem(exp + d, 8)} for d in range(1, 8)]
    )
    token_places(r.expert_ids[...], r.spread, r.fetch)
    gate_row, drain = mixer(r, ctx, exp, mx, my, halves, arrive)
    experts(r, gate_row, drain, r.out, exp, mx, my, halves, loads)


def shards(
    mixer_in,
    gate_in,
    conv_weight,
    conv_bias,
    x_proj,
    dt_proj,
    dt_bias,
    decay_rate,
    skip,
    out_proj,
    residual,
    gain,
    router,
    w_gate,
    w_up,
    w_down,
    expert_ids,
):
    pick = np.zeros((3, 40, 128), np.float32)
    for w in range(3):
        for j in range(8):
            for s in range(5):
                pick[w, j * 5 + s, j * 16 + w * 5 + s] = 1.0
    vmem = pl.BlockSpec(memory_space=pltpu.VMEM)
    anywhere = pl.BlockSpec(memory_space=pl.ANY)
    return pl.pallas_call(
        block_kernel,
        out_shape=jax.ShapeDtypeStruct((16, 4096), BF16),
        in_specs=[anywhere if name.startswith("w_") else vmem for name in INPUTS],
        out_specs=anywhere,
        scratch_shapes=list(SCRATCH.values()),
        compiler_params=pltpu.CompilerParams(
            collective_id=0, has_side_effects=True, vmem_limit_bytes=VMEM_LIMIT
        ),
        cost_estimate=pl.CostEstimate(
            flops=13_500_000_000, bytes_accessed=24_000_000, transcendentals=0
        ),
    )(
        mixer_in,
        gate_in,
        conv_weight,
        conv_bias[None],
        x_proj.T,
        dt_proj,
        dt_bias[None],
        decay_rate,
        skip[None],
        out_proj,
        residual,
        gain[None],
        router.T,
        expert_ids.T,
        w_gate,
        w_up,
        w_down,
        jnp.asarray(pick, BF16),
    )


def solution(mesh):
    in_specs = (
        P("ctx", "exp"),
        P("ctx", "exp"),
        P(None, "exp"),
        P("exp"),
        P("exp", None),
        P(None, "exp"),
        P("exp"),
        P(None, "exp"),
        P("exp"),
        P("exp", "ctx"),
        P(("ctx", "exp"), None),
        P(),
        P(),
        P("exp", None, "ctx"),
        P("exp", None, "ctx"),
        P("exp", "ctx", None),
        P(("ctx", "exp"), None),
    )
    out_specs = P(("ctx", "exp"), None)
    return jax.shard_map(shards, mesh=mesh, in_specs=in_specs, out_specs=out_specs, check_vma=False)
```

```python
import types

import jax
import jax.numpy as jnp
import numpy as np
from jax import lax
from jax.experimental import pallas as pl
from jax.experimental.pallas import tpu as pltpu
from jax.sharding import PartitionSpec as P

F32 = jnp.float32
BF16 = jnp.bfloat16
VMEM_LIMIT = 60 * 1024 * 1024


def remote(src, dst, send_sem, recv_sem, device):
    return pltpu.make_async_remote_copy(
        src_ref=src,
        dst_ref=dst,
        send_sem=send_sem,
        recv_sem=recv_sem,
        device_id=device,
        device_id_type=pl.DeviceIdType.MESH,
    )


def greet(devices):
    barrier = pltpu.get_barrier_semaphore()
    for device in devices:
        pl.semaphore_signal(barrier, inc=1, device_id=device, device_id_type=pl.DeviceIdType.MESH)
    return lambda: pl.semaphore_wait(barrier, len(devices))


def settle(view, sem):
    pltpu.make_async_copy(view, view, sem).wait()


def wrap(index, count):
    return lax.rem(index + count, count)


def dot(a, b):
    return jnp.dot(a, b, preferred_element_type=F32)


def dot_t(a, b):
    return lax.dot_general(a, b, (((1,), (1,)), ((), ())), preferred_element_type=F32)


class Half:
    def __init__(self, half, mx, my):
        self.half = half
        self.mx, self.my = mx, my
        self.p, self.q = (mx, my) if half == 0 else (my, mx)

    def one(self, step):
        p = wrap(self.p + step, 4)
        return {"ctx": p * 4 + self.my if self.half == 0 else self.mx * 4 + p}

    def two(self, step):
        q = wrap(self.q + step, 4)
        return {"ctx": self.mx * 4 + q if self.half == 0 else q * 4 + self.my}

    def unit(self, u, v):
        return (u, v) if self.half == 0 else (v, u)

    def group(self, v):
        return (slice(None), v) if self.half == 0 else (v, slice(None))


LOG2E = 1.4426950408889634

INPUTS = (
    "mixer_in",
    "gate_in",
    "conv_weight",
    "conv_bias",
    "x_proj",
    "dt_proj",
    "dt_bias",
    "decay_rate",
    "skip",
    "out_proj",
    "residual",
    "gain",
    "router",
    "expert_ids",
    "w_gate",
    "w_up",
    "w_down",
    "pick",
)

SCRATCH = dict(
    stream=pltpu.VMEM((16, 4096), F32),
    result=pltpu.VMEM((16, 4096), BF16),
    e_sem=pltpu.SemaphoreType.DMA((2,)),
    normed=pltpu.VMEM((16, 4096), BF16),
    spread=pltpu.VMEM((3, 128, 16), BF16),
    fetch=pltpu.VMEM((3, 2, 128, 16), BF16),
    rim=pltpu.VMEM((16, 1024), BF16),
    padded=pltpu.VMEM((136, 1024), F32),
    conv_out=pltpu.VMEM((128, 1024), BF16),
    part=pltpu.VMEM((8, 16, 512), BF16),
    own_maps=pltpu.VMEM((8, 16, 128), F32),
    part_maps=pltpu.VMEM((8, 16, 128), F32),
    parts=pltpu.VMEM((8, 16, 512), BF16),
    low_rank=pltpu.VMEM((8, 16, 512), BF16),
    maps=pltpu.VMEM((8, 16, 128), F32),
    bc_s=pltpu.SMEM((8, 16, 128), F32),
    step_t=pltpu.VMEM((1024, 128), F32),
    drive_t=pltpu.VMEM((1024, 128), F32),
    cum_t=pltpu.VMEM((1024, 128), F32),
    y_t=pltpu.VMEM((1024, 128), F32),
    rate_t=pltpu.VMEM((128, 128), F32),
    enter_t=pltpu.VMEM((128, 128), F32),
    fin_own=pltpu.VMEM((2, 128, 128), BF16),
    fin_y=pltpu.VMEM((4, 128, 128), BF16),
    sum_y=pltpu.VMEM((4, 8, 128), F32),
    fin_x=pltpu.VMEM((4, 128, 128), BF16),
    sum_x=pltpu.VMEM((4, 8, 128), F32),
    opg=pltpu.VMEM((2, 4, 1024, 256), BF16),
    ga=pltpu.VMEM((2, 4, 64, 1024), BF16),
    zs=pltpu.VMEM((4, 4, 2, 16, 1024), BF16),
    pair=pltpu.VMEM((4, 4, 16, 1024), BF16),
    both=pltpu.VMEM((4, 4, 16, 1024), BF16),
    p_send=pltpu.SemaphoreType.DMA((1,)),
    p_recv=pltpu.SemaphoreType.DMA((4,)),
    rz=pltpu.VMEM((4, 4, 16, 1024), BF16),
    ms=pltpu.VMEM((3, 16, 1024), BF16),
    mo=pltpu.VMEM((4, 16, 1024), BF16),
    h_sem=pltpu.SemaphoreType.DMA((2,)),
    a_sem=pltpu.SemaphoreType.DMA((4,)),
    b_sem=pltpu.SemaphoreType.DMA((4,)),
    o_send=pltpu.SemaphoreType.DMA((2,)),
    o_recv=pltpu.SemaphoreType.DMA((2, 3)),
    c_send=pltpu.SemaphoreType.DMA((2, 2)),
    c_recv=pltpu.SemaphoreType.DMA((2, 2)),
    g_send=pltpu.SemaphoreType.DMA((2,)),
    g_recv=pltpu.SemaphoreType.DMA((2, 3)),
    z_send=pltpu.SemaphoreType.DMA((1,)),
    z_recv=pltpu.SemaphoreType.DMA((4,)),
    m_sem=pltpu.SemaphoreType.DMA((2,)),
    l_sem=pltpu.SemaphoreType.DMA((1,)),
    go=pltpu.VMEM((2, 8, 16, 768), BF16),
    rcv=pltpu.VMEM((2, 8, 16, 768), BF16),
    rback=pltpu.VMEM((2, 8, 16, 768), BF16),
    xa=pltpu.VMEM((4, 4, 40, 2048), BF16),
    xb=pltpu.VMEM((4, 4, 40, 2048), BF16),
    wgu=pltpu.VMEM((4096, 1536), BF16),
    wd=pltpu.VMEM((768, 4096), BF16),
    lhs=pltpu.VMEM((4, 40, 2048), BF16),
    lhs_down=pltpu.VMEM((6, 40, 768), BF16),
    acc=pltpu.VMEM((4, 4, 40, 1536), F32),
    hid=pltpu.VMEM((4, 4, 40, 768), BF16),
    oa=pltpu.VMEM((4, 4, 40, 2048), BF16),
    ob=pltpu.VMEM((4, 4, 40, 2048), BF16),
    far=pltpu.VMEM((2, 2, 4, 40, 1024), BF16),
    near=pltpu.VMEM((2, 2, 4, 40, 2048), BF16),
    tot=pltpu.VMEM((2, 4, 40, 2048), BF16),
    far2=pltpu.VMEM((2, 2, 40, 1024), BF16),
    near2=pltpu.VMEM((2, 2, 40, 2048), BF16),
    w_sem=pltpu.SemaphoreType.DMA((3,)),
    d_send=pltpu.SemaphoreType.DMA((2,)),
    d_recv=pltpu.SemaphoreType.DMA((2,)),
    u_send=pltpu.SemaphoreType.DMA((2, 3)),
    u_recv=pltpu.SemaphoreType.DMA((2, 8)),
    s_send=pltpu.SemaphoreType.DMA((2, 2)),
    s_recv=pltpu.SemaphoreType.DMA((2, 11)),
    r_send=pltpu.SemaphoreType.DMA((2,)),
    r_recv=pltpu.SemaphoreType.DMA((2,)),
)


def mixer(r, ctx, exp, mx, my, halves, arrive):
    mixer_in = r.mixer_in
    gate_in = r.gate_in
    conv_weight = r.conv_weight
    conv_bias = r.conv_bias
    x_proj = r.x_proj
    dt_proj = r.dt_proj
    dt_bias = r.dt_bias
    decay_rate = r.decay_rate
    skip = r.skip
    out_proj = r.out_proj
    residual = r.residual
    gain = r.gain
    router = r.router
    expert_ids = r.expert_ids
    stream = r.stream
    normed = r.normed
    rim = r.rim
    padded = r.padded
    conv_out = r.conv_out
    part = r.part
    own_maps = r.own_maps
    part_maps = r.part_maps
    parts = r.parts
    low_rank = r.low_rank
    maps = r.maps
    bc_s = r.bc_s
    step_t = r.step_t
    drive_t = r.drive_t
    cum_t = r.cum_t
    y_t = r.y_t
    rate_t = r.rate_t
    enter_t = r.enter_t
    fin_own = r.fin_own
    fin_y = r.fin_y
    sum_y = r.sum_y
    fin_x = r.fin_x
    sum_x = r.sum_x
    opg = r.opg
    ga = r.ga
    zs = r.zs
    pair = r.pair
    both = r.both
    p_send = r.p_send
    p_recv = r.p_recv
    rz = r.rz
    ms = r.ms
    mo = r.mo
    h_sem = r.h_sem
    a_sem = r.a_sem
    b_sem = r.b_sem
    o_send = r.o_send
    o_recv = r.o_recv
    c_send = r.c_send
    c_recv = r.c_recv
    g_send = r.g_send
    g_recv = r.g_recv
    z_send = r.z_send
    z_recv = r.z_recv
    m_sem = r.m_sem
    l_sem = r.l_sem
    every = slice(None)

    def along_x(d):
        return {"ctx": wrap(mx + d, 4) * 4 + my}

    def along_y(d):
        return {"ctx": mx * 4 + wrap(my + d, 4)}

    def peer(d):
        return {"exp": lax.rem(exp + d, 8)}

    ahead = {"ctx": lax.rem(ctx + 1, 16)}

    def send(src, dst, ss, rs, device):
        remote(src, dst, ss, rs, device).start()

    own_maps[...] = jnp.zeros_like(own_maps)
    padded[pl.ds(8, 128), :] = mixer_in[...].astype(F32)
    for g in range(8):
        rate_t[pl.ds(g, 16, stride=8), :] = decay_rate[:, g * 128 : (g + 1) * 128] * (-LOG2E)

    def convolve(start, rows):
        for g in range(8):
            cols = pl.ds(g * 128, 128)
            total = conv_bias[:, cols]
            for k in range(4):
                taps = conv_weight[k : k + 1, cols]
                total = total + taps * padded[pl.ds(start + 5 + k, rows), cols]
            conv_out[pl.ds(start, rows), cols] = (total * jax.nn.sigmoid(total)).astype(BF16)

    def channel_sums(start, rows):
        sums = dot_t(conv_out[pl.ds(start, rows), :], x_proj[...])
        blocks = pl.ds(start // 16, rows // 16)
        part[blocks] = sums[:, :512].astype(BF16).reshape(rows // 16, 16, 512)
        own_maps[blocks, :, pl.ds(0, 32)] = sums[:, 512:].reshape(rows // 16, 16, 32)

    convolve(16, 112)

    arrive()
    send(mixer_in.at[pl.ds(112, 16)], rim, h_sem.at[0], h_sem.at[1], ahead)
    channel_sums(16, 112)
    settle(rim, h_sem.at[1])
    keep = jnp.where(ctx > 0, 1.0, 0.0).astype(F32)
    padded[pl.ds(0, 8), :] = rim[pl.ds(0, 16), :].astype(F32)[8:] * keep
    convolve(0, 16)
    channel_sums(0, 16)

    for d in range(1, 8):
        to = lax.rem(exp + d, 8)
        send(part.at[to], parts.at[exp], a_sem.at[0], a_sem.at[1], peer(d))
        send(own_maps.at[to], part_maps.at[exp], a_sem.at[2], a_sem.at[3], peer(d))
    parts[pl.ds(exp, 1)] = part[pl.ds(exp, 1)]
    part_maps[pl.ds(exp, 1)] = own_maps[pl.ds(exp, 1)]
    for i, h in enumerate(halves):
        send(out_proj, opg.at[i, h.q], o_send.at[i], o_recv.at[i, 0], h.two(1))
        send(out_proj, opg.at[i, h.q], o_send.at[i], o_recv.at[i, 1], h.two(-1))
        opg[i, pl.ds(h.q, 1)] = out_proj[...][None]
    settle(parts.at[pl.ds(0, 7)], a_sem.at[1])
    settle(part_maps.at[pl.ds(0, 7)], a_sem.at[3])
    total, total_maps = parts[0].astype(F32), part_maps[0]
    for j in range(1, 8):
        total = total + parts[j].astype(F32)
        total_maps = total_maps + part_maps[j]
    low_rank[pl.ds(exp, 1)] = total.astype(BF16)[None]
    maps[pl.ds(exp, 1)] = total_maps[None]
    for d in range(1, 8):
        for k, ref in enumerate((low_rank, maps)):
            send(ref.at[exp], ref.at[exp], b_sem.at[k], b_sem.at[2 + k], peer(d))
    settle(low_rank.at[pl.ds(0, 7)], b_sem.at[2])
    settle(maps.at[pl.ds(0, 7)], b_sem.at[3])
    scalars = pltpu.make_async_copy(maps, bc_s, l_sem.at[0])
    scalars.start()
    step_low = low_rank[...].reshape(128, 512)
    for j in range(4):
        cols = pl.ds(j * 256, 256)
        raw = dot(step_low, dt_proj[:, cols]) + dt_bias[:, cols]
        step = jnp.maximum(raw, 0.0) + jnp.log1p(jnp.exp(-jnp.abs(raw)))
        drive = step * conv_out[:, cols].astype(F32)
        for i in range(2):
            rows = pl.ds(j * 2 + i, 128, stride=8)
            step_t[rows, :] = step[:, i * 128 : (i + 1) * 128]
            drive_t[rows, :] = drive[:, i * 128 : (i + 1) * 128]
    scalars.wait()
    top, low = pl.ds(0, 512), pl.ds(512, 512)
    for i, h in enumerate(halves):
        for k, d, rows in ((0, 1, top), (1, -1, low)):
            settle(opg.at[0, 0], o_recv.at[i, k])
            place = opg.at[i, wrap(h.q - d, 4), rows]
            send(place, place, o_send.at[i], o_recv.at[i, 2], h.two(d))

    rates = [rate_t[pl.ds(n * 8, 8), :] for n in range(16)]
    zero = jnp.zeros((8, 128), F32)

    def scan_step(t, carry):
        states, running = carry
        rows = pl.ds(pl.multiple_of(t * 8, 8), 8)
        s, d = step_t[rows, :], drive_t[rows, :]
        outs = [zero, zero]
        after = []
        for n in range(16):
            h = jnp.exp2(rates[n] * s) * states[n] + bc_s[t // 16, t % 16, n] * d
            outs[n % 2] = outs[n % 2] + bc_s[t // 16, t % 16, 16 + n] * h
            after.append(h)
        running = running + s
        y_t[rows, :] = outs[0] + outs[1]
        cum_t[rows, :] = running
        return (tuple(after), running)

    states, running = lax.fori_loop(0, 128, scan_step, ((zero,) * 16, zero), unroll=2)

    def exchange(finals, total, fin, sums, place, base, step):
        for n in range(16):
            fin_own[base, pl.ds(n * 8, 8), :] = finals[n].astype(BF16)
        sums[pl.ds(place, 1)] = total[None]
        fin[pl.ds(place, 1)] = fin_own[base][None]
        for d in (1, -1, 2):
            send(fin_own.at[base], fin.at[place], c_send.at[0, base], c_recv.at[0, base], step(d))
            send(sums.at[place], sums.at[place], c_send.at[1, base], c_recv.at[1, base], step(d))
        settle(fin.at[pl.ds(0, 3)], c_recv.at[0, base])
        settle(sums.at[pl.ds(0, 3)], c_recv.at[1, base])

    exchange(states, running, fin_y, sum_y, my, 0, along_y)
    before, row_total = zero, zero
    for v in range(4):
        before = before + jnp.where(v < my, 1.0, 0.0).astype(F32) * sum_y[v]
        row_total = row_total + sum_y[v]
    row_final = []
    for n in range(16):
        entering, whole = zero, zero
        for v in range(4):
            own = fin_y[v, pl.ds(n * 8, 8), :].astype(F32)
            decay = jnp.exp2(rates[n] * sum_y[v])
            entering = jnp.where(v < my, decay * entering + own, entering)
            whole = decay * whole + own
        enter_t[pl.ds(n * 8, 8), :] = entering
        row_final.append(whole)
    exchange(row_final, row_total, fin_x, sum_x, mx, 1, along_x)
    for n in range(16):
        entering = zero
        for u in range(4):
            own = fin_x[u, pl.ds(n * 8, 8), :].astype(F32)
            decay = jnp.exp2(rates[n] * sum_x[u])
            entering = jnp.where(u < mx, decay * entering + own, entering)
        rows = pl.ds(n * 8, 8)
        enter_t[rows, :] = enter_t[rows, :] + jnp.exp2(rates[n] * before) * entering

    def add_entering(t, carry):
        rows = pl.ds(pl.multiple_of(t * 8, 8), 8)
        c = cum_t[rows, :]
        outs = [y_t[rows, :], zero]
        for n in range(16):
            outs[n % 2] = outs[n % 2] + bc_s[t // 16, t % 16, 16 + n] * (jnp.exp2(rates[n] * c) * entered[n])
        y_t[rows, :] = outs[0] + outs[1]
        return carry

    entered = [enter_t[pl.ds(n * 8, 8), :] for n in range(16)]
    for half in range(2):
        lax.fori_loop(half * 64, half * 64 + 64, add_entering, 0, unroll=2)
        rows = pl.ds(half * 64, 64)
        for g in range(8):
            cols = pl.ds(g * 128, 128)
            y = y_t[pl.ds(half * 512 + g, 64, stride=8), :]
            y = y + skip[:, cols] * conv_out[rows, cols].astype(F32)
            z = gate_in[rows, cols].astype(F32)
            block = (y * (z * jax.nn.sigmoid(z))).astype(BF16)
            ga[half, pl.ds(halves[half].p, 1), :, cols] = block[None]
        place = ga.at[half, halves[half].p]
        for k, d in enumerate((1, -1)):
            send(place, place, g_send.at[half], g_recv.at[half, k], halves[half].one(d))

    hops = (0, -1, 1, 2)

    def project(i, k):
        rows = ga[i, wrap(halves[i].p + hops[k], 4)]
        for v in range(4):
            block = dot(rows, opg[i, v]).astype(BF16).reshape(2, 2, 16, 256)
            zs[k, pl.ds(2 * i, 2), :, :, pl.ds(v * 256, 256)] = block

    mz, core = exp // 2, exp % 2

    def pair_group(k):
        sibling = {"exp": 2 * mz + 1 - core}
        send(zs.at[k, :, 1 - core], pair.at[k], p_send.at[0], p_recv.at[k], sibling)

    def scatter_group(k):
        settle(pair.at[0], p_recv.at[k])
        own = zs[k, :, pl.ds(core, 1)].reshape(4, 16, 1024).astype(F32)
        both[k] = (own + pair[k].astype(F32)).astype(BF16)
        for d in (1, 3, 2):
            z = wrap(mz + d, 4)
            send(both.at[k, z], rz.at[k, mz], z_send.at[0], z_recv.at[k], {"exp": 2 * z + core})
        rz[k, pl.ds(mz, 1)] = both[k, pl.ds(mz, 1)]

    second = exp // 4
    place = mx + second * (my - mx)

    def finish_group(k):
        settle(rz.at[0, pl.ds(0, 3)], z_recv.at[k])
        total = rz[k, 0].astype(F32)
        for j in range(1, 4):
            total = total + rz[k, j].astype(F32)
        d = hops[k]
        if d == 0:
            mo[pl.ds(place, 1)] = total.astype(BF16)[None]
        else:
            ms[k - 1] = total.astype(BF16)
            near_x, near_y = along_x(d)["ctx"], along_y(d)["ctx"]
            device = {"ctx": near_x + second * (near_y - near_x)}
            send(ms.at[k - 1], mo.at[place], m_sem.at[0], m_sem.at[1], device)

    top, low = pl.ds(0, 32), pl.ds(32, 32)
    for i in range(2):
        settle(opg.at[0, 0], o_recv.at[i, 2])
        project(i, 0)
    pair_group(0)
    for i, h in enumerate(halves):
        for k, d, rows in ((0, 1, top), (1, -1, low)):
            settle(ga.at[0, 0], g_recv.at[i, k])
            block = ga.at[i, wrap(h.p - d, 4), rows]
            send(block, block, g_send.at[i], g_recv.at[i, 2], h.one(d))
    scatter_group(0)
    for k in (1, 2):
        project(0, k)
        project(1, k)
        pair_group(k)
    scatter_group(1)
    scatter_group(2)
    for i in range(2):
        settle(ga.at[0, 0], g_recv.at[i, 2])
        project(i, 3)
    pair_group(3)
    finish_group(0)
    scatter_group(3)
    for k in (1, 2, 3):
        finish_group(k)
    settle(mo.at[pl.ds(0, 3)], m_sem.at[1])

    squares = jnp.zeros((16, 1), F32)
    for u in range(4):
        cols = pl.ds(u * 1024, 1024)
        across = [mo[v, :, pl.ds(u * 256, 256)] for v in range(4)]
        mixed = jnp.where(second == 0, mo[u].astype(F32), jnp.concatenate(across, 1).astype(F32))
        rows = residual[:, cols].astype(F32) + mixed
        stream[:, cols] = rows
        squares = squares + jnp.sum(rows * rows, axis=1, keepdims=True)
    scale = lax.rsqrt(squares * (1.0 / 4096.0) + 1e-06)
    logits = jnp.zeros((8, 16), F32)
    for u in range(4):
        cols = pl.ds(u * 1024, 1024)
        rows = (stream[:, cols] * scale * gain[:, cols]).astype(BF16)
        normed[:, cols] = rows
        logits = logits + dot_t(router[:, cols], rows)
    ids = expert_ids[...]
    lanes = lax.broadcasted_iota(jnp.int32, (8, 16), 0)
    signs = jnp.where(ids[0:1] == lanes, 1.0, 0.0) - jnp.where(ids[1:2] == lanes, 1.0, 0.0)
    first = jax.nn.sigmoid(jnp.sum(logits * signs, axis=0, keepdims=True))

    def drain():
        settle(rim, h_sem.at[0])
        for i in range(2):
            settle(opg.at[0, pl.ds(0, 3)], o_send.at[i])
            settle(ga.at[0, pl.ds(0, 3)], g_send.at[i])
        settle(parts.at[pl.ds(0, 7)], a_sem.at[0])
        settle(part_maps.at[pl.ds(0, 7)], a_sem.at[2])
        settle(low_rank.at[pl.ds(0, 7)], b_sem.at[0])
        settle(maps.at[pl.ds(0, 7)], b_sem.at[1])
        for base, (fin, sums) in enumerate(((fin_y, sum_y), (fin_x, sum_x))):
            settle(fin.at[pl.ds(0, 3)], c_send.at[0, base])
            settle(sums.at[pl.ds(0, 3)], c_send.at[1, base])
        settle(pair, p_send.at[0])
        settle(rz.at[:, pl.ds(0, 3)], z_send.at[0])
        settle(mo.at[pl.ds(0, 3)], m_sem.at[0])

    return first, drain


def experts(r, gate_row, drain, out, exp, mx, my, halves, loads):
    pick = r.pick
    result = r.result
    e_sem = r.e_sem
    stream = r.stream
    normed = r.normed
    spread = r.spread
    fetch = r.fetch
    go = r.go
    rcv = r.rcv
    rback = r.rback
    xa = r.xa
    xb = r.xb
    wgu = r.wgu
    wd = r.wd
    lhs = r.lhs
    lhs_down = r.lhs_down
    acc = r.acc
    hid = r.hid
    oa = r.oa
    ob = r.ob
    far = r.far
    near = r.near
    tot = r.tot
    far2 = r.far2
    near2 = r.near2
    d_send = r.d_send
    d_recv = r.d_recv
    u_send = r.u_send
    u_recv = r.u_recv
    s_send = r.s_send
    s_recv = r.s_recv
    r_send = r.r_send
    r_recv = r.r_recv
    xs, os = (xa, xb), (oa, ob)
    lo, hi = pl.ds(0, 1024), pl.ds(1024, 1024)
    every = slice(None)

    windows = (0, 768, 1280)

    def all_to_all(half, into, ss, rs):
        for d in range(1, 8):
            peer = lax.rem(exp + d, 8)
            src, dst = go.at[half, peer], into.at[half, exp]
            remote(src, dst, ss.at[half], rs.at[half], {"exp": peer}).start()
        into[half, pl.ds(exp, 1)] = go[half, pl.ds(exp, 1)]

    for i in range(2):
        packed = jnp.zeros((128, 768), F32)
        for k, w in enumerate(windows):
            packed = packed + dot(spread[k], normed[:, pl.ds(i * 2048 + w, 768)])
        go[i] = packed.astype(BF16).reshape(8, 16, 768)
        all_to_all(i, rcv, d_send, d_recv)
    acc[...] = jnp.zeros_like(acc)

    def push(i, at, cols, ss, rs, device):
        place = xs[i].at[at + (every, cols)] if cols is not None else xs[i].at[at]
        remote(place, place, u_send.at[i, ss], u_recv.at[i, rs], device).start()

    steps = [[wrap(h.p + d, 4) for d in (0, -1, 1, 2)] for h in halves]

    def second_start(i, g):
        h = halves[i]
        at = h.unit(steps[i][g], h.q)
        push(i, at, None, 1, 3 + g, h.two(1))
        push(i, at, None, 1, 3 + g, h.two(-1))

    def second_pass(i, g):
        h, u = halves[i], steps[i][g]
        settle(xs[i].at[0, pl.ds(0, 2)], u_recv.at[i, 3 + g])
        push(i, h.unit(u, wrap(h.q - 1, 4)), lo, 2, 7, h.two(1))
        push(i, h.unit(u, wrap(h.q + 1, 4)), hi, 2, 7, h.two(-1))

    for i, (h, x) in enumerate(zip(halves, xs)):
        settle(rcv.at[i, pl.ds(0, 7)], d_recv.at[i])
        flat = rcv[i].reshape(128, 768)
        for k, w in enumerate(windows):
            block = dot(pick[k], flat).astype(BF16)[None, None]
            x[pl.ds(mx, 1), pl.ds(my, 1), :, pl.ds(w, 768)] = block
        at = h.unit(h.p, h.q)
        push(i, at, None, 0, 0, h.one(1))
        push(i, at, None, 0, 1, h.one(-1))
        if i == 0:
            second_start(0, 0)
    for i, (h, x) in enumerate(zip(halves, xs)):
        settle(x.at[0, 0], u_recv.at[i, 0])
        push(i, h.unit(steps[i][1], h.q), lo, 0, 2, h.one(1))
        settle(x.at[0, 0], u_recv.at[i, 1])
        push(i, h.unit(steps[i][2], h.q), hi, 0, 2, h.one(-1))
        if i == 0:
            second_start(1, 0)
    second_start(0, 1)
    second_start(1, 1)
    for i in range(2):
        settle(xs[i].at[0, 0], u_recv.at[i, 2])
        second_start(i, 2)
        second_start(i, 3)

    def gate_up(i, units):
        for n, at in enumerate(units):
            lhs[n] = xs[i][at]
        for j in range(6):
            cols = pl.ds(j * 256, 256)
            part = dot(lhs[...].reshape(160, 2048), wgu[pl.ds(i * 2048, 2048), cols])
            for n, at in enumerate(units):
                place = at + (every, cols)
                acc[place] = acc[place] + part[n * 40 : (n + 1) * 40]

    def line(i, v):
        return [halves[i].unit(u, v) for u in steps[i]]

    def beside(i, gs):
        h = halves[i]
        return [h.unit(steps[i][g], wrap(h.q + d, 4)) for g in gs for d in (-1, 1)]

    loads[0].wait()
    loads[1].wait()
    gate_up(0, line(0, halves[0].q))
    second_pass(0, 0)
    second_pass(1, 0)
    gate_up(1, line(1, halves[1].q))
    second_pass(0, 1)
    second_pass(1, 1)
    gate_up(0, beside(0, (0, 1)))
    second_pass(0, 2)
    second_pass(1, 2)
    gate_up(1, beside(1, (0, 1)))
    second_pass(0, 3)
    second_pass(1, 3)
    gate_up(0, beside(0, (2, 3)))
    gate_up(1, beside(1, (2, 3)))

    def activate(units):
        for at in units:
            gate = acc[at + (every, pl.ds(0, 768))]
            up = acc[at + (every, pl.ds(768, 768))]
            hid[at] = (gate * jax.nn.sigmoid(gate) * up).astype(BF16)

    def down(i, units):
        count = len(units)
        for n, at in enumerate(units):
            lhs_down[n] = hid[at]
        for j in range(8):
            cols = pl.ds(j * 256, 256)
            rows = lhs_down[pl.ds(0, count)].reshape(count * 40, 768)
            part = dot(rows, wd[:, pl.ds(i * 2048 + j * 256, 256)]).astype(BF16)
            for n, at in enumerate(units):
                os[i][at + (every, cols)] = part[n * 40 : (n + 1) * 40]

    def send(src, dst, i, ss, rs, device):
        remote(src, dst, s_send.at[i, ss], s_recv.at[i, rs], device).start()

    def add_into(ref, at, other, other_at):
        ref[at] = (ref[at].astype(F32) + other[other_at].astype(F32)).astype(BF16)

    order = [[wrap(h.p + d, 4) for d in (2, 1, -1, 0)] for h in halves]

    def send_near(i, ks):
        h = halves[i]
        sides = ((wrap(h.q + 1, 4), 1, hi, 0), (wrap(h.q - 1, 4), -1, lo, 1))
        down(i, [h.unit(order[i][k], v) for v, _, _, _ in sides for k in ks])
        for v, d, cols, b in sides:
            for k in ks:
                u = order[i][k]
                src, dst = os[i].at[h.unit(u, v) + (every, cols)], near.at[i, b, u, :, cols]
                send(src, dst, i, 0, 4, h.two(d))

    xx, yy = [wrap(mx + d, 4) for d in (0, 1, -1)], [wrap(my + d, 4) for d in (0, 1, -1)]
    activate([(u, v) for u in xx for v in yy])
    loads[2].wait()
    for i in range(2):
        send_near(i, (1, 2, 3))
    for i, h in enumerate(halves):
        settle(xs[i].at[0], u_recv.at[i, 7])
        gate_up(i, line(i, wrap(h.q + 2, 4)))
    fx, fy = wrap(mx + 2, 4), wrap(my + 2, 4)
    activate([(fx, v) for v in yy] + [(u, fy) for u in xx] + [(fx, fy)])
    for i, h in enumerate(halves):
        v = wrap(h.q + 2, 4)
        down(i, [h.unit(u, v) for u in order[i]])
        for k, u in enumerate(order[i]):
            at = h.unit(u, v)
            send(os[i].at[at + (every, lo)], far.at[i, 0, u], i, 0, k, h.two(1))
            send(os[i].at[at + (every, hi)], far.at[i, 1, u], i, 0, k, h.two(-1))
    for i in range(2):
        send_near(i, (0,))
    down(0, line(0, halves[0].q))
    for k in range(4):
        for i, h in enumerate(halves):
            u = order[i][k]
            settle(xs[i].at[0, 0], s_recv.at[i, k])
            for b, d, cols in ((0, 1, lo), (1, -1, hi)):
                at = h.unit(u, wrap(h.q + d, 4)) + (every, cols)
                add_into(os[i], at, far, (i, b, u))
                send(os[i].at[at], near.at[i, b, u, :, cols], i, 0, 5 + k, h.two(d))
    down(1, line(1, halves[1].q))
    for i in range(2):
        settle(xs[i].at[0], s_recv.at[i, 4])
    for k in range(4):
        for i, h in enumerate(halves):
            u = order[i][k]
            settle(xs[i].at[0, 0], s_recv.at[i, 5 + k])
            mine = os[i][h.unit(u, h.q)].astype(F32)
            mine = mine + near[i, 0, u].astype(F32) + near[i, 1, u].astype(F32)
            tot[i, u] = mine.astype(BF16)
            if k == 0:
                send(tot.at[i, u, :, lo], far2.at[i, 0], i, 1, 9, h.one(1))
                send(tot.at[i, u, :, hi], far2.at[i, 1], i, 1, 9, h.one(-1))
            if k == 1:
                send(tot.at[i, u, :, hi], near2.at[i, 0, :, hi], i, 1, 10, h.one(1))
            if k == 2:
                send(tot.at[i, u, :, lo], near2.at[i, 1, :, lo], i, 1, 10, h.one(-1))
    for i, h in enumerate(halves):
        settle(xs[i].at[0, 0], s_recv.at[i, 9])
        for b, d, cols in ((0, 1, lo), (1, -1, hi)):
            u = order[i][1 + b]
            add_into(tot, (i, u, every, cols), far2, (i, b))
            send(tot.at[i, u, :, cols], near2.at[i, b, :, cols], i, 1, 10, h.one(d))

    across = (((0,), (0,)), ((), ()))
    for i, h in enumerate(halves):
        settle(xs[i].at[0, pl.ds(0, 2)], s_recv.at[i, 10])
        final = tot[i, h.p].astype(F32) + near2[i, 0].astype(F32) + near2[i, 1].astype(F32)
        final = final.astype(BF16)
        back = jnp.zeros((128, 768), F32)
        for k, w in enumerate(windows):
            block = final[:, w : w + 768]
            back = back + lax.dot_general(pick[k], block, across, preferred_element_type=F32)
        settle(rcv.at[i, pl.ds(0, 7)], d_send.at[i])
        go[i] = back.astype(BF16).reshape(8, 16, 768)
        all_to_all(i, rback, r_send, r_recv)
    eye = lax.broadcasted_iota(jnp.int32, (16, 16), 0) == lax.broadcasted_iota(
        jnp.int32, (16, 16), 1
    )
    gate = jnp.sum(jnp.where(eye, jnp.broadcast_to(gate_row, (16, 16)), 0.0), axis=1, keepdims=True)
    stores = []
    for i in range(2):
        settle(rback.at[i, pl.ds(0, 7)], r_recv.at[i])
        flat = rback[i].reshape(128, 768)
        for j, w in enumerate(windows):
            cols = pl.ds(i * 2048 + w, 768)
            pair = [
                lax.dot_general(fetch[j, k], flat, across, preferred_element_type=F32)
                for k in range(2)
            ]
            mix = gate * pair[0] + (1.0 - gate) * pair[1]
            result[:, cols] = (stream[:, cols] + mix).astype(BF16)
        cols = pl.ds(i * 2048, 2048)
        stores.append(pltpu.make_async_copy(result.at[:, cols], out.at[:, cols], e_sem.at[i]))
        stores[i].start()
    drain()
    for i in range(2):
        settle(rback.at[i, pl.ds(0, 7)], r_send.at[i])
        settle(xs[i].at[0, pl.ds(0, 3)], u_send.at[i, 0])
        settle(xs[i].at[pl.ds(0, 2)], u_send.at[i, 1])
        settle(xs[i].at[0], u_send.at[i, 2])
        settle(xs[i].at[pl.ds(0, 3)], s_send.at[i, 0])
        settle(xs[i].at[0, pl.ds(0, 3)], s_send.at[i, 1])
    for c in stores:
        c.wait()


def token_places(ids, spread, fetch):
    experts_of = lax.broadcasted_iota(jnp.int32, (8, 16), 0)
    hits = [ids[k : k + 1] == experts_of for k in range(2)]
    either = jnp.where(hits[0] | hits[1], 1.0, 0.0).astype(BF16)
    before = lax.broadcasted_iota(jnp.int32, (16, 16), 0) < lax.broadcasted_iota(
        jnp.int32, (16, 16), 1
    )
    earlier = dot(either, jnp.where(before, 1.0, 0.0).astype(BF16))
    rows = lax.broadcasted_iota(jnp.int32, (128, 16), 0).astype(F32)
    for j in range(3):
        found = []
        for k in range(2):
            slot = jnp.sum(jnp.where(hits[k], earlier, 0.0), axis=0, keepdims=True)
            place = ids[k : k + 1].astype(F32) * 16.0 + slot + j * 5.0
            found.append(jnp.where(rows == place, 1.0, 0.0))
            fetch[j, k] = found[k].astype(BF16)
        spread[j] = (found[0] + found[1]).astype(BF16)


def block_kernel(*refs):
    names = INPUTS + ("out",) + tuple(SCRATCH)
    r = types.SimpleNamespace(**dict(zip(names, refs, strict=True)))
    ctx, exp = lax.axis_index("ctx"), lax.axis_index("exp")
    mx, my = ctx // 4, ctx % 4
    halves = (Half(0, mx, my), Half(1, mx, my))
    wgu, wd, w_sem = r.wgu, r.wd, r.w_sem
    loads = [
        pltpu.make_async_copy(r.w_gate.at[0], wgu.at[:, pl.ds(0, 768)], w_sem.at[0]),
        pltpu.make_async_copy(r.w_up.at[0], wgu.at[:, pl.ds(768, 768)], w_sem.at[1]),
        pltpu.make_async_copy(r.w_down.at[0], wd, w_sem.at[2]),
    ]
    for load in loads:
        load.start()
    arrive = greet(
        [{"ctx": lax.rem(ctx + 15, 16)}, {"ctx": lax.rem(ctx + 1, 16)}]
        + [h.one(d) for h in halves for d in (1, 2, -1)]
        + [{"exp": lax.rem(exp + d, 8)} for d in range(1, 8)]
    )
    token_places(r.expert_ids[...], r.spread, r.fetch)
    gate_row, drain = mixer(r, ctx, exp, mx, my, halves, arrive)
    experts(r, gate_row, drain, r.out, exp, mx, my, halves, loads)


def shards(
    mixer_in,
    gate_in,
    conv_weight,
    conv_bias,
    x_proj,
    dt_proj,
    dt_bias,
    decay_rate,
    skip,
    out_proj,
    residual,
    gain,
    router,
    w_gate,
    w_up,
    w_down,
    expert_ids,
):
    pick = np.zeros((3, 40, 128), np.float32)
    for w in range(3):
        for j in range(8):
            for s in range(5):
                pick[w, j * 5 + s, j * 16 + w * 5 + s] = 1.0
    vmem = pl.BlockSpec(memory_space=pltpu.VMEM)
    anywhere = pl.BlockSpec(memory_space=pl.ANY)
    return pl.pallas_call(
        block_kernel,
        out_shape=jax.ShapeDtypeStruct((16, 4096), BF16),
        in_specs=[anywhere if name.startswith("w_") else vmem for name in INPUTS],
        out_specs=anywhere,
        scratch_shapes=list(SCRATCH.values()),
        compiler_params=pltpu.CompilerParams(
            collective_id=0, has_side_effects=True, vmem_limit_bytes=VMEM_LIMIT
        ),
        cost_estimate=pl.CostEstimate(
            flops=13_500_000_000, bytes_accessed=24_000_000, transcendentals=0
        ),
    )(
        mixer_in,
        gate_in,
        conv_weight,
        conv_bias[None],
        x_proj.T,
        dt_proj,
        dt_bias[None],
        decay_rate,
        skip[None],
        out_proj,
        residual,
        gain[None],
        router.T,
        expert_ids.T,
        w_gate,
        w_up,
        w_down,
        jnp.asarray(pick, BF16),
    )


def solution(mesh):
    in_specs = (
        P("ctx", "exp"),
        P("ctx", "exp"),
        P(None, "exp"),
        P("exp"),
        P("exp", None),
        P(None, "exp"),
        P("exp"),
        P(None, "exp"),
        P("exp"),
        P("exp", "ctx"),
        P(("ctx", "exp"), None),
        P(),
        P(),
        P("exp", None, "ctx"),
        P("exp", None, "ctx"),
        P("exp", "ctx", None),
        P(("ctx", "exp"), None),
    )
    out_specs = P(("ctx", "exp"), None)
    return jax.shard_map(shards, mesh=mesh, in_specs=in_specs, out_specs=out_specs, check_vma=False)
```

```python
import types

import jax
import jax.numpy as jnp
import numpy as np
from jax import lax
from jax.experimental import pallas as pl
from jax.experimental.pallas import tpu as pltpu
from jax.sharding import PartitionSpec as P

F32 = jnp.float32
BF16 = jnp.bfloat16
VMEM_LIMIT = 60 * 1024 * 1024


def remote(src, dst, send_sem, recv_sem, device):
    return pltpu.make_async_remote_copy(
        src_ref=src,
        dst_ref=dst,
        send_sem=send_sem,
        recv_sem=recv_sem,
        device_id=device,
        device_id_type=pl.DeviceIdType.MESH,
    )


def greet(devices):
    barrier = pltpu.get_barrier_semaphore()
    for device in devices:
        pl.semaphore_signal(barrier, inc=1, device_id=device, device_id_type=pl.DeviceIdType.MESH)
    return lambda: pl.semaphore_wait(barrier, len(devices))


def settle(view, sem):
    pltpu.make_async_copy(view, view, sem).wait()


def wrap(index, count):
    return lax.rem(index + count, count)


def dot(a, b):
    return jnp.dot(a, b, preferred_element_type=F32)


def dot_t(a, b):
    return lax.dot_general(a, b, (((1,), (1,)), ((), ())), preferred_element_type=F32)


class Half:
    def __init__(self, half, mx, my):
        self.half = half
        self.mx, self.my = mx, my
        self.p, self.q = (mx, my) if half == 0 else (my, mx)

    def one(self, step):
        p = wrap(self.p + step, 4)
        return {"ctx": p * 4 + self.my if self.half == 0 else self.mx * 4 + p}

    def two(self, step):
        q = wrap(self.q + step, 4)
        return {"ctx": self.mx * 4 + q if self.half == 0 else q * 4 + self.my}

    def unit(self, u, v):
        return (u, v) if self.half == 0 else (v, u)

    def group(self, v):
        return (slice(None), v) if self.half == 0 else (v, slice(None))


LOG2E = 1.4426950408889634
FAR_FIRST = (4, 3, 5, 2, 6, 1, 7)

INPUTS = (
    "mixer_in",
    "gate_in",
    "conv_weight",
    "conv_bias",
    "x_proj",
    "dt_proj",
    "dt_bias",
    "decay_rate",
    "skip",
    "out_proj",
    "residual",
    "gain",
    "router",
    "expert_ids",
    "w_gate",
    "w_up",
    "w_down",
    "pick",
)

SCRATCH = dict(
    stream=pltpu.VMEM((16, 4096), F32),
    result=pltpu.VMEM((16, 4096), F32),
    e_sem=pltpu.SemaphoreType.DMA((2,)),
    normed=pltpu.VMEM((16, 4096), BF16),
    spread=pltpu.VMEM((3, 128, 16), BF16),
    fetch=pltpu.VMEM((3, 2, 128, 16), BF16),
    rim=pltpu.VMEM((16, 1024), BF16),
    padded=pltpu.VMEM((136, 1024), F32),
    conv_out=pltpu.VMEM((128, 1024), BF16),
    part=pltpu.VMEM((8, 16, 512), BF16),
    own_maps=pltpu.VMEM((8, 16, 128), F32),
    part_maps=pltpu.VMEM((8, 16, 128), F32),
    parts=pltpu.VMEM((8, 16, 512), BF16),
    low_rank=pltpu.VMEM((8, 16, 512), BF16),
    maps=pltpu.VMEM((8, 16, 128), F32),
    bc_s=pltpu.SMEM((8, 16, 128), F32),
    step_t=pltpu.VMEM((1024, 128), F32),
    drive_t=pltpu.VMEM((1024, 128), F32),
    cum_t=pltpu.VMEM((1024, 128), F32),
    y_t=pltpu.VMEM((1024, 128), F32),
    rate_t=pltpu.VMEM((128, 128), F32),
    enter_t=pltpu.VMEM((128, 128), F32),
    fin_own=pltpu.VMEM((2, 128, 128), BF16),
    fin_y=pltpu.VMEM((4, 128, 128), BF16),
    sum_y=pltpu.VMEM((4, 8, 128), F32),
    fin_x=pltpu.VMEM((4, 128, 128), BF16),
    sum_x=pltpu.VMEM((4, 8, 128), F32),
    opg=pltpu.VMEM((2, 4, 1024, 256), BF16),
    ga=pltpu.VMEM((2, 4, 64, 1024), BF16),
    zs=pltpu.VMEM((4, 4, 2, 16, 1024), BF16),
    pair=pltpu.VMEM((4, 4, 16, 1024), BF16),
    both=pltpu.VMEM((4, 4, 16, 1024), BF16),
    p_send=pltpu.SemaphoreType.DMA((1,)),
    p_recv=pltpu.SemaphoreType.DMA((4,)),
    rz=pltpu.VMEM((4, 4, 16, 1024), BF16),
    ms=pltpu.VMEM((3, 16, 1024), BF16),
    mo=pltpu.VMEM((4, 16, 1024), BF16),
    h_sem=pltpu.SemaphoreType.DMA((2,)),
    a_sem=pltpu.SemaphoreType.DMA((4,)),
    b_sem=pltpu.SemaphoreType.DMA((4,)),
    o_send=pltpu.SemaphoreType.DMA((2,)),
    o_recv=pltpu.SemaphoreType.DMA((2, 3)),
    c_send=pltpu.SemaphoreType.DMA((2, 2)),
    c_recv=pltpu.SemaphoreType.DMA((2, 2)),
    g_send=pltpu.SemaphoreType.DMA((2,)),
    g_recv=pltpu.SemaphoreType.DMA((2, 3)),
    z_send=pltpu.SemaphoreType.DMA((1,)),
    z_recv=pltpu.SemaphoreType.DMA((4,)),
    m_sem=pltpu.SemaphoreType.DMA((2,)),
    l_sem=pltpu.SemaphoreType.DMA((1,)),
    go=pltpu.VMEM((2, 8, 16, 768), BF16),
    rcv=pltpu.VMEM((2, 8, 16, 768), BF16),
    rback=pltpu.VMEM((2, 8, 16, 768), BF16),
    xa=pltpu.VMEM((4, 4, 40, 2048), BF16),
    xb=pltpu.VMEM((4, 4, 40, 2048), BF16),
    wgu=pltpu.VMEM((4096, 1536), BF16),
    wd=pltpu.VMEM((768, 4096), BF16),
    lhs=pltpu.VMEM((4, 40, 2048), BF16),
    lhs_down=pltpu.VMEM((6, 40, 768), BF16),
    acc=pltpu.VMEM((4, 4, 40, 1536), F32),
    hid=pltpu.VMEM((4, 4, 40, 768), BF16),
    oa=pltpu.VMEM((4, 4, 40, 2048), BF16),
    ob=pltpu.VMEM((4, 4, 40, 2048), BF16),
    far=pltpu.VMEM((2, 2, 4, 40, 1024), BF16),
    near=pltpu.VMEM((2, 2, 4, 40, 2048), BF16),
    tot=pltpu.VMEM((2, 4, 40, 2048), BF16),
    far2=pltpu.VMEM((2, 2, 40, 1024), BF16),
    near2=pltpu.VMEM((2, 2, 40, 2048), BF16),
    w_sem=pltpu.SemaphoreType.DMA((3,)),
    d_send=pltpu.SemaphoreType.DMA((2,)),
    d_recv=pltpu.SemaphoreType.DMA((2,)),
    u_send=pltpu.SemaphoreType.DMA((2, 3)),
    u_recv=pltpu.SemaphoreType.DMA((2, 8)),
    s_send=pltpu.SemaphoreType.DMA((2, 2)),
    s_recv=pltpu.SemaphoreType.DMA((2, 11)),
    r_send=pltpu.SemaphoreType.DMA((2,)),
    r_recv=pltpu.SemaphoreType.DMA((2,)),
)


def mixer(r, ctx, exp, mx, my, halves, arrive):
    mixer_in = r.mixer_in
    gate_in = r.gate_in
    conv_weight = r.conv_weight
    conv_bias = r.conv_bias
    x_proj = r.x_proj
    dt_proj = r.dt_proj
    dt_bias = r.dt_bias
    decay_rate = r.decay_rate
    skip = r.skip
    out_proj = r.out_proj
    residual = r.residual
    gain = r.gain
    router = r.router
    expert_ids = r.expert_ids
    stream = r.stream
    normed = r.normed
    rim = r.rim
    padded = r.padded
    conv_out = r.conv_out
    part = r.part
    own_maps = r.own_maps
    part_maps = r.part_maps
    parts = r.parts
    low_rank = r.low_rank
    maps = r.maps
    bc_s = r.bc_s
    step_t = r.step_t
    drive_t = r.drive_t
    cum_t = r.cum_t
    y_t = r.y_t
    rate_t = r.rate_t
    enter_t = r.enter_t
    fin_own = r.fin_own
    fin_y = r.fin_y
    sum_y = r.sum_y
    fin_x = r.fin_x
    sum_x = r.sum_x
    opg = r.opg
    ga = r.ga
    zs = r.zs
    pair = r.pair
    both = r.both
    p_send = r.p_send
    p_recv = r.p_recv
    rz = r.rz
    ms = r.ms
    mo = r.mo
    h_sem = r.h_sem
    a_sem = r.a_sem
    b_sem = r.b_sem
    o_send = r.o_send
    o_recv = r.o_recv
    c_send = r.c_send
    c_recv = r.c_recv
    g_send = r.g_send
    g_recv = r.g_recv
    z_send = r.z_send
    z_recv = r.z_recv
    m_sem = r.m_sem
    l_sem = r.l_sem
    every = slice(None)

    def along_x(d):
        return {"ctx": wrap(mx + d, 4) * 4 + my}

    def along_y(d):
        return {"ctx": mx * 4 + wrap(my + d, 4)}

    def peer(d):
        return {"exp": lax.rem(exp + d, 8)}

    ahead = {"ctx": lax.rem(ctx + 1, 16)}

    def send(src, dst, ss, rs, device):
        remote(src, dst, ss, rs, device).start()

    own_maps[...] = jnp.zeros_like(own_maps)
    padded[pl.ds(8, 128), :] = mixer_in[...].astype(F32)
    for g in range(8):
        rate_t[pl.ds(g, 16, stride=8), :] = decay_rate[:, g * 128 : (g + 1) * 128] * (-LOG2E)

    def convolve(start, rows):
        for g in range(8):
            cols = pl.ds(g * 128, 128)
            total = conv_bias[:, cols]
            for k in range(4):
                taps = conv_weight[k : k + 1, cols]
                total = total + taps * padded[pl.ds(start + 5 + k, rows), cols]
            conv_out[pl.ds(start, rows), cols] = (total * jax.nn.sigmoid(total)).astype(BF16)

    def channel_sums(start, rows):
        sums = dot_t(conv_out[pl.ds(start, rows), :], x_proj[...])
        blocks = pl.ds(start // 16, rows // 16)
        part[blocks] = sums[:, :512].astype(BF16).reshape(rows // 16, 16, 512)
        own_maps[blocks, :, pl.ds(0, 32)] = sums[:, 512:].reshape(rows // 16, 16, 32)

    convolve(16, 112)

    arrive()
    send(mixer_in.at[pl.ds(112, 16)], rim, h_sem.at[0], h_sem.at[1], ahead)
    for i, h in enumerate(halves):
        send(out_proj, opg.at[i, h.q], o_send.at[i], o_recv.at[i, 0], h.two(1))
        send(out_proj, opg.at[i, h.q], o_send.at[i], o_recv.at[i, 1], h.two(-1))
        opg[i, pl.ds(h.q, 1)] = out_proj[...][None]
    channel_sums(16, 112)
    settle(rim, h_sem.at[1])
    keep = jnp.where(ctx > 0, 1.0, 0.0).astype(F32)
    padded[pl.ds(0, 8), :] = rim[pl.ds(0, 16), :].astype(F32)[8:] * keep
    convolve(0, 16)
    channel_sums(0, 16)

    for d in FAR_FIRST:
        to = lax.rem(exp + d, 8)
        send(part.at[to], parts.at[exp], a_sem.at[0], a_sem.at[1], peer(d))
        send(own_maps.at[to], part_maps.at[exp], a_sem.at[2], a_sem.at[3], peer(d))
    parts[pl.ds(exp, 1)] = part[pl.ds(exp, 1)]
    part_maps[pl.ds(exp, 1)] = own_maps[pl.ds(exp, 1)]
    settle(parts.at[pl.ds(0, 7)], a_sem.at[1])
    settle(part_maps.at[pl.ds(0, 7)], a_sem.at[3])
    total, total_maps = parts[0].astype(F32), part_maps[0]
    for j in range(1, 8):
        total = total + parts[j].astype(F32)
        total_maps = total_maps + part_maps[j]
    low_rank[pl.ds(exp, 1)] = total.astype(BF16)[None]
    maps[pl.ds(exp, 1)] = total_maps[None]
    for d in FAR_FIRST:
        for k, ref in enumerate((low_rank, maps)):
            send(ref.at[exp], ref.at[exp], b_sem.at[k], b_sem.at[2 + k], peer(d))
    settle(low_rank.at[pl.ds(0, 7)], b_sem.at[2])
    settle(maps.at[pl.ds(0, 7)], b_sem.at[3])
    top, low = pl.ds(0, 512), pl.ds(512, 512)
    for i, h in enumerate(halves):
        for k, d, rows in ((0, 1, top), (1, -1, low)):
            settle(opg.at[0, 0], o_recv.at[i, k])
            place = opg.at[i, wrap(h.q - d, 4), rows]
            send(place, place, o_send.at[i], o_recv.at[i, 2], h.two(d))
    scalars = pltpu.make_async_copy(maps, bc_s, l_sem.at[0])
    scalars.start()
    step_low = low_rank[...].reshape(128, 512)
    for j in range(4):
        cols = pl.ds(j * 256, 256)
        raw = dot(step_low, dt_proj[:, cols]) + dt_bias[:, cols]
        step = jnp.maximum(raw, 0.0) + jnp.log1p(jnp.exp(-jnp.abs(raw)))
        drive = step * conv_out[:, cols].astype(F32)
        for i in range(2):
            rows = pl.ds(j * 2 + i, 128, stride=8)
            step_t[rows, :] = step[:, i * 128 : (i + 1) * 128]
            drive_t[rows, :] = drive[:, i * 128 : (i + 1) * 128]
    scalars.wait()

    rates = [rate_t[pl.ds(n * 8, 8), :] for n in range(16)]
    zero = jnp.zeros((8, 128), F32)

    def scan_step(t, carry):
        states, running = carry
        rows = pl.ds(pl.multiple_of(t * 8, 8), 8)
        s, d = step_t[rows, :], drive_t[rows, :]
        outs = [zero, zero]
        after = []
        for n in range(16):
            h = jnp.exp2(rates[n] * s) * states[n] + bc_s[t // 16, t % 16, n] * d
            outs[n % 2] = outs[n % 2] + bc_s[t // 16, t % 16, 16 + n] * h
            after.append(h)
        running = running + s
        y_t[rows, :] = outs[0] + outs[1]
        cum_t[rows, :] = running
        return (tuple(after), running)

    states, running = lax.fori_loop(0, 128, scan_step, ((zero,) * 16, zero), unroll=2)

    def exchange(finals, total, fin, sums, place, base, step):
        for n in range(16):
            fin_own[base, pl.ds(n * 8, 8), :] = finals[n].astype(BF16)
        sums[pl.ds(place, 1)] = total[None]
        fin[pl.ds(place, 1)] = fin_own[base][None]
        for d in (1, -1, 2):
            send(fin_own.at[base], fin.at[place], c_send.at[0, base], c_recv.at[0, base], step(d))
            send(sums.at[place], sums.at[place], c_send.at[1, base], c_recv.at[1, base], step(d))
        settle(fin.at[pl.ds(0, 3)], c_recv.at[0, base])
        settle(sums.at[pl.ds(0, 3)], c_recv.at[1, base])

    exchange(states, running, fin_y, sum_y, my, 0, along_y)
    before, row_total = zero, zero
    for v in range(4):
        before = before + jnp.where(v < my, 1.0, 0.0).astype(F32) * sum_y[v]
        row_total = row_total + sum_y[v]
    row_final = []
    for n in range(16):
        entering, whole = zero, zero
        for v in range(4):
            own = fin_y[v, pl.ds(n * 8, 8), :].astype(F32)
            decay = jnp.exp2(rates[n] * sum_y[v])
            entering = jnp.where(v < my, decay * entering + own, entering)
            whole = decay * whole + own
        enter_t[pl.ds(n * 8, 8), :] = entering
        row_final.append(whole)
    exchange(row_final, row_total, fin_x, sum_x, mx, 1, along_x)
    for n in range(16):
        entering = zero
        for u in range(4):
            own = fin_x[u, pl.ds(n * 8, 8), :].astype(F32)
            decay = jnp.exp2(rates[n] * sum_x[u])
            entering = jnp.where(u < mx, decay * entering + own, entering)
        rows = pl.ds(n * 8, 8)
        enter_t[rows, :] = enter_t[rows, :] + jnp.exp2(rates[n] * before) * entering

    def add_entering(t, carry):
        rows = pl.ds(pl.multiple_of(t * 8, 8), 8)
        c = cum_t[rows, :]
        outs = [y_t[rows, :], zero]
        for n in range(16):
            outs[n % 2] = outs[n % 2] + bc_s[t // 16, t % 16, 16 + n] * (jnp.exp2(rates[n] * c) * entered[n])
        y_t[rows, :] = outs[0] + outs[1]
        return carry

    entered = [enter_t[pl.ds(n * 8, 8), :] for n in range(16)]
    for half in range(2):
        lax.fori_loop(half * 64, half * 64 + 64, add_entering, 0, unroll=2)
        rows = pl.ds(half * 64, 64)
        for g in range(8):
            cols = pl.ds(g * 128, 128)
            y = y_t[pl.ds(half * 512 + g, 64, stride=8), :]
            y = y + skip[:, cols] * conv_out[rows, cols].astype(F32)
            z = gate_in[rows, cols].astype(F32)
            block = (y * (z * jax.nn.sigmoid(z))).astype(BF16)
            ga[half, pl.ds(halves[half].p, 1), :, cols] = block[None]
        place = ga.at[half, halves[half].p]
        for k, d in enumerate((1, -1)):
            send(place, place, g_send.at[half], g_recv.at[half, k], halves[half].one(d))

    hops = (0, -1, 1, 2)

    def project(i, k):
        rows = ga[i, wrap(halves[i].p + hops[k], 4)]
        for v in range(4):
            block = dot(rows, opg[i, v]).astype(BF16).reshape(2, 2, 16, 256)
            zs[k, pl.ds(2 * i, 2), :, :, pl.ds(v * 256, 256)] = block

    mz, core = exp // 2, exp % 2

    def pair_group(k):
        sibling = {"exp": 2 * mz + 1 - core}
        send(zs.at[k, :, 1 - core], pair.at[k], p_send.at[0], p_recv.at[k], sibling)

    def scatter_group(k):
        settle(pair.at[0], p_recv.at[k])
        own = zs[k, :, pl.ds(core, 1)].reshape(4, 16, 1024).astype(F32)
        both[k] = (own + pair[k].astype(F32)).astype(BF16)
        for d in (1, 3, 2):
            z = wrap(mz + d, 4)
            send(both.at[k, z], rz.at[k, mz], z_send.at[0], z_recv.at[k], {"exp": 2 * z + core})
        rz[k, pl.ds(mz, 1)] = both[k, pl.ds(mz, 1)]

    second = exp // 4
    place = mx + second * (my - mx)

    def finish_group(k):
        settle(rz.at[0, pl.ds(0, 3)], z_recv.at[k])
        total = rz[k, 0].astype(F32)
        for j in range(1, 4):
            total = total + rz[k, j].astype(F32)
        d = hops[k]
        if d == 0:
            mo[pl.ds(place, 1)] = total.astype(BF16)[None]
        else:
            ms[k - 1] = total.astype(BF16)
            near_x, near_y = along_x(d)["ctx"], along_y(d)["ctx"]
            device = {"ctx": near_x + second * (near_y - near_x)}
            send(ms.at[k - 1], mo.at[place], m_sem.at[0], m_sem.at[1], device)

    top, low = pl.ds(0, 32), pl.ds(32, 32)
    for i in range(2):
        settle(opg.at[0, 0], o_recv.at[i, 2])
        project(i, 0)
    pair_group(0)
    for i, h in enumerate(halves):
        for k, d, rows in ((0, 1, top), (1, -1, low)):
            settle(ga.at[0, 0], g_recv.at[i, k])
            block = ga.at[i, wrap(h.p - d, 4), rows]
            send(block, block, g_send.at[i], g_recv.at[i, 2], h.one(d))
    scatter_group(0)
    for k in (1, 2):
        project(0, k)
        project(1, k)
        pair_group(k)
    scatter_group(1)
    scatter_group(2)
    for i in range(2):
        settle(ga.at[0, 0], g_recv.at[i, 2])
        project(i, 3)
    pair_group(3)
    finish_group(0)
    scatter_group(3)
    for k in (1, 2, 3):
        finish_group(k)
    settle(mo.at[pl.ds(0, 3)], m_sem.at[1])

    squares = jnp.zeros((16, 1), F32)
    for u in range(4):
        cols = pl.ds(u * 1024, 1024)
        across = [mo[v, :, pl.ds(u * 256, 256)] for v in range(4)]
        mixed = jnp.where(second == 0, mo[u].astype(F32), jnp.concatenate(across, 1).astype(F32))
        rows = residual[:, cols].astype(F32) + mixed
        stream[:, cols] = rows
        squares = squares + jnp.sum(rows * rows, axis=1, keepdims=True)
    scale = lax.rsqrt(squares * (1.0 / 4096.0) + 1e-06)
    logits = jnp.zeros((8, 16), F32)
    for u in range(4):
        cols = pl.ds(u * 1024, 1024)
        rows = (stream[:, cols] * scale * gain[:, cols]).astype(BF16)
        normed[:, cols] = rows
        logits = logits + dot_t(router[:, cols], rows)
    ids = expert_ids[...]
    lanes = lax.broadcasted_iota(jnp.int32, (8, 16), 0)
    signs = jnp.where(ids[0:1] == lanes, 1.0, 0.0) - jnp.where(ids[1:2] == lanes, 1.0, 0.0)
    first = jax.nn.sigmoid(jnp.sum(logits * signs, axis=0, keepdims=True))

    def drain():
        settle(rim, h_sem.at[0])
        for i in range(2):
            settle(opg.at[0, pl.ds(0, 3)], o_send.at[i])
            settle(ga.at[0, pl.ds(0, 3)], g_send.at[i])
        settle(parts.at[pl.ds(0, 7)], a_sem.at[0])
        settle(part_maps.at[pl.ds(0, 7)], a_sem.at[2])
        settle(low_rank.at[pl.ds(0, 7)], b_sem.at[0])
        settle(maps.at[pl.ds(0, 7)], b_sem.at[1])
        for base, (fin, sums) in enumerate(((fin_y, sum_y), (fin_x, sum_x))):
            settle(fin.at[pl.ds(0, 3)], c_send.at[0, base])
            settle(sums.at[pl.ds(0, 3)], c_send.at[1, base])
        settle(pair, p_send.at[0])
        settle(rz.at[:, pl.ds(0, 3)], z_send.at[0])
        settle(mo.at[pl.ds(0, 3)], m_sem.at[0])

    return first, drain


def experts(r, gate_row, drain, out, exp, mx, my, halves, loads):
    pick = r.pick
    result = r.result
    e_sem = r.e_sem
    stream = r.stream
    normed = r.normed
    spread = r.spread
    fetch = r.fetch
    go = r.go
    rcv = r.rcv
    rback = r.rback
    xa = r.xa
    xb = r.xb
    wgu = r.wgu
    wd = r.wd
    lhs = r.lhs
    lhs_down = r.lhs_down
    acc = r.acc
    hid = r.hid
    oa = r.oa
    ob = r.ob
    far = r.far
    near = r.near
    tot = r.tot
    far2 = r.far2
    near2 = r.near2
    d_send = r.d_send
    d_recv = r.d_recv
    u_send = r.u_send
    u_recv = r.u_recv
    s_send = r.s_send
    s_recv = r.s_recv
    r_send = r.r_send
    r_recv = r.r_recv
    xs, os = (xa, xb), (oa, ob)
    lo, hi = pl.ds(0, 1024), pl.ds(1024, 1024)
    every = slice(None)

    windows = (0, 768, 1280)

    def all_to_all(half, into, ss, rs):
        for d in FAR_FIRST:
            peer = lax.rem(exp + d, 8)
            src, dst = go.at[half, peer], into.at[half, exp]
            remote(src, dst, ss.at[half], rs.at[half], {"exp": peer}).start()
        into[half, pl.ds(exp, 1)] = go[half, pl.ds(exp, 1)]

    for i in range(2):
        packed = jnp.zeros((128, 768), F32)
        for k, w in enumerate(windows):
            packed = packed + dot(spread[k], normed[:, pl.ds(i * 2048 + w, 768)])
        go[i] = packed.astype(BF16).reshape(8, 16, 768)
        all_to_all(i, rcv, d_send, d_recv)
    acc[...] = jnp.zeros_like(acc)

    def push(i, at, cols, ss, rs, device):
        place = xs[i].at[at + (every, cols)] if cols is not None else xs[i].at[at]
        remote(place, place, u_send.at[i, ss], u_recv.at[i, rs], device).start()

    steps = [[wrap(h.p + d, 4) for d in (0, -1, 1, 2)] for h in halves]

    def second_start(i, g):
        h = halves[i]
        at = h.unit(steps[i][g], h.q)
        push(i, at, None, 1, 3 + g, h.two(1))
        push(i, at, None, 1, 3 + g, h.two(-1))

    def second_pass(i, g):
        h, u = halves[i], steps[i][g]
        settle(xs[i].at[0, pl.ds(0, 2)], u_recv.at[i, 3 + g])
        push(i, h.unit(u, wrap(h.q - 1, 4)), lo, 2, 7, h.two(1))
        push(i, h.unit(u, wrap(h.q + 1, 4)), hi, 2, 7, h.two(-1))

    for i, (h, x) in enumerate(zip(halves, xs)):
        settle(rcv.at[i, pl.ds(0, 7)], d_recv.at[i])
        flat = rcv[i].reshape(128, 768)
        for k, w in enumerate(windows):
            block = dot(pick[k], flat).astype(BF16)[None, None]
            x[pl.ds(mx, 1), pl.ds(my, 1), :, pl.ds(w, 768)] = block
        at = h.unit(h.p, h.q)
        push(i, at, None, 0, 0, h.one(1))
        push(i, at, None, 0, 1, h.one(-1))
        if i == 0:
            second_start(0, 0)
    for i, (h, x) in enumerate(zip(halves, xs)):
        settle(x.at[0, 0], u_recv.at[i, 0])
        push(i, h.unit(steps[i][1], h.q), lo, 0, 2, h.one(1))
        settle(x.at[0, 0], u_recv.at[i, 1])
        push(i, h.unit(steps[i][2], h.q), hi, 0, 2, h.one(-1))
        if i == 0:
            second_start(1, 0)
    second_start(0, 1)
    second_start(1, 1)
    for i in range(2):
        settle(xs[i].at[0, 0], u_recv.at[i, 2])
        second_start(i, 2)
        second_start(i, 3)

    def gate_up(i, units):
        for n, at in enumerate(units):
            lhs[n] = xs[i][at]
        for j in range(6):
            cols = pl.ds(j * 256, 256)
            part = dot(lhs[...].reshape(160, 2048), wgu[pl.ds(i * 2048, 2048), cols])
            for n, at in enumerate(units):
                place = at + (every, cols)
                acc[place] = acc[place] + part[n * 40 : (n + 1) * 40]

    def line(i, v):
        return [halves[i].unit(u, v) for u in steps[i]]

    def beside(i, gs):
        h = halves[i]
        return [h.unit(steps[i][g], wrap(h.q + d, 4)) for g in gs for d in (-1, 1)]

    loads[0].wait()
    loads[1].wait()
    gate_up(0, line(0, halves[0].q))
    second_pass(0, 0)
    second_pass(1, 0)
    gate_up(1, line(1, halves[1].q))
    second_pass(0, 1)
    second_pass(1, 1)
    gate_up(0, beside(0, (0, 1)))
    second_pass(0, 2)
    second_pass(1, 2)
    gate_up(1, beside(1, (0, 1)))
    second_pass(0, 3)
    second_pass(1, 3)
    gate_up(0, beside(0, (2, 3)))
    gate_up(1, beside(1, (2, 3)))

    def activate(units):
        for at in units:
            gate = acc[at + (every, pl.ds(0, 768))]
            up = acc[at + (every, pl.ds(768, 768))]
            hid[at] = (gate * jax.nn.sigmoid(gate) * up).astype(BF16)

    def down(i, units):
        count = len(units)
        for n, at in enumerate(units):
            lhs_down[n] = hid[at]
        for j in range(8):
            cols = pl.ds(j * 256, 256)
            rows = lhs_down[pl.ds(0, count)].reshape(count * 40, 768)
            part = dot(rows, wd[:, pl.ds(i * 2048 + j * 256, 256)]).astype(BF16)
            for n, at in enumerate(units):
                os[i][at + (every, cols)] = part[n * 40 : (n + 1) * 40]

    def send(src, dst, i, ss, rs, device):
        remote(src, dst, s_send.at[i, ss], s_recv.at[i, rs], device).start()

    def add_into(ref, at, other, other_at):
        ref[at] = (ref[at].astype(F32) + other[other_at].astype(F32)).astype(BF16)

    order = [[wrap(h.p + d, 4) for d in (2, 1, -1, 0)] for h in halves]

    def send_near(i, ks):
        h = halves[i]
        sides = ((wrap(h.q + 1, 4), 1, hi, 0), (wrap(h.q - 1, 4), -1, lo, 1))
        down(i, [h.unit(order[i][k], v) for v, _, _, _ in sides for k in ks])
        for v, d, cols, b in sides:
            for k in ks:
                u = order[i][k]
                src, dst = os[i].at[h.unit(u, v) + (every, cols)], near.at[i, b, u, :, cols]
                send(src, dst, i, 0, 4, h.two(d))

    xx, yy = [wrap(mx + d, 4) for d in (0, 1, -1)], [wrap(my + d, 4) for d in (0, 1, -1)]
    activate([(u, v) for u in xx for v in yy])
    loads[2].wait()
    for i in range(2):
        send_near(i, (1, 2, 3))
    for i, h in enumerate(halves):
        settle(xs[i].at[0], u_recv.at[i, 7])
        gate_up(i, line(i, wrap(h.q + 2, 4)))
    fx, fy = wrap(mx + 2, 4), wrap(my + 2, 4)
    activate([(fx, v) for v in yy] + [(u, fy) for u in xx] + [(fx, fy)])
    for i, h in enumerate(halves):
        v = wrap(h.q + 2, 4)
        down(i, [h.unit(u, v) for u in order[i]])
        for k, u in enumerate(order[i]):
            at = h.unit(u, v)
            send(os[i].at[at + (every, lo)], far.at[i, 0, u], i, 0, k, h.two(1))
            send(os[i].at[at + (every, hi)], far.at[i, 1, u], i, 0, k, h.two(-1))
    for i in range(2):
        send_near(i, (0,))
    down(0, line(0, halves[0].q))
    for k in range(4):
        for i, h in enumerate(halves):
            u = order[i][k]
            settle(xs[i].at[0, 0], s_recv.at[i, k])
            for b, d, cols in ((0, 1, lo), (1, -1, hi)):
                at = h.unit(u, wrap(h.q + d, 4)) + (every, cols)
                add_into(os[i], at, far, (i, b, u))
                send(os[i].at[at], near.at[i, b, u, :, cols], i, 0, 5 + k, h.two(d))
    down(1, line(1, halves[1].q))
    for i in range(2):
        settle(xs[i].at[0], s_recv.at[i, 4])
    for k in range(4):
        for i, h in enumerate(halves):
            u = order[i][k]
            settle(xs[i].at[0, 0], s_recv.at[i, 5 + k])
            mine = os[i][h.unit(u, h.q)].astype(F32)
            mine = mine + near[i, 0, u].astype(F32) + near[i, 1, u].astype(F32)
            tot[i, u] = mine.astype(BF16)
            if k == 0:
                send(tot.at[i, u, :, lo], far2.at[i, 0], i, 1, 9, h.one(1))
                send(tot.at[i, u, :, hi], far2.at[i, 1], i, 1, 9, h.one(-1))
            if k == 1:
                send(tot.at[i, u, :, hi], near2.at[i, 0, :, hi], i, 1, 10, h.one(1))
            if k == 2:
                send(tot.at[i, u, :, lo], near2.at[i, 1, :, lo], i, 1, 10, h.one(-1))
    for i, h in enumerate(halves):
        settle(xs[i].at[0, 0], s_recv.at[i, 9])
        for b, d, cols in ((0, 1, lo), (1, -1, hi)):
            u = order[i][1 + b]
            add_into(tot, (i, u, every, cols), far2, (i, b))
            send(tot.at[i, u, :, cols], near2.at[i, b, :, cols], i, 1, 10, h.one(d))

    across = (((0,), (0,)), ((), ()))
    for i, h in enumerate(halves):
        settle(xs[i].at[0, pl.ds(0, 2)], s_recv.at[i, 10])
        final = tot[i, h.p].astype(F32) + near2[i, 0].astype(F32) + near2[i, 1].astype(F32)
        final = final.astype(BF16)
        back = jnp.zeros((128, 768), F32)
        for k, w in enumerate(windows):
            block = final[:, w : w + 768]
            back = back + lax.dot_general(pick[k], block, across, preferred_element_type=F32)
        settle(rcv.at[i, pl.ds(0, 7)], d_send.at[i])
        go[i] = back.astype(BF16).reshape(8, 16, 768)
        all_to_all(i, rback, r_send, r_recv)
    eye = lax.broadcasted_iota(jnp.int32, (16, 16), 0) == lax.broadcasted_iota(
        jnp.int32, (16, 16), 1
    )
    gate = jnp.sum(jnp.where(eye, jnp.broadcast_to(gate_row, (16, 16)), 0.0), axis=1, keepdims=True)
    stores = []
    for i in range(2):
        settle(rback.at[i, pl.ds(0, 7)], r_recv.at[i])
        flat = rback[i].reshape(128, 768)
        for j, w in enumerate(windows):
            cols = pl.ds(i * 2048 + w, 768)
            pair = [
                lax.dot_general(fetch[j, k], flat, across, preferred_element_type=F32)
                for k in range(2)
            ]
            mix = gate * pair[0] + (1.0 - gate) * pair[1]
            result[:, cols] = stream[:, cols] + mix
        cols = pl.ds(i * 2048, 2048)
        stores.append(pltpu.make_async_copy(result.at[:, cols], out.at[:, cols], e_sem.at[i]))
        stores[i].start()
    drain()
    for i in range(2):
        settle(rback.at[i, pl.ds(0, 7)], r_send.at[i])
        settle(xs[i].at[0, pl.ds(0, 3)], u_send.at[i, 0])
        settle(xs[i].at[pl.ds(0, 2)], u_send.at[i, 1])
        settle(xs[i].at[0], u_send.at[i, 2])
        settle(xs[i].at[pl.ds(0, 3)], s_send.at[i, 0])
        settle(xs[i].at[0, pl.ds(0, 3)], s_send.at[i, 1])
    for c in stores:
        c.wait()


def token_places(ids, spread, fetch):
    experts_of = lax.broadcasted_iota(jnp.int32, (8, 16), 0)
    hits = [ids[k : k + 1] == experts_of for k in range(2)]
    either = jnp.where(hits[0] | hits[1], 1.0, 0.0).astype(BF16)
    before = lax.broadcasted_iota(jnp.int32, (16, 16), 0) < lax.broadcasted_iota(
        jnp.int32, (16, 16), 1
    )
    earlier = dot(either, jnp.where(before, 1.0, 0.0).astype(BF16))
    rows = lax.broadcasted_iota(jnp.int32, (128, 16), 0).astype(F32)
    for j in range(3):
        found = []
        for k in range(2):
            slot = jnp.sum(jnp.where(hits[k], earlier, 0.0), axis=0, keepdims=True)
            place = ids[k : k + 1].astype(F32) * 16.0 + slot + j * 5.0
            found.append(jnp.where(rows == place, 1.0, 0.0))
            fetch[j, k] = found[k].astype(BF16)
        spread[j] = (found[0] + found[1]).astype(BF16)


def block_kernel(*refs):
    names = INPUTS + ("out",) + tuple(SCRATCH)
    r = types.SimpleNamespace(**dict(zip(names, refs, strict=True)))
    ctx, exp = lax.axis_index("ctx"), lax.axis_index("exp")
    mx, my = ctx // 4, ctx % 4
    halves = (Half(0, mx, my), Half(1, mx, my))
    wgu, wd, w_sem = r.wgu, r.wd, r.w_sem
    loads = [
        pltpu.make_async_copy(r.w_gate.at[0], wgu.at[:, pl.ds(0, 768)], w_sem.at[0]),
        pltpu.make_async_copy(r.w_up.at[0], wgu.at[:, pl.ds(768, 768)], w_sem.at[1]),
        pltpu.make_async_copy(r.w_down.at[0], wd, w_sem.at[2]),
    ]
    for load in loads:
        load.start()
    arrive = greet(
        [{"ctx": lax.rem(ctx + 15, 16)}, {"ctx": lax.rem(ctx + 1, 16)}]
        + [h.one(d) for h in halves for d in (1, 2, -1)]
        + [{"exp": lax.rem(exp + d, 8)} for d in range(1, 8)]
    )
    token_places(r.expert_ids[...], r.spread, r.fetch)
    gate_row, drain = mixer(r, ctx, exp, mx, my, halves, arrive)
    experts(r, gate_row, drain, r.out, exp, mx, my, halves, loads)


def shards(
    mixer_in,
    gate_in,
    conv_weight,
    conv_bias,
    x_proj,
    dt_proj,
    dt_bias,
    decay_rate,
    skip,
    out_proj,
    residual,
    gain,
    router,
    w_gate,
    w_up,
    w_down,
    expert_ids,
):
    pick = np.zeros((3, 40, 128), np.float32)
    for w in range(3):
        for j in range(8):
            for s in range(5):
                pick[w, j * 5 + s, j * 16 + w * 5 + s] = 1.0
    vmem = pl.BlockSpec(memory_space=pltpu.VMEM)
    anywhere = pl.BlockSpec(memory_space=pl.ANY)
    block = pl.pallas_call(
        block_kernel,
        out_shape=jax.ShapeDtypeStruct((16, 4096), F32),
        in_specs=[anywhere if name.startswith("w_") else vmem for name in INPUTS],
        out_specs=anywhere,
        scratch_shapes=list(SCRATCH.values()),
        compiler_params=pltpu.CompilerParams(
            collective_id=0, has_side_effects=True, vmem_limit_bytes=VMEM_LIMIT
        ),
        cost_estimate=pl.CostEstimate(
            flops=13_500_000_000, bytes_accessed=24_000_000, transcendentals=0
        ),
    )(
        mixer_in,
        gate_in,
        conv_weight,
        conv_bias[None],
        x_proj.T,
        dt_proj,
        dt_bias[None],
        decay_rate,
        skip[None],
        out_proj,
        residual,
        gain[None],
        router.T,
        expert_ids.T,
        w_gate,
        w_up,
        w_down,
        jnp.asarray(pick, BF16),
    )
    return block.astype(BF16)


def solution(mesh):
    in_specs = (
        P("ctx", "exp"),
        P("ctx", "exp"),
        P(None, "exp"),
        P("exp"),
        P("exp", None),
        P(None, "exp"),
        P("exp"),
        P(None, "exp"),
        P("exp"),
        P("exp", "ctx"),
        P(("ctx", "exp"), None),
        P(),
        P(),
        P("exp", None, "ctx"),
        P("exp", None, "ctx"),
        P("exp", "ctx", None),
        P(("ctx", "exp"), None),
    )
    out_specs = P(("ctx", "exp"), None)
    return jax.shard_map(shards, mesh=mesh, in_specs=in_specs, out_specs=out_specs, check_vma=False)
```
